32 devices in a mesh: ma: 2 (over y), fr: 4 (over x, core), fc: 4 (over z).
Axes of the slice: x: 2, y: 2, z: 4, core: 2. Of those that a mesh axis runs over, the one named last changes fastest.
Arguments:
- beam_transfer: bfloat16 [2, 256, 64, 512], P(None, ('ma', 'fr'), 'fc'), parts along dimension 1, may hold values from -0.25 to 0.25
- noise_var: float32 [256, 64], P(('ma', 'fr'), 'fc'), parts along dimension 0, may hold values from 0.3 to 30
- spectra: float32 [2, 512], replicated, may hold values from 0.05 to 5
- freq_covariance: float32 [2, 128, 128], replicated, as said below
- start_vectors: float32 [2, 256, 64, 128], P(None, ('ma', 'fr'), 'fc'), parts along dimension 1, may hold values from -6 to 6
Outputs:
- basis: float32 [2, 256, 64, 128], P(None, ('ma', 'fr'), 'fc'), parts along dimension 1
The draws below stay inside these ranges and needn't reach their ends.
There are 2 independent parts, one for each index of `ma`. The reference program is written for one: setup_inputs(seed, part) draws one part's arguments, and reference() takes and returns one part's arrays. A program takes and returns all parts, laid end to end along the dimension named above; an argument that names none is the same for every part. Nothing has to cross between parts.
Inputs may be any that keep to these rules, and one draw needn't show every extreme that they name: freq_covariance[k] is symmetric and positive definite for each k.
All inputs are finite; a program needn't handle non-finite values.
Results may differ from the reference program's by a relative error of at most 0.0071.
Values may be sent and summed in bfloat16 or wider, within the bound.
No kernel may reach another device: no remote copies, remote signals or barrier semaphores. Data moves between devices by JAX's collectives and lax.ppermute only.
A program may use at most 192 MiB of HBM per device.

```python
import math
import jax
import jax.numpy as jnp
from jax import lax

F = 128
P_SIZE = 64
L = 512
R = 128
K = 2
ITERS = 2


def draw_freq_covariance(key, part):
    first, second = jax.random.split(jax.random.fold_in(key, 11))
    factor = jax.random.normal(first, (K, F, F), jnp.float32)
    diagonal = jax.random.uniform(second, (K, F), jnp.float32, 0.5, 1.5)
    symmetric = jnp.einsum('kab,kcb->kac', factor, factor) * (0.5 / F)
    return symmetric + diagonal[:, :, None] * jnp.eye(F, dtype=jnp.float32)[None]


def level_of(key, dims, cuts, low, top_value):
    factor_of, own = 1.0, jax.random.fold_in(key, 6)
    for dim, blocks in cuts:
        steps = jnp.exp(jax.random.uniform(jax.random.fold_in(own, dim), (blocks,), jnp.float32, low / len(cuts), top_value / len(cuts)))
        factor_of = factor_of * jnp.repeat(steps, dims[dim] // blocks).reshape([-1 if axis == dim else 1 for axis in range(len(dims))])
    return factor_of


def scatter_about(key, extent, scale, most, shards=(), held_as=jnp.bfloat16):
    loudness = level_of(key, extent, shards, -0.22, 0.18) if shards else 1.0
    values = jax.random.normal(key, extent, jnp.float32) * scale * loudness
    return jnp.minimum(jnp.maximum(values, -most), most).astype(held_as)


def setup_inputs(seed: int = 0, part: int = 0) -> dict:
    arg_keys = jax.random.split(jax.random.key(seed), 6)
    own_keys = jax.random.split(jax.random.fold_in(arg_keys[5], part), 6)
    return {
        "beam_transfer": scatter_about(own_keys[0], (2, F, P_SIZE, L), L ** -0.5, 0.25, ((1, 4), (2, 4))),
        "noise_var": jnp.clip(jnp.exp(math.log(30.0) - 4.6051701 * jax.random.uniform(own_keys[1], (F, P_SIZE), jnp.float32) ** level_of(own_keys[1], (F, P_SIZE), ((0, 4), (1, 4)), -0.2, 0.2)), 0.3, 30.0),
        "spectra": jnp.clip(jnp.exp(jax.random.uniform(arg_keys[2], (K, L), jnp.float32, math.log(0.05), math.log(5.0))), 0.05, 5.0),
        "freq_covariance": draw_freq_covariance(jax.random.fold_in(arg_keys[5], 71), part),
        "start_vectors": scatter_about(own_keys[4], (2, F, P_SIZE, R), 1.0, 6.0, ((1, 4), (2, 4)), jnp.float32),
    }


def row_operands(row_part, spectra):
    scaled = (row_part.astype(jnp.float32)[None] * spectra[:, None, None, :]).astype(jnp.bfloat16)
    real_rows = jnp.concatenate([scaled[:, 0], scaled[:, 1]], axis=-1)
    imag_rows = jnp.concatenate([scaled[:, 1], -scaled[:, 0]], axis=-1)
    return jnp.stack([real_rows, imag_rows], axis=1)

def apply_tile(pair_tile, vec_bf):
    row_count = pair_tile.shape[1]
    stacked = pair_tile.reshape(2 * row_count, pair_tile.shape[2])
    with_real = jnp.dot(stacked.astype(jnp.float32), vec_bf[0].astype(jnp.float32), preferred_element_type=jnp.float32)
    with_imag = jnp.dot(stacked.astype(jnp.float32), vec_bf[1].astype(jnp.float32), preferred_element_type=jnp.float32)
    real_part = with_real[:row_count] - with_imag[row_count:]
    imag_part = with_real[row_count:] + with_imag[:row_count]
    return jnp.stack([real_part, imag_part], axis=0)

def orthonormalize(image):
    gram_matrix = jnp.dot(image.T.astype(jnp.float32), image.astype(jnp.float32), precision=lax.Precision.HIGHEST, preferred_element_type=jnp.float32)
    lower = jnp.linalg.cholesky(gram_matrix)
    return lax.linalg.triangular_solve(lower, image, left_side=False, lower=True, transpose_a=True)

def reference(beam_transfer, noise_var, spectra, freq_covariance, start_vectors):
    whitened = (beam_transfer.astype(jnp.float32) * lax.rsqrt(noise_var)[None, :, :, None]).astype(jnp.bfloat16)
    order_all = F * P_SIZE
    col_operand = jnp.concatenate([whitened[0].reshape(order_all, L), whitened[1].reshape(order_all, L)], axis=-1)
    vectors = start_vectors
    for iteration in range(ITERS):
        vec_bf = vectors.astype(jnp.bfloat16).reshape(2, order_all, R)

        def block(freq):
            row_part = lax.dynamic_index_in_dim(whitened, freq, 1, keepdims=False)
            operand = row_operands(row_part, spectra)
            products = lax.dot_general(operand.astype(jnp.float32), col_operand.astype(jnp.float32), (((3,), (1,)), ((), ())), preferred_element_type=jnp.float32)
            cov_row = lax.dynamic_index_in_dim(freq_covariance, freq, 1, keepdims=False)
            weight = jnp.repeat(cov_row, P_SIZE, axis=1)
            pair_tile = jnp.einsum('kn,kcpn->cpn', weight, products).astype(jnp.bfloat16)
            return apply_tile(pair_tile, vec_bf)
        image = lax.map(block, jnp.arange(F, dtype=jnp.int32))
        image = jnp.transpose(image, (1, 0, 2, 3)).reshape(2 * order_all, R)
        vectors = orthonormalize(image).reshape(2, F, P_SIZE, R)
    return vectors * math.sqrt(2.0 * F * P_SIZE)
```

```python
import functools
import math

import jax
import jax.numpy as jnp
from jax import lax
from jax.experimental import pallas as pl
from jax.experimental.pallas import tpu as pltpu
from jax.sharding import Mesh
from jax.sharding import PartitionSpec as P

ITERS = 2
BF16 = jnp.bfloat16
F32 = jnp.float32
VMEM_BYTES = 56 * 1024 * 1024
HIGH = lax.Precision.HIGHEST


def rolled(value, shift):
    return pltpu.roll(value, shift % value.shape[-1], 1)


def apply_kernel(n_vec, n_chunk, own, *refs):
    vec_refs = refs[:n_vec]
    beam_refs = refs[n_vec : n_vec + n_chunk]
    cov_ref, spec_ref, out_ref, z_ref, y_ref = refs[n_vec + n_chunk :]
    freqs, rows, lanes = vec_refs[0].shape
    half = rows // 2
    components = spec_ref.shape[1]
    lane = lax.broadcasted_iota(jnp.int32, (half, lanes), 1)
    is_real = (lane // own) % 2 == 0
    sign = jnp.where(is_real, -1.0, 1.0).astype(F32)

    for chunk in range(n_chunk):
        beam_ref = beam_refs[chunk]

        def project(freq, carry):
            vec = vec_refs[0][freq]
            for other in vec_refs[1:]:
                vec = vec + other[freq]
            z_ref[pl.ds(freq, rows, stride=freqs), :] = jnp.dot(
                vec.astype(BF16), beam_ref[freq], preferred_element_type=F32
            )
            return carry

        lax.fori_loop(0, freqs, project, 0, unroll=8)

        def mix(row, carry):
            start = pl.multiple_of(row * freqs, freqs)
            z = z_ref[pl.ds(start, freqs), :]
            scaled = [(z * spec_ref[chunk, k][None, :]).astype(BF16) for k in range(components)]
            stacked = jnp.concatenate(scaled, axis=0)
            y_ref[pl.ds(start, freqs), :] = jnp.dot(
                cov_ref[...], stacked, preferred_element_type=F32
            )
            return carry

        lax.fori_loop(0, rows, mix, 0, unroll=4)

        def expand(freq, carry):
            y = y_ref[pl.ds(freq, rows, stride=freqs), :].astype(BF16)
            product = lax.dot_general(
                y, beam_ref[freq], (((1,), (1,)), ((), ())), preferred_element_type=F32
            )
            swapped = jnp.where(
                jnp.concatenate([is_real, is_real], axis=0),
                rolled(product, -own),
                rolled(product, own),
            )
            top = product[:half] + sign * swapped[half:]
            bottom = product[half:] - sign * swapped[:half]
            image = jnp.concatenate([top, bottom], axis=0)
            if chunk:
                image = image + out_ref[freq]
            out_ref[freq] = image
            return carry

        lax.fori_loop(0, freqs, expand, 0, unroll=8)


def apply_covariance(vecs, beams, cov, spec, own):
    freqs, rows, lanes = vecs[0].shape
    depth = beams[0].shape[2]
    flops = 2 * len(beams) * freqs * rows * (2 * lanes * depth + 2 * freqs * depth)
    return pl.pallas_call(
        functools.partial(apply_kernel, len(vecs), len(beams), own),
        out_shape=jax.ShapeDtypeStruct((freqs, rows, lanes), F32),
        in_specs=[pl.BlockSpec(memory_space=pltpu.VMEM)] * (len(vecs) + len(beams) + 2),
        out_specs=pl.BlockSpec(memory_space=pltpu.VMEM),
        scratch_shapes=[
            pltpu.VMEM((rows * freqs, depth), F32),
            pltpu.VMEM((rows * freqs, depth), F32),
        ],
        compiler_params=pltpu.CompilerParams(vmem_limit_bytes=VMEM_BYTES),
        cost_estimate=pl.CostEstimate(
            flops=flops, bytes_accessed=len(beams) * freqs * lanes * depth * 2, transcendentals=0
        ),
    )(*vecs, *beams, cov, spec)


def pack_kernel(own, first_ref, second_ref, out_ref):
    x_count, z_count, groups = out_ref.shape[:3]
    freqs, rows, lanes = first_ref.shape
    per_group = lanes // own
    lane = lax.broadcasted_iota(jnp.int32, (rows, lanes), 1) // own

    def group(index, carry):
        x_index, group_index = index // groups, index % groups
        totals = [jnp.zeros((rows, lanes), F32)] * z_count
        for place in range(per_group):
            freq = index * per_group + place
            image = first_ref[freq] + second_ref[freq]
            for z_index in range(z_count):
                moved = rolled(image, (place - 2 * z_index) * own)
                totals[z_index] = jnp.where(lane == place, moved, totals[z_index])
        for z_index in range(z_count):
            out_ref[x_index, z_index, group_index] = totals[z_index].astype(BF16)
        return carry

    lax.fori_loop(0, x_count * groups, group, 0)


def pack(first, second, x_count, z_count, own):
    freqs, rows, lanes = first.shape
    groups = freqs * own // (x_count * lanes)
    return pl.pallas_call(
        functools.partial(pack_kernel, own),
        out_shape=jax.ShapeDtypeStruct((x_count, z_count, groups, rows, lanes), BF16),
        in_specs=[pl.BlockSpec(memory_space=pltpu.VMEM)] * 2,
        out_specs=pl.BlockSpec(memory_space=pltpu.VMEM),
        compiler_params=pltpu.CompilerParams(vmem_limit_bytes=VMEM_BYTES),
    )(first, second)


def gram_kernel(rows_ref, out_ref):
    senders, images, groups, parts, vectors, lanes = rows_ref.shape
    total = senders * vectors
    for image in range(images):
        gram = jnp.zeros((total, total), F32)
        for group in range(groups):
            for part in range(parts):
                flat = rows_ref[:, image, group, part].reshape(total, lanes)
                gram += lax.dot_general(
                    flat, flat, (((1,), (1,)), ((), ())), preferred_element_type=F32
                )
        out_ref[image] = gram


def grams(rows):
    total = rows.shape[0] * rows.shape[4]
    return pl.pallas_call(
        gram_kernel,
        out_shape=jax.ShapeDtypeStruct((rows.shape[1], total, total), F32),
        in_specs=[pl.BlockSpec(memory_space=pltpu.VMEM)],
        out_specs=pl.BlockSpec(memory_space=pltpu.VMEM),
        compiler_params=pltpu.CompilerParams(vmem_limit_bytes=VMEM_BYTES),
    )(rows)


def finish_kernel(rows_ref, mixing_ref, out_ref):
    senders, groups, parts, vectors, lanes = rows_ref.shape
    total = senders * vectors
    mixing = mixing_ref[...]
    high = mixing.astype(BF16)
    rest = mixing - high.astype(F32)
    middle = rest.astype(BF16)
    low = (rest - middle.astype(F32)).astype(BF16)
    for group in range(groups):
        for part in range(parts):
            flat = rows_ref[:, group, part].reshape(total, lanes)
            turned = flat.astype(F32).T.astype(BF16)
            dot = functools.partial(
                lax.dot_general,
                turned,
                dimension_numbers=(((1,), (1,)), ((), ())),
                preferred_element_type=F32,
            )
            out_ref[part, group] = (dot(low) + dot(middle)) + dot(high)


def finish(rows, mixing):
    senders, groups, parts, vectors, lanes = rows.shape
    return pl.pallas_call(
        finish_kernel,
        out_shape=jax.ShapeDtypeStruct((parts, groups, lanes, senders * vectors), F32),
        in_specs=[pl.BlockSpec(memory_space=pltpu.VMEM)] * 2,
        out_specs=pl.BlockSpec(memory_space=pltpu.VMEM),
        compiler_params=pltpu.CompilerParams(vmem_limit_bytes=VMEM_BYTES),
    )(rows, mixing)


def swap_cores(value):
    return lax.ppermute(value, "core", [(0, 1), (1, 0)])


def line_blocks(block, count):
    place = lax.axis_index("fc")
    found = []
    down = up = merged = block
    joined = False
    for step in range(1, count):
        from_above = [(j, j - 1) for j in range(1, count) if j + step - 1 < count]
        from_below = [(j, j + 1) for j in range(count - 1) if j >= step - 1]
        low_side = [pair[1] for pair in from_above]
        high_side = [pair[1] for pair in from_below]
        distance = jnp.where(place + step < count, step, -step)
        if joined:
            merged = lax.ppermute(merged, "fc", from_above + from_below)
            found.append((merged, distance, low_side + high_side))
            continue
        down = lax.ppermute(down, "fc", from_above)
        up = lax.ppermute(up, "fc", from_below)
        if set(low_side) & set(high_side):
            found.append((down, step, low_side))
            found.append((up, -step, high_side))
        else:
            merged = jnp.where(place + step < count, down, up)
            joined = True
            found.append((merged, distance, low_side + high_side))
    return found


def gather_chunk(block, x_count, z_count):
    cores, freqs, rows, depth = block.shape
    x_place, z_place = lax.axis_index("x"), lax.axis_index("fc")
    whole = jnp.zeros((x_count, cores, freqs, z_count, rows, depth), block.dtype)

    def put(whole, piece, x_at, z_at):
        return lax.dynamic_update_slice(
            whole, piece[None, :, :, None], (x_at, 0, 0, z_at, 0, 0)
        )

    def across(piece, receivers):
        pairs = []
        for x_index in range(x_count):
            for z_index in receivers:
                pairs.append((x_index * z_count + z_index, (1 - x_index) * z_count + z_index))
        return lax.ppermute(piece, ("x", "fc"), pairs)

    everyone = list(range(z_count))
    mirrored = across(block, everyone)
    found = line_blocks(block, z_count)
    whole = put(whole, block, x_place, z_place)
    whole = put(whole, mirrored, 1 - x_place, z_place)
    for piece, distance, receivers in found:
        opposite = across(piece, receivers)
        z_at = z_place + distance
        if len(receivers) < z_count:
            has = functools.reduce(jnp.logical_or, [z_place == z for z in receivers])
            piece = jnp.where(has, piece, block)
            opposite = jnp.where(has, opposite, mirrored)
            z_at = jnp.where(has, z_at, z_place)
        whole = put(whole, piece, x_place, z_at)
        whole = put(whole, opposite, 1 - x_place, z_at)
    return whole.reshape(x_count * cores * freqs, z_count * rows, depth)


def sum_devices(value, z_count):
    value = value + swap_cores(value)
    value = value + lax.ppermute(value, "x", [(0, 1), (1, 0)])
    if z_count & (z_count - 1):
        return lax.psum(value, "fc")
    parts = [lax.ppermute(value, "fc", [(j, j ^ s) for j in range(z_count)]) for s in range(1, z_count)]
    even = z_count == 1
    if even:
        return value
    place = lax.axis_index("fc")
    stacked = jnp.stack([value] + parts)
    ordered = [lax.dynamic_index_in_dim(stacked, place ^ s, 0, False) for s in range(z_count)]
    return functools.reduce(jnp.add, ordered)


def body_split(x_count, z_count, chunks, beam_transfer, noise_var, spectra, freq_covariance, start_vectors):
    parts, freqs, own, multipoles = beam_transfer.shape
    vectors = start_vectors.shape[3]
    cores = 2
    core = lax.axis_index("core")
    all_freqs = x_count * cores * freqs
    mine = vectors // (x_count * z_count)
    depth = multipoles // (cores * chunks)

    whitened = (beam_transfer.astype(F32) * lax.rsqrt(noise_var)[None, :, :, None]).astype(BF16)
    rows = whitened.transpose(1, 0, 2, 3).reshape(freqs, parts * own, cores, chunks, depth)
    rows = rows.transpose(2, 3, 0, 1, 4)
    kept = lax.dynamic_index_in_dim(rows, core, 0, False)
    given = swap_cores(lax.dynamic_index_in_dim(rows, 1 - core, 0, False))
    beams = []
    for chunk in range(chunks):
        first = jnp.where(core == 0, kept[chunk], given[chunk])
        second = jnp.where(core == 0, given[chunk], kept[chunk])
        beams.append(gather_chunk(jnp.stack([first, second]), x_count, z_count))

    spec = spectra.reshape(-1, cores, chunks, depth).transpose(1, 2, 0, 3)
    spec = lax.dynamic_index_in_dim(spec, core, 0, False)
    cov = freq_covariance.transpose(1, 0, 2).reshape(all_freqs, -1).astype(BF16)

    start = start_vectors.astype(BF16).reshape(parts, freqs, own, x_count * z_count, mine)
    start = start.transpose(3, 1, 0, 4, 2)
    start = lax.all_to_all(start, ("x", "fc"), 0, 0, tiled=True)
    other = swap_cores(start)
    both = jnp.stack([jnp.where(core == 0, start, other), jnp.where(core == 0, other, start)])
    both = both.reshape(cores, x_count, z_count, freqs, parts, mine, own)
    both = both.transpose(1, 0, 3, 4, 5, 2, 6)
    real, imag = both[:, :, :, 0], both[:, :, :, 1]
    top = jnp.stack([real, imag], axis=5)
    bottom = jnp.stack([imag, -real], axis=5)
    operand = jnp.stack([top, bottom], axis=3).reshape(all_freqs, parts * mine, z_count * parts * own)

    partials = [
        apply_covariance([operand], [beams[c]], cov, spec[c : c + 1], own) for c in range(chunks)
    ]
    first_own = functools.reduce(jnp.add, partials)
    first_other = swap_cores(first_own)
    second_own = apply_covariance([first_own, first_other], beams, cov, spec, own)

    def of_core(value, which):
        split = value.reshape(x_count, cores, freqs, *value.shape[1:])
        return lax.dynamic_index_in_dim(split, which, 1, False).reshape(-1, *value.shape[1:])

    first_packed = pack(of_core(first_own, core), of_core(first_other, core), x_count, z_count, own)
    second_other = swap_cores(of_core(second_own, 1 - core))
    second_packed = pack(of_core(second_own, core), second_other, x_count, z_count, own)
    packed = jnp.stack([first_packed, second_packed], axis=2)
    packed = packed.reshape(x_count * z_count, *packed.shape[2:])
    received = lax.all_to_all(packed, ("x", "fc"), 0, 0, tiled=True)
    groups, lanes = received.shape[2], received.shape[4]
    received = received.reshape(-1, ITERS, groups, parts, mine, lanes)

    gram_pair = sum_devices(grams(received), z_count)
    lower = jnp.linalg.cholesky(gram_pair[0])
    eye = jnp.eye(vectors, dtype=F32)
    solve = functools.partial(lax.linalg.triangular_solve, left_side=True, lower=True)
    inverse = solve(lower, eye)
    dot = functools.partial(jnp.dot, precision=HIGH, preferred_element_type=F32)
    gram_second = dot(dot(inverse, gram_pair[1]), inverse.T)
    lower = jnp.linalg.cholesky(gram_second)
    mixing = solve(lower, inverse) * math.sqrt(2.0 * all_freqs * z_count * own)
    basis = finish(received[:, 1], mixing)
    return basis.reshape(parts, freqs, own, vectors)


def row_operands(row_part, spectra):
    scaled = (row_part.astype(F32)[None] * spectra[:, None, None, :]).astype(BF16)
    real_rows = jnp.concatenate([scaled[:, 0], scaled[:, 1]], axis=-1)
    imag_rows = jnp.concatenate([scaled[:, 1], -scaled[:, 0]], axis=-1)
    return jnp.stack([real_rows, imag_rows], axis=1)


def apply_tile(pair_tile, vec_bf):
    row_count = pair_tile.shape[1]
    stacked = pair_tile.reshape(2 * row_count, pair_tile.shape[2])
    with_real = jnp.dot(stacked, vec_bf[0], preferred_element_type=F32)
    with_imag = jnp.dot(stacked, vec_bf[1], preferred_element_type=F32)
    real_part = with_real[:row_count] - with_imag[row_count:]
    imag_part = with_real[row_count:] + with_imag[:row_count]
    return jnp.stack([real_part, imag_part], axis=0)


def partial_gram(image):
    flat = image.reshape(-1, image.shape[-1])
    return jnp.dot(flat.T, flat, precision=HIGH, preferred_element_type=F32)


def orthonormalize(image, gram_matrix):
    lower = jnp.linalg.cholesky(gram_matrix)
    flat = image.reshape(-1, image.shape[-1])
    solved = lax.linalg.triangular_solve(lower, flat, left_side=False, lower=True, transpose_a=True)
    return solved.reshape(image.shape)


def body_general(beam_transfer, noise_var, spectra, freq_covariance, start_vectors):
    row_axes = ("x", "core")
    whitened = (beam_transfer.astype(F32) * lax.rsqrt(noise_var)[None, :, :, None]).astype(BF16)
    row_beams = lax.all_gather(whitened, "fc", axis=2, tiled=True)
    _, freq_rows, mode_count, multipoles = row_beams.shape
    row_total = freq_rows * mode_count
    components = spectra.shape[0]
    vectors_count = start_vectors.shape[3]
    row_operand = row_operands(row_beams.reshape(2, row_total, multipoles), spectra)
    row_start = lax.axis_index(row_axes) * freq_rows
    row_cov = lax.dynamic_slice_in_dim(freq_covariance, row_start, freq_rows, 1)
    piece = lax.all_gather(whitened, row_axes, axis=1, tiled=True)
    _, piece_freqs, piece_modes, _ = piece.shape
    columns = piece.reshape(2, piece_freqs * piece_modes, multipoles)
    col_operand = jnp.concatenate([columns[0], columns[1]], axis=-1)
    products = lax.dot_general(
        row_operand, col_operand, (((3,), (1,)), ((), ())), preferred_element_type=F32
    )
    weight = jnp.broadcast_to(
        row_cov[:, :, None, :, None], (components, freq_rows, mode_count, piece_freqs, piece_modes)
    )
    weight = weight.reshape(components, row_total, piece_freqs * piece_modes)
    pair_tile = jnp.einsum("kxy,kcxy->cxy", weight, products).astype(BF16)
    vectors = start_vectors
    own_modes = start_vectors.shape[2]
    for _ in range(ITERS):
        gathered = lax.all_gather(vectors.astype(BF16), row_axes, axis=1, tiled=True)
        vec_bf = gathered.reshape(2, -1, vectors_count)
        partial_value = apply_tile(pair_tile, vec_bf).reshape(2, freq_rows, mode_count, vectors_count)
        summed = lax.psum(partial_value, "fc")
        gram_matrix = lax.psum(partial_gram(summed), row_axes)
        own_rows = lax.dynamic_slice_in_dim(summed, lax.axis_index("fc") * own_modes, own_modes, 2)
        vectors = orthonormalize(own_rows, gram_matrix)
    return vectors * math.sqrt(2.0 * piece_freqs * mode_count)


def body(x_count, z_count, *args):
    beam_transfer, start_vectors = args[0], args[4]
    parts, freqs, own, multipoles = beam_transfer.shape
    vectors = start_vectors.shape[3]
    lanes = parts * own * z_count
    chunks = multipoles // (2 * 128)
    fits = (
        x_count == 2
        and vectors % (16 * x_count * z_count) == 0
        and lanes == 128
        and own % 16 == 0
        and chunks * 256 == multipoles
        and (freqs * own) % lanes == 0
    )
    if fits:
        return body_split(x_count, z_count, chunks, *args)
    return body_general(*args)


def solution(mesh):
    sizes = dict(mesh.shape)
    x_count = sizes["fr"] // 2
    shape = (sizes["ma"], x_count, 2, sizes["fc"])
    devices = mesh.devices.reshape(shape)
    split = Mesh(devices, ("ma", "x", "core", "fc"))
    rows = ("ma", "x", "core")
    in_specs = (
        P(None, rows, "fc", None),
        P(rows, "fc"),
        P(),
        P(),
        P(None, rows, "fc", None),
    )
    return jax.shard_map(
        functools.partial(body, x_count, sizes["fc"]),
        mesh=split,
        in_specs=in_specs,
        out_specs=P(None, rows, "fc", None),
        check_vma=False,
    )
```

```python
import functools
import math

import jax
import jax.numpy as jnp
from jax import lax
from jax.experimental import pallas as pl
from jax.experimental.pallas import tpu as pltpu
from jax.sharding import Mesh
from jax.sharding import PartitionSpec as P

ITERS = 2
BF16 = jnp.bfloat16
F32 = jnp.float32
VMEM_BYTES = 56 * 1024 * 1024
HIGH = lax.Precision.HIGHEST


def rolled(value, shift):
    return pltpu.roll(value, shift % value.shape[-1], 1)


def apply_kernel(n_vec, n_chunk, own, *refs):
    vec_refs = refs[:n_vec]
    beam_refs = refs[n_vec : n_vec + n_chunk]
    cov_ref, spec_ref, *added, out_ref, z_ref, y_ref = refs[n_vec + n_chunk :]
    freqs, rows, lanes = vec_refs[0].shape
    half = rows // 2
    components = spec_ref.shape[1]
    lane = lax.broadcasted_iota(jnp.int32, (half, lanes), 1)
    is_real = (lane // own) % 2 == 0
    sign = jnp.where(is_real, -1.0, 1.0).astype(F32)

    for chunk in range(n_chunk):
        beam_ref = beam_refs[chunk]

        def project(freq, carry):
            vec = vec_refs[0][freq]
            for other in vec_refs[1:]:
                vec = vec + other[freq]
            z_ref[pl.ds(freq, rows, stride=freqs), :] = jnp.dot(
                vec.astype(BF16), beam_ref[freq], preferred_element_type=F32
            )
            return carry

        lax.fori_loop(0, freqs, project, 0, unroll=32)

        def mix(row, carry):
            start = pl.multiple_of(row * freqs, freqs)
            z = z_ref[pl.ds(start, freqs), :]
            scaled = [(z * spec_ref[chunk, k][None, :]).astype(BF16) for k in range(components)]
            stacked = jnp.concatenate(scaled, axis=0)
            y_ref[pl.ds(start, freqs), :] = jnp.dot(
                cov_ref[...], stacked, preferred_element_type=F32
            )
            return carry

        lax.fori_loop(0, rows, mix, 0, unroll=16)

        def expand(freq, carry):
            y = y_ref[pl.ds(freq, rows, stride=freqs), :].astype(BF16)
            product = lax.dot_general(
                y, beam_ref[freq], (((1,), (1,)), ((), ())), preferred_element_type=F32
            )
            swapped = jnp.where(
                jnp.concatenate([is_real, is_real], axis=0),
                rolled(product, -own),
                rolled(product, own),
            )
            top = product[:half] + sign * swapped[half:]
            bottom = product[half:] - sign * swapped[:half]
            image = jnp.concatenate([top, bottom], axis=0)
            if chunk:
                image = image + out_ref[freq]
            elif added:
                image = image + added[0][freq]
            out_ref[freq] = image
            return carry

        lax.fori_loop(0, freqs, expand, 0, unroll=32)


def apply_covariance(vecs, beams, cov, spec, own, added=()):
    freqs, rows, lanes = vecs[0].shape
    depth = beams[0].shape[2]
    flops = 2 * len(beams) * freqs * rows * (2 * lanes * depth + 2 * freqs * depth)
    return pl.pallas_call(
        functools.partial(apply_kernel, len(vecs), len(beams), own),
        out_shape=jax.ShapeDtypeStruct((freqs, rows, lanes), F32),
        in_specs=[pl.BlockSpec(memory_space=pltpu.VMEM)] * (len(vecs) + len(beams) + 2 + len(added)),
        out_specs=pl.BlockSpec(memory_space=pltpu.VMEM),
        scratch_shapes=[
            pltpu.VMEM((rows * freqs, depth), F32),
            pltpu.VMEM((rows * freqs, depth), F32),
        ],
        compiler_params=pltpu.CompilerParams(vmem_limit_bytes=VMEM_BYTES),
        cost_estimate=pl.CostEstimate(
            flops=flops, bytes_accessed=len(beams) * freqs * lanes * depth * 2, transcendentals=0
        ),
    )(*vecs, *beams, cov, spec, *added)


def pack_kernel(own, first_ref, second_ref, out_ref):
    x_count, z_count, groups = out_ref.shape[:3]
    freqs, rows, lanes = first_ref.shape
    per_group = lanes // own
    lane = lax.broadcasted_iota(jnp.int32, (rows, lanes), 1) // own

    def group(index, carry):
        x_index, group_index = index // groups, index % groups
        totals = [jnp.zeros((rows, lanes), F32)] * z_count
        for place in range(per_group):
            freq = index * per_group + place
            image = first_ref[freq] + second_ref[freq]
            for z_index in range(z_count):
                moved = rolled(image, (place - 2 * z_index) * own)
                totals[z_index] = jnp.where(lane == place, moved, totals[z_index])
        for z_index in range(z_count):
            out_ref[x_index, z_index, group_index] = totals[z_index].astype(BF16)
        return carry

    lax.fori_loop(0, x_count * groups, group, 0)


def pack(first, second, x_count, z_count, own):
    freqs, rows, lanes = first.shape
    groups = freqs * own // (x_count * lanes)
    return pl.pallas_call(
        functools.partial(pack_kernel, own),
        out_shape=jax.ShapeDtypeStruct((x_count, z_count, groups, rows, lanes), BF16),
        in_specs=[pl.BlockSpec(memory_space=pltpu.VMEM)] * 2,
        out_specs=pl.BlockSpec(memory_space=pltpu.VMEM),
        compiler_params=pltpu.CompilerParams(vmem_limit_bytes=VMEM_BYTES),
    )(first, second)


def gram_kernel(rows_ref, out_ref):
    senders, images, groups, parts, vectors, lanes = rows_ref.shape
    total = senders * vectors
    for image in range(images):
        gram = jnp.zeros((total, total), F32)
        for group in range(groups):
            for part in range(parts):
                flat = rows_ref[:, image, group, part].reshape(total, lanes)
                gram += lax.dot_general(
                    flat, flat, (((1,), (1,)), ((), ())), preferred_element_type=F32
                )
        out_ref[image] = gram


def grams(rows):
    total = rows.shape[0] * rows.shape[4]
    return pl.pallas_call(
        gram_kernel,
        out_shape=jax.ShapeDtypeStruct((rows.shape[1], total, total), F32),
        in_specs=[pl.BlockSpec(memory_space=pltpu.VMEM)],
        out_specs=pl.BlockSpec(memory_space=pltpu.VMEM),
        compiler_params=pltpu.CompilerParams(vmem_limit_bytes=VMEM_BYTES),
    )(rows)


def inverse_factor(work_ref, matrix):
    order = matrix.shape[0]
    step = 8
    row = lax.broadcasted_iota(jnp.int32, (step, order), 0)
    lane = lax.broadcasted_iota(jnp.int32, (step, order), 1)
    at = lax.broadcasted_iota(jnp.int32, (order, order), 0)
    work_ref[:, :order] = matrix
    work_ref[:, order:] = jnp.where(at == lax.broadcasted_iota(jnp.int32, (order, order), 1), 1.0, 0.0)
    for begin in range(0, order, step):
        block = slice(begin, begin + step)
        left, right = work_ref[block, :order], work_ref[block, order:]
        columns = [
            jnp.broadcast_to(left[:, begin + k : begin + k + 1], (step, order)) for k in range(step)
        ]
        for k in range(step):
            root = lax.rsqrt(columns[k][k : k + 1])
            factor = columns[k] * root

            def eliminate(value):
                pivot = value[k : k + 1] * root
                return jnp.where(row == k, pivot, jnp.where(row > k, value - factor * pivot, value))

            left, right = eliminate(left), eliminate(right)
            columns = columns[: k + 1] + [eliminate(c) for c in columns[k + 1 :]]
        work_ref[block, order:] = right
        after = begin + step
        if after < order:
            kept = jnp.where(lane >= after, left, 0.0)
            change = lax.dot_general(
                kept,
                jnp.concatenate([kept, right], axis=1),
                (((0,), (0,)), ((), ())),
                precision=HIGH,
                preferred_element_type=F32,
            )
            work_ref[after:, :] = work_ref[after:, :] - change[after:]
    return work_ref[:, order:]


def finish_kernel(scale, rows_ref, gram_ref, out_ref, work_ref):
    senders, groups, parts, vectors, lanes = rows_ref.shape
    total = senders * vectors
    exact = functools.partial(lax.dot_general, precision=HIGH, preferred_element_type=F32)
    across = (((1,), (1,)), ((), ()))
    plain = (((1,), (0,)), ((), ()))
    first = inverse_factor(work_ref, gram_ref[0])
    gram_second = exact(exact(first, gram_ref[1], plain), first, across)
    second = inverse_factor(work_ref, gram_second)
    mixing = exact(second, first, plain) * scale
    high = mixing.astype(BF16)
    rest = mixing - high.astype(F32)
    middle = rest.astype(BF16)
    low = (rest - middle.astype(F32)).astype(BF16)
    for group in range(groups):
        for part in range(parts):
            flat = rows_ref[:, group, part].reshape(total, lanes)
            turned = flat.astype(F32).T.astype(BF16)
            dot = functools.partial(
                lax.dot_general, turned, dimension_numbers=across, preferred_element_type=F32
            )
            out_ref[part, group] = (dot(low) + dot(middle)) + dot(high)


def finish(rows, gram_pair, scale):
    senders, groups, parts, vectors, lanes = rows.shape
    total = senders * vectors
    return pl.pallas_call(
        functools.partial(finish_kernel, scale),
        out_shape=jax.ShapeDtypeStruct((parts, groups, lanes, total), F32),
        in_specs=[pl.BlockSpec(memory_space=pltpu.VMEM)] * 2,
        out_specs=pl.BlockSpec(memory_space=pltpu.VMEM),
        scratch_shapes=[pltpu.VMEM((total, 2 * total), F32)],
        compiler_params=pltpu.CompilerParams(vmem_limit_bytes=VMEM_BYTES),
    )(rows, gram_pair)


def turn_kernel(start_ref, out_ref):
    parts, freqs, own, vectors = start_ref.shape
    receivers, groups, mine, lanes = out_ref.shape
    per_group = lanes // (parts * own)

    def group(index, carry):
        tiles = [
            start_ref[part, index * per_group + place]
            for place in range(per_group)
            for part in range(parts)
        ]
        turned = jnp.concatenate(tiles, axis=0).T
        out_ref[:, index] = turned.reshape(receivers, mine, lanes).astype(BF16)
        return carry

    lax.fori_loop(0, groups, group, 0)


def turn(start, receivers, lanes):
    parts, freqs, own, vectors = start.shape
    groups = parts * freqs * own // lanes
    return pl.pallas_call(
        turn_kernel,
        out_shape=jax.ShapeDtypeStruct((receivers, groups, vectors // receivers, lanes), BF16),
        in_specs=[pl.BlockSpec(memory_space=pltpu.VMEM)],
        out_specs=pl.BlockSpec(memory_space=pltpu.VMEM),
        compiler_params=pltpu.CompilerParams(vmem_limit_bytes=VMEM_BYTES),
    )(start)


def operand_kernel(own, rows_ref, out_ref):
    cores, x_count, z_count, groups, mine, lanes = rows_ref.shape
    parts = lanes // (z_count * own)
    width = parts * own
    lane = lax.broadcasted_iota(jnp.int32, (mine, lanes), 1)
    is_real = (lane // own) % 2 == 0

    def group(index, carry):
        x_index = index // (cores * groups)
        core, at = (index // groups) % cores, index % groups
        tiles = [rows_ref[core, x_index, z, at].astype(F32) for z in range(z_count)]
        for place in range(z_count):
            top = tiles[0]
            for z in range(z_count):
                top = jnp.where(lane // width == z, rolled(tiles[z], (z - place) * width), top)
            bottom = jnp.where(is_real, rolled(top, -own), -rolled(top, own))
            out_ref[index * z_count + place] = jnp.concatenate([top, bottom], axis=0).astype(BF16)
        return carry

    lax.fori_loop(0, x_count * cores * groups, group, 0, unroll=2)


def start_operand(rows, own):
    cores, x_count, z_count, groups, mine, lanes = rows.shape
    freqs = x_count * cores * groups * z_count
    return pl.pallas_call(
        functools.partial(operand_kernel, own),
        out_shape=jax.ShapeDtypeStruct((freqs, 2 * mine, lanes), BF16),
        in_specs=[pl.BlockSpec(memory_space=pltpu.VMEM)],
        out_specs=pl.BlockSpec(memory_space=pltpu.VMEM),
        compiler_params=pltpu.CompilerParams(vmem_limit_bytes=VMEM_BYTES),
    )(rows)


def swap_cores(value):
    return lax.ppermute(value, "core", [(0, 1), (1, 0)])


def gather_ring(sets, x_count, z_count):
    count = x_count * z_count
    ring = [k if k < z_count else z_count + count - 1 - k for k in range(count)]
    pairs = {
        1: [(ring[k], ring[(k + 1) % count]) for k in range(count)],
        -1: [(ring[(k + 1) % count], ring[k]) for k in range(count)],
    }
    x_place, z_place = lax.axis_index("x"), lax.axis_index("fc")
    place = jnp.where(x_place == 0, z_place, count - 1 - z_place)
    freqs, rows, depth = sets[0][0].shape
    cores = len(sets[0])
    wholes = [jnp.zeros((x_count, cores, freqs, z_count, rows, depth), BF16) for _ in sets]

    def put(chunk, core, piece, at):
        x_at = at // z_count
        z_at = jnp.where(x_at == 0, at, count - 1 - at)
        wholes[chunk] = lax.dynamic_update_slice(
            wholes[chunk], piece[None, None, :, None], (x_at, core, 0, z_at, 0, 0)
        )

    moving = {
        (chunk, core, way): sets[chunk][core]
        for chunk in range(len(sets))
        for core in range(cores)
        for way in (1, -1)
    }
    arrived = []
    for hop in range(1, count // 2 + 1):
        for (chunk, core, way), piece in moving.items():
            if 2 * hop == count and (way == 1) != (core == 0):
                continue
            piece = lax.ppermute(piece, ("x", "fc"), pairs[way])
            moving[chunk, core, way] = piece
            arrived.append((chunk, core, piece, (place - way * hop) % count))
    for chunk, pieces in enumerate(sets):
        for core, piece in enumerate(pieces):
            put(chunk, core, piece, place)
    for item in arrived:
        put(*item)
    return [w.reshape(x_count * cores * freqs, z_count * rows, depth) for w in wholes]


def sum_devices(value, z_count):
    value = value + swap_cores(value)
    value = value + lax.ppermute(value, "x", [(0, 1), (1, 0)])
    if z_count & (z_count - 1):
        return lax.psum(value, "fc")
    parts = [lax.ppermute(value, "fc", [(j, j ^ s) for j in range(z_count)]) for s in range(1, z_count)]
    even = z_count == 1
    if even:
        return value
    place = lax.axis_index("fc")
    stacked = jnp.stack([value] + parts)
    ordered = [lax.dynamic_index_in_dim(stacked, place ^ s, 0, False) for s in range(z_count)]
    return functools.reduce(jnp.add, ordered)


def body_split(x_count, z_count, chunks, beam_transfer, noise_var, spectra, freq_covariance, start_vectors):
    parts, freqs, own, multipoles = beam_transfer.shape
    vectors = start_vectors.shape[3]
    cores = 2
    core = lax.axis_index("core")
    all_freqs = x_count * cores * freqs
    mine = vectors // (x_count * z_count)
    depth = multipoles // (cores * chunks)

    whitened = (beam_transfer.astype(F32) * lax.rsqrt(noise_var)[None, :, :, None]).astype(BF16)
    rows = whitened.transpose(1, 0, 2, 3).reshape(freqs, parts * own, cores, chunks, depth)
    rows = rows.transpose(2, 3, 0, 1, 4)
    kept = lax.dynamic_index_in_dim(rows, core, 0, False)
    given = swap_cores(lax.dynamic_index_in_dim(rows, 1 - core, 0, False))
    sets = [
        [
            jnp.where(core == 0, kept[chunk], given[chunk]),
            jnp.where(core == 0, given[chunk], kept[chunk]),
        ]
        for chunk in range(chunks)
    ]
    beams = gather_ring(sets, x_count, z_count)

    spec = spectra.reshape(-1, cores, chunks, depth).transpose(1, 2, 0, 3)
    spec = lax.dynamic_index_in_dim(spec, core, 0, False)
    cov = freq_covariance.transpose(1, 0, 2).reshape(all_freqs, -1).astype(BF16)

    start = turn(start_vectors, x_count * z_count, z_count * parts * own)
    start = lax.all_to_all(start, ("x", "fc"), 0, 0, tiled=True)
    other = swap_cores(start)
    both = jnp.stack([jnp.where(core == 0, start, other), jnp.where(core == 0, other, start)])
    operand = start_operand(both.reshape(cores, x_count, z_count, *both.shape[2:]), own)

    added = ()
    for chunk in range(chunks):
        first_own = apply_covariance(
            [operand], [beams[chunk]], cov, spec[chunk : chunk + 1], own, added
        )
        added = (first_own,)
    first_other = swap_cores(first_own)
    second_own = apply_covariance([first_own, first_other], beams, cov, spec, own)

    def of_core(value, which):
        split = value.reshape(x_count, cores, freqs, *value.shape[1:])
        return lax.dynamic_index_in_dim(split, which, 1, False).reshape(-1, *value.shape[1:])

    first_packed = pack(of_core(first_own, core), of_core(first_other, core), x_count, z_count, own)
    second_other = swap_cores(of_core(second_own, 1 - core))
    second_packed = pack(of_core(second_own, core), second_other, x_count, z_count, own)
    packed = jnp.stack([first_packed, second_packed], axis=2)
    packed = packed.reshape(x_count * z_count, *packed.shape[2:])
    received = lax.all_to_all(packed, ("x", "fc"), 0, 0, tiled=True)
    groups, lanes = received.shape[2], received.shape[4]
    received = received.reshape(-1, ITERS, groups, parts, mine, lanes)

    gram_pair = sum_devices(grams(received), z_count)
    basis = finish(received[:, 1], gram_pair, math.sqrt(2.0 * all_freqs * z_count * own))
    return basis.reshape(parts, freqs, own, vectors)


def row_operands(row_part, spectra):
    scaled = (row_part.astype(F32)[None] * spectra[:, None, None, :]).astype(BF16)
    real_rows = jnp.concatenate([scaled[:, 0], scaled[:, 1]], axis=-1)
    imag_rows = jnp.concatenate([scaled[:, 1], -scaled[:, 0]], axis=-1)
    return jnp.stack([real_rows, imag_rows], axis=1)


def apply_tile(pair_tile, vec_bf):
    row_count = pair_tile.shape[1]
    stacked = pair_tile.reshape(2 * row_count, pair_tile.shape[2])
    with_real = jnp.dot(stacked, vec_bf[0], preferred_element_type=F32)
    with_imag = jnp.dot(stacked, vec_bf[1], preferred_element_type=F32)
    real_part = with_real[:row_count] - with_imag[row_count:]
    imag_part = with_real[row_count:] + with_imag[:row_count]
    return jnp.stack([real_part, imag_part], axis=0)


def partial_gram(image):
    flat = image.reshape(-1, image.shape[-1])
    return jnp.dot(flat.T, flat, precision=HIGH, preferred_element_type=F32)


def orthonormalize(image, gram_matrix):
    lower = jnp.linalg.cholesky(gram_matrix)
    flat = image.reshape(-1, image.shape[-1])
    solved = lax.linalg.triangular_solve(lower, flat, left_side=False, lower=True, transpose_a=True)
    return solved.reshape(image.shape)


def body_general(beam_transfer, noise_var, spectra, freq_covariance, start_vectors):
    row_axes = ("x", "core")
    whitened = (beam_transfer.astype(F32) * lax.rsqrt(noise_var)[None, :, :, None]).astype(BF16)
    row_beams = lax.all_gather(whitened, "fc", axis=2, tiled=True)
    _, freq_rows, mode_count, multipoles = row_beams.shape
    row_total = freq_rows * mode_count
    components = spectra.shape[0]
    vectors_count = start_vectors.shape[3]
    row_operand = row_operands(row_beams.reshape(2, row_total, multipoles), spectra)
    row_start = lax.axis_index(row_axes) * freq_rows
    row_cov = lax.dynamic_slice_in_dim(freq_covariance, row_start, freq_rows, 1)
    piece = lax.all_gather(whitened, row_axes, axis=1, tiled=True)
    _, piece_freqs, piece_modes, _ = piece.shape
    columns = piece.reshape(2, piece_freqs * piece_modes, multipoles)
    col_operand = jnp.concatenate([columns[0], columns[1]], axis=-1)
    products = lax.dot_general(
        row_operand, col_operand, (((3,), (1,)), ((), ())), preferred_element_type=F32
    )
    weight = jnp.broadcast_to(
        row_cov[:, :, None, :, None], (components, freq_rows, mode_count, piece_freqs, piece_modes)
    )
    weight = weight.reshape(components, row_total, piece_freqs * piece_modes)
    pair_tile = jnp.einsum("kxy,kcxy->cxy", weight, products).astype(BF16)
    vectors = start_vectors
    own_modes = start_vectors.shape[2]
    for _ in range(ITERS):
        gathered = lax.all_gather(vectors.astype(BF16), row_axes, axis=1, tiled=True)
        vec_bf = gathered.reshape(2, -1, vectors_count)
        partial_value = apply_tile(pair_tile, vec_bf).reshape(2, freq_rows, mode_count, vectors_count)
        summed = lax.psum(partial_value, "fc")
        gram_matrix = lax.psum(partial_gram(summed), row_axes)
        own_rows = lax.dynamic_slice_in_dim(summed, lax.axis_index("fc") * own_modes, own_modes, 2)
        vectors = orthonormalize(own_rows, gram_matrix)
    return vectors * math.sqrt(2.0 * piece_freqs * mode_count)


def body(x_count, z_count, *args):
    beam_transfer, start_vectors = args[0], args[4]
    parts, freqs, own, multipoles = beam_transfer.shape
    vectors = start_vectors.shape[3]
    lanes = parts * own * z_count
    chunks = multipoles // (2 * 128)
    fits = (
        x_count == 2
        and vectors % (16 * x_count * z_count) == 0
        and lanes == 128
        and own % 16 == 0
        and chunks * 256 == multipoles
        and (freqs * own) % lanes == 0
    )
    if fits:
        return body_split(x_count, z_count, chunks, *args)
    return body_general(*args)


def solution(mesh):
    sizes = dict(mesh.shape)
    x_count = sizes["fr"] // 2
    shape = (sizes["ma"], x_count, 2, sizes["fc"])
    devices = mesh.devices.reshape(shape)
    split = Mesh(devices, ("ma", "x", "core", "fc"))
    rows = ("ma", "x", "core")
    in_specs = (
        P(None, rows, "fc", None),
        P(rows, "fc"),
        P(),
        P(),
        P(None, rows, "fc", None),
    )
    return jax.shard_map(
        functools.partial(body, x_count, sizes["fc"]),
        mesh=split,
        in_specs=in_specs,
        out_specs=P(None, rows, "fc", None),
        check_vma=False,
    )
```

```python
import functools
import math

import jax
import jax.numpy as jnp
from jax import lax
from jax.experimental import pallas as pl
from jax.experimental.pallas import tpu as pltpu
from jax.sharding import Mesh
from jax.sharding import PartitionSpec as P

ITERS = 2
BF16 = jnp.bfloat16
F32 = jnp.float32
VMEM_BYTES = 56 * 1024 * 1024
HIGH = lax.Precision.HIGHEST


def rolled(value, shift):
    return pltpu.roll(value, shift % value.shape[-1], 1)


def apply_kernel(n_vec, z_count, own, offsets, *refs):
    place_ref, *refs = refs
    vec_refs = (refs[:n_vec], refs[n_vec : 2 * n_vec])
    piece_refs = refs[2 * n_vec : 2 * n_vec + len(offsets)]
    cov_ref, spec_ref, mine_ref, theirs_ref, beam_ref, vec_ref, *tiles, sems = refs[2 * n_vec + len(offsets) :]
    z_refs, y_refs = tiles[: len(tiles) // 2], tiles[len(tiles) // 2 :]
    out_refs = (mine_ref, theirs_ref)
    count, rows, lanes = mine_ref.shape
    freqs = 2 * count
    half = rows // 2
    components = spec_ref.shape[0]
    size, width, depth = piece_refs[0].shape
    chips = count // size * z_count
    step = depth // len(z_refs)
    lane = lax.broadcasted_iota(jnp.int32, (half, lanes), 1)
    is_real = (lane // own) % 2 == 0
    sign = jnp.where(is_real, -1.0, 1.0).astype(F32)

    copies = []
    for index, (core, offset) in enumerate(offsets):
        at = lax.rem(place_ref[0] + (offset % chips), chips)
        x_at = at // z_count
        z_at = jnp.where(x_at == 0, at, chips - 1 - at)
        target = beam_ref.at[
            pl.ds(core * count + x_at * size, size), pl.ds(pl.multiple_of(z_at * width, width), width)
        ]
        copies.append(pltpu.make_async_copy(piece_refs[index], target, sems.at[index]))
    for copy in copies:
        copy.start()

    def gather(side, place, carry):
        vec = vec_refs[side][0][place]
        for other in vec_refs[side][1:]:
            vec = vec + other[place]
        vec_ref[side * count + place] = vec.astype(BF16)
        return carry

    for side in range(2):
        lax.fori_loop(0, count, functools.partial(gather, side), 0, unroll=8)
    for copy in copies:
        copy.wait()

    def project(freq, carry):
        z = jnp.dot(vec_ref[freq], beam_ref[freq], preferred_element_type=F32)
        for tile, z_ref in enumerate(z_refs):
            z_ref[pl.ds(freq, rows, stride=freqs), :] = z[:, tile * step : (tile + 1) * step]
        return carry

    lax.fori_loop(0, freqs, project, 0, unroll=32)

    def mix(row, carry):
        start = pl.multiple_of(row * freqs, freqs)
        z = jnp.concatenate([z_ref[pl.ds(start, freqs), :] for z_ref in z_refs], axis=1)
        scaled = [(z * spec_ref[k][None, :]).astype(BF16) for k in range(components)]
        y = jnp.dot(cov_ref[...], jnp.concatenate(scaled, axis=0), preferred_element_type=F32)
        for tile, y_ref in enumerate(y_refs):
            y_ref[pl.ds(start, freqs), :] = y[:, tile * step : (tile + 1) * step]
        return carry

    lax.fori_loop(0, rows, mix, 0, unroll=8)

    def expand(side, place, carry):
        freq = side * count + place
        y = [y_ref[pl.ds(freq, rows, stride=freqs), :].astype(BF16) for y_ref in y_refs]
        product = lax.dot_general(
            jnp.concatenate(y, axis=1),
            beam_ref[freq],
            (((1,), (1,)), ((), ())),
            preferred_element_type=F32,
        )
        swapped = jnp.where(
            jnp.concatenate([is_real, is_real], axis=0),
            rolled(product, -own),
            rolled(product, own),
        )
        top = product[:half] + sign * swapped[half:]
        bottom = product[half:] - sign * swapped[:half]
        out_refs[side][place] = jnp.concatenate([top, bottom], axis=0)
        return carry

    for side in range(2):
        lax.fori_loop(0, count, functools.partial(expand, side), 0, unroll=32)


def apply_covariance(place, vecs, beams, cov, spec, own, z_count):
    count, rows, lanes = vecs[0][0].shape
    freqs = 2 * count
    depth = spec.shape[1]
    step = min(depth, 128)
    flops = 2 * freqs * rows * (2 * lanes * depth + 2 * freqs * depth)
    vmem = pl.BlockSpec(memory_space=pltpu.VMEM)
    n_vec = len(vecs[0])
    offsets = tuple((core, offset) for _, core, offset in beams)
    tile = pltpu.VMEM((rows * freqs, step), F32)
    return pl.pallas_call(
        functools.partial(apply_kernel, n_vec, z_count, own, offsets),
        out_shape=[jax.ShapeDtypeStruct((count, rows, lanes), F32)] * 2,
        in_specs=[pl.BlockSpec(memory_space=pltpu.SMEM)]
        + [vmem] * (2 * n_vec)
        + [pl.BlockSpec(memory_space=pl.ANY)] * len(beams)
        + [vmem] * 2,
        out_specs=[vmem] * 2,
        scratch_shapes=[
            pltpu.VMEM((freqs, lanes, depth), BF16),
            pltpu.VMEM((freqs, rows, lanes), BF16),
            *[tile] * (2 * depth // step),
            pltpu.SemaphoreType.DMA((len(beams),)),
        ],
        compiler_params=pltpu.CompilerParams(vmem_limit_bytes=VMEM_BYTES),
        cost_estimate=pl.CostEstimate(
            flops=flops, bytes_accessed=freqs * lanes * depth * 2, transcendentals=0
        ),
    )(place, *vecs[0], *vecs[1], *[piece for piece, _, _ in beams], cov, spec)


def pack_kernel(own, *refs):
    out_ref = refs[-1]
    x_count, z_count, images, groups = out_ref.shape[:4]
    freqs, rows, lanes = refs[0].shape
    per_group = lanes // own
    lane = lax.broadcasted_iota(jnp.int32, (rows, lanes), 1) // own

    def group(step, index, carry):
        x_index, group_index = index // groups, index % groups
        totals = [jnp.zeros((rows, lanes), F32)] * z_count
        for place in range(per_group):
            freq = index * per_group + place
            image = refs[2 * step][freq] + refs[2 * step + 1][freq]
            for z_index in range(z_count):
                moved = rolled(image, (place - 2 * z_index) * own)
                totals[z_index] = jnp.where(lane == place, moved, totals[z_index])
        for z_index in range(z_count):
            out_ref[x_index, z_index, step, group_index] = totals[z_index].astype(BF16)
        return carry

    for step in range(images):
        lax.fori_loop(0, x_count * groups, functools.partial(group, step), 0)


def pack(pairs, x_count, z_count, own):
    freqs, rows, lanes = pairs[0][0].shape
    groups = freqs * own // (x_count * lanes)
    flat = [part for pair in pairs for part in pair]
    return pl.pallas_call(
        functools.partial(pack_kernel, own),
        out_shape=jax.ShapeDtypeStruct((x_count, z_count, len(pairs), groups, rows, lanes), BF16),
        in_specs=[pl.BlockSpec(memory_space=pltpu.VMEM)] * len(flat),
        out_specs=pl.BlockSpec(memory_space=pltpu.VMEM),
        compiler_params=pltpu.CompilerParams(vmem_limit_bytes=VMEM_BYTES),
    )(*flat)


def gram_kernel(core_ref, rows_ref, keep_ref, send_ref):
    senders, images, groups, parts, vectors, lanes = rows_ref.shape
    total = senders * vectors
    found = []
    for image in range(images):
        gram = jnp.zeros((total, total), F32)
        for group in range(groups):
            for part in range(parts):
                flat = rows_ref[:, image, group, part].reshape(total, lanes)
                gram += lax.dot_general(
                    flat, flat, (((1,), (1,)), ((), ())), preferred_element_type=F32
                )
        found.append(gram)
    is_first = core_ref[0] == 0
    keep_ref[...] = jnp.where(is_first, found[0], found[1])
    send_ref[...] = jnp.where(is_first, found[1], found[0])


def grams(core, rows):
    total = rows.shape[0] * rows.shape[4]
    return pl.pallas_call(
        gram_kernel,
        out_shape=[jax.ShapeDtypeStruct((total, total), F32)] * 2,
        in_specs=[pl.BlockSpec(memory_space=pltpu.SMEM), pl.BlockSpec(memory_space=pltpu.VMEM)],
        out_specs=[pl.BlockSpec(memory_space=pltpu.VMEM)] * 2,
        compiler_params=pltpu.CompilerParams(vmem_limit_bytes=VMEM_BYTES),
    )(core, rows)


def inverse_factor(work_ref, matrix):
    order = matrix.shape[0]
    step = 8
    row = lax.broadcasted_iota(jnp.int32, (step, order), 0)
    lane = lax.broadcasted_iota(jnp.int32, (step, order), 1)
    at = lax.broadcasted_iota(jnp.int32, (order, order), 0)
    work_ref[:, :order] = matrix
    work_ref[:, order:] = jnp.where(at == lax.broadcasted_iota(jnp.int32, (order, order), 1), 1.0, 0.0)
    for begin in range(0, order, step):
        block = slice(begin, begin + step)
        left, right = work_ref[block, :order], work_ref[block, order:]
        columns = [
            jnp.broadcast_to(left[:, begin + k : begin + k + 1], (step, order)) for k in range(step)
        ]
        for k in range(step):
            root = lax.rsqrt(columns[k][k : k + 1])
            factor = columns[k] * root

            def eliminate(value):
                pivot = value[k : k + 1] * root
                return jnp.where(row == k, pivot, jnp.where(row > k, value - factor * pivot, value))

            left, right = eliminate(left), eliminate(right)
            columns = columns[: k + 1] + [eliminate(c) for c in columns[k + 1 :]]
        work_ref[block, order:] = right
        after = begin + step
        if after < order:
            kept = jnp.where(lane >= after, left, 0.0)
            change = lax.dot_general(
                kept,
                jnp.concatenate([kept, right], axis=1),
                (((0,), (0,)), ((), ())),
                precision=HIGH,
                preferred_element_type=F32,
            )
            work_ref[after:, :] = work_ref[after:, :] - change[after:]
    return work_ref[:, order:]


def finish_kernel(scale, core_ref, rows_ref, kept_ref, given_ref, out_ref, work_ref):
    senders, groups, parts, vectors, lanes = rows_ref.shape
    total = senders * vectors
    exact = functools.partial(lax.dot_general, precision=HIGH, preferred_element_type=F32)
    across = (((1,), (1,)), ((), ()))
    plain = (((1,), (0,)), ((), ()))
    is_first = core_ref[0] == 0
    first = inverse_factor(work_ref, jnp.where(is_first, kept_ref[...], given_ref[...]))
    gram_second = jnp.where(is_first, given_ref[...], kept_ref[...])
    gram_second = exact(exact(first, gram_second, plain), first, across)
    second = inverse_factor(work_ref, gram_second)
    mixing = exact(second, first, plain) * scale
    high = mixing.astype(BF16)
    rest = mixing - high.astype(F32)
    middle = rest.astype(BF16)
    low = (rest - middle.astype(F32)).astype(BF16)
    for group in range(groups):
        for part in range(parts):
            flat = rows_ref[:, group, part].reshape(total, lanes)
            turned = flat.astype(F32).T.astype(BF16)
            dot = functools.partial(
                lax.dot_general, turned, dimension_numbers=across, preferred_element_type=F32
            )
            out_ref[part, group] = (dot(low) + dot(middle)) + dot(high)


def finish(core, rows, kept, given, scale):
    senders, groups, parts, vectors, lanes = rows.shape
    total = senders * vectors
    return pl.pallas_call(
        functools.partial(finish_kernel, scale),
        out_shape=jax.ShapeDtypeStruct((parts, groups, lanes, total), F32),
        in_specs=[pl.BlockSpec(memory_space=pltpu.SMEM)] + [pl.BlockSpec(memory_space=pltpu.VMEM)] * 3,
        out_specs=pl.BlockSpec(memory_space=pltpu.VMEM),
        scratch_shapes=[pltpu.VMEM((total, 2 * total), F32)],
        compiler_params=pltpu.CompilerParams(vmem_limit_bytes=VMEM_BYTES),
    )(core, rows, kept, given)


def turn_kernel(start_ref, out_ref):
    parts, freqs, own, vectors = start_ref.shape
    receivers, groups, mine, lanes = out_ref.shape
    per_group = lanes // (parts * own)

    def group(index, carry):
        tiles = [
            start_ref[part, index * per_group + place]
            for place in range(per_group)
            for part in range(parts)
        ]
        turned = jnp.concatenate(tiles, axis=0).T
        out_ref[:, index] = turned.reshape(receivers, mine, lanes).astype(BF16)
        return carry

    lax.fori_loop(0, groups, group, 0)


def turn(start, receivers, lanes):
    parts, freqs, own, vectors = start.shape
    groups = parts * freqs * own // lanes
    return pl.pallas_call(
        turn_kernel,
        out_shape=jax.ShapeDtypeStruct((receivers, groups, vectors // receivers, lanes), BF16),
        in_specs=[pl.BlockSpec(memory_space=pltpu.VMEM)],
        out_specs=pl.BlockSpec(memory_space=pltpu.VMEM),
        compiler_params=pltpu.CompilerParams(vmem_limit_bytes=VMEM_BYTES),
    )(start)


def operand_kernel(own, *refs):
    x_count, z_count, groups, mine, lanes = refs[0].shape
    parts = lanes // (z_count * own)
    width = parts * own
    lane = lax.broadcasted_iota(jnp.int32, (mine, lanes), 1)
    is_real = (lane // own) % 2 == 0

    def group(side, index, carry):
        x_index, at = index // groups, index % groups
        tiles = [refs[side][x_index, z, at].astype(F32) for z in range(z_count)]
        for place in range(z_count):
            top = tiles[0]
            for z in range(z_count):
                top = jnp.where(lane // width == z, rolled(tiles[z], (z - place) * width), top)
            bottom = jnp.where(is_real, rolled(top, -own), -rolled(top, own))
            image = jnp.concatenate([top, bottom], axis=0).astype(BF16)
            refs[2 + side][index * z_count + place] = image
        return carry

    for side in range(2):
        lax.fori_loop(0, x_count * groups, functools.partial(group, side), 0, unroll=2)


def start_operand(sides, own):
    x_count, z_count, groups, mine, lanes = sides[0].shape
    freqs = x_count * groups * z_count
    return pl.pallas_call(
        functools.partial(operand_kernel, own),
        out_shape=[jax.ShapeDtypeStruct((freqs, 2 * mine, lanes), BF16)] * 2,
        in_specs=[pl.BlockSpec(memory_space=pltpu.VMEM)] * 2,
        out_specs=[pl.BlockSpec(memory_space=pltpu.VMEM)] * 2,
        compiler_params=pltpu.CompilerParams(vmem_limit_bytes=VMEM_BYTES),
    )(*sides)


def swap_cores(value):
    return lax.ppermute(value, "core", [(0, 1), (1, 0)])


def after(value, event):
    return lax.optimization_barrier((value, event))


def gather_ring(blocks, late, x_count, z_count):
    count = x_count * z_count
    ring = [k if k < z_count else z_count + count - 1 - k for k in range(count)]
    pairs = {
        1: [(ring[k], ring[(k + 1) % count]) for k in range(count)],
        -1: [(ring[(k + 1) % count], ring[k]) for k in range(count)],
    }
    x_place, z_place = lax.axis_index("x"), lax.axis_index("fc")
    place = jnp.where(x_place == 0, z_place, count - 1 - z_place).astype(jnp.int32).reshape(1)
    moving = {(core, way): block for core, block in enumerate(blocks) for way in (1, -1)}
    found = [(block, core, 0) for core, block in enumerate(blocks)]
    for hop in range(1, count // 2 + 1):
        for core, way in moving:
            if 2 * hop == count and (way == 1) != (core == 0):
                continue
            moving[core, way] = lax.ppermute(moving[core, way], ("x", "fc"), pairs[way])
            if hop == 1 and core == 0 and way == 1:
                late, moving[core, way] = after(late, moving[core, way])
            found.append((moving[core, way], core, -way * hop))
    return place, found, late


def sum_devices(keep, send, z_count):
    value = keep + swap_cores(send)
    value = value + lax.ppermute(value, "x", [(0, 1), (1, 0)])
    if z_count & (z_count - 1):
        value = lax.psum(value, "fc")
    else:
        terms = [value] + [
            lax.ppermute(value, "fc", [(j, j ^ s) for j in range(z_count)]) for s in range(1, z_count)
        ]
        while len(terms) > 1:
            terms = [terms[i] + terms[i + 1] for i in range(0, len(terms), 2)]
        value = terms[0]
    return value, swap_cores(value)


def body_split(x_count, z_count, beam_transfer, noise_var, spectra, freq_covariance, start_vectors):
    parts, freqs, own, multipoles = beam_transfer.shape
    vectors = start_vectors.shape[3]
    cores = 2
    core = lax.axis_index("core")
    all_freqs = x_count * cores * freqs
    mine_vectors = vectors // (x_count * z_count)
    depth = multipoles // cores

    whitened = (beam_transfer.astype(F32) * lax.rsqrt(noise_var)[None, :, :, None]).astype(BF16)
    rows = whitened.transpose(1, 0, 2, 3).reshape(freqs, parts * own, cores, depth)
    rows = rows.transpose(2, 0, 1, 3)
    kept = lax.dynamic_index_in_dim(rows, core, 0, False)
    given = swap_cores(lax.dynamic_index_in_dim(rows, 1 - core, 0, False))
    start = turn(start_vectors, x_count * z_count, z_count * parts * own)
    place, beams, start = gather_ring([kept, given], start, x_count, z_count)

    spec = spectra.reshape(-1, cores, depth)
    spec = lax.dynamic_index_in_dim(spec, core, 1, False)
    cov = freq_covariance.reshape(-1, x_count, cores, freqs, x_count, cores, freqs).astype(BF16)
    cov = jnp.where(core == 0, cov, jnp.flip(cov, (2, 5)))
    cov = cov.transpose(2, 1, 3, 0, 5, 4, 6).reshape(all_freqs, -1)

    start = lax.all_to_all(start, ("x", "fc"), 0, 0, tiled=True)
    start = start.reshape(x_count, z_count, *start.shape[1:])
    operand = start_operand([start, swap_cores(start)], own)

    mine, theirs = apply_covariance(
        place, [[operand[0]], [operand[1]]], beams, cov, spec, own, z_count
    )
    got_mine, got_theirs = swap_cores(theirs), swap_cores(mine)
    second_mine, second_theirs = apply_covariance(
        place, [[mine, got_mine], [theirs, got_theirs]], beams, cov, spec, own, z_count
    )
    packed = pack(
        [(mine, got_mine), (second_mine, swap_cores(second_theirs))], x_count, z_count, own
    )
    packed = packed.reshape(x_count * z_count, *packed.shape[2:])
    received = lax.all_to_all(packed, ("x", "fc"), 0, 0, tiled=True)
    groups, lanes = received.shape[2], received.shape[4]
    received = received.reshape(-1, ITERS, groups, parts, mine_vectors, lanes)

    core_index = core.astype(jnp.int32).reshape(1)
    kept_gram, given_gram = sum_devices(*grams(core_index, received), z_count)
    scale = math.sqrt(2.0 * all_freqs * z_count * own)
    basis = finish(core_index, received[:, 1], kept_gram, given_gram, scale)
    return basis.reshape(parts, freqs, own, vectors)


def row_operands(row_part, spectra):
    scaled = (row_part.astype(F32)[None] * spectra[:, None, None, :]).astype(BF16)
    real_rows = jnp.concatenate([scaled[:, 0], scaled[:, 1]], axis=-1)
    imag_rows = jnp.concatenate([scaled[:, 1], -scaled[:, 0]], axis=-1)
    return jnp.stack([real_rows, imag_rows], axis=1)


def apply_tile(pair_tile, vec_bf):
    row_count = pair_tile.shape[1]
    stacked = pair_tile.reshape(2 * row_count, pair_tile.shape[2])
    with_real = jnp.dot(stacked, vec_bf[0], preferred_element_type=F32)
    with_imag = jnp.dot(stacked, vec_bf[1], preferred_element_type=F32)
    real_part = with_real[:row_count] - with_imag[row_count:]
    imag_part = with_real[row_count:] + with_imag[:row_count]
    return jnp.stack([real_part, imag_part], axis=0)


def partial_gram(image):
    flat = image.reshape(-1, image.shape[-1])
    return jnp.dot(flat.T, flat, precision=HIGH, preferred_element_type=F32)


def orthonormalize(image, gram_matrix):
    lower = jnp.linalg.cholesky(gram_matrix)
    flat = image.reshape(-1, image.shape[-1])
    solved = lax.linalg.triangular_solve(lower, flat, left_side=False, lower=True, transpose_a=True)
    return solved.reshape(image.shape)


def body_general(beam_transfer, noise_var, spectra, freq_covariance, start_vectors):
    row_axes = ("x", "core")
    whitened = (beam_transfer.astype(F32) * lax.rsqrt(noise_var)[None, :, :, None]).astype(BF16)
    row_beams = lax.all_gather(whitened, "fc", axis=2, tiled=True)
    _, freq_rows, mode_count, multipoles = row_beams.shape
    row_total = freq_rows * mode_count
    components = spectra.shape[0]
    vectors_count = start_vectors.shape[3]
    row_operand = row_operands(row_beams.reshape(2, row_total, multipoles), spectra)
    row_start = lax.axis_index(row_axes) * freq_rows
    row_cov = lax.dynamic_slice_in_dim(freq_covariance, row_start, freq_rows, 1)
    piece = lax.all_gather(whitened, row_axes, axis=1, tiled=True)
    _, piece_freqs, piece_modes, _ = piece.shape
    columns = piece.reshape(2, piece_freqs * piece_modes, multipoles)
    col_operand = jnp.concatenate([columns[0], columns[1]], axis=-1)
    products = lax.dot_general(
        row_operand, col_operand, (((3,), (1,)), ((), ())), preferred_element_type=F32
    )
    weight = jnp.broadcast_to(
        row_cov[:, :, None, :, None], (components, freq_rows, mode_count, piece_freqs, piece_modes)
    )
    weight = weight.reshape(components, row_total, piece_freqs * piece_modes)
    pair_tile = jnp.einsum("kxy,kcxy->cxy", weight, products).astype(BF16)
    vectors = start_vectors
    own_modes = start_vectors.shape[2]
    for _ in range(ITERS):
        gathered = lax.all_gather(vectors.astype(BF16), row_axes, axis=1, tiled=True)
        vec_bf = gathered.reshape(2, -1, vectors_count)
        partial_value = apply_tile(pair_tile, vec_bf).reshape(2, freq_rows, mode_count, vectors_count)
        summed = lax.psum(partial_value, "fc")
        gram_matrix = lax.psum(partial_gram(summed), row_axes)
        own_rows = lax.dynamic_slice_in_dim(summed, lax.axis_index("fc") * own_modes, own_modes, 2)
        vectors = orthonormalize(own_rows, gram_matrix)
    return vectors * math.sqrt(2.0 * piece_freqs * mode_count)


def body(x_count, z_count, *args):
    beam_transfer, start_vectors = args[0], args[4]
    parts, freqs, own, multipoles = beam_transfer.shape
    vectors = start_vectors.shape[3]
    lanes = parts * own * z_count
    fits = (
        x_count == 2
        and vectors % (16 * x_count * z_count) == 0
        and lanes == 128
        and own % 16 == 0
        and multipoles % 256 == 0
        and (freqs * own) % lanes == 0
    )
    if fits:
        return body_split(x_count, z_count, *args)
    return body_general(*args)


def solution(mesh):
    sizes = dict(mesh.shape)
    x_count = sizes["fr"] // 2
    shape = (sizes["ma"], x_count, 2, sizes["fc"])
    devices = mesh.devices.reshape(shape)
    split = Mesh(devices, ("ma", "x", "core", "fc"))
    rows = ("ma", "x", "core")
    in_specs = (
        P(None, rows, "fc", None),
        P(rows, "fc"),
        P(),
        P(),
        P(None, rows, "fc", None),
    )
    return jax.shard_map(
        functools.partial(body, x_count, sizes["fc"]),
        mesh=split,
        in_specs=in_specs,
        out_specs=P(None, rows, "fc", None),
        check_vma=False,
    )
```

```python
import functools
import math

import jax
import jax.numpy as jnp
from jax import lax
from jax.experimental import pallas as pl
from jax.experimental.pallas import tpu as pltpu
from jax.sharding import Mesh
from jax.sharding import PartitionSpec as P

ITERS = 2
BF16 = jnp.bfloat16
F32 = jnp.float32
VMEM_BYTES = 56 * 1024 * 1024
HIGH = lax.Precision.HIGHEST


def rolled(value, shift):
    return pltpu.roll(value, shift % value.shape[-1], 1)


def apply_kernel(n_vec, z_count, own, offsets, *refs):
    place_ref, *refs = refs
    vec_refs = (refs[:n_vec], refs[n_vec : 2 * n_vec])
    piece_refs = refs[2 * n_vec : 2 * n_vec + len(offsets)]
    cov_ref, spec_ref, mine_ref, theirs_ref, beam_ref, vec_ref, *tiles, sems = refs[2 * n_vec + len(offsets) :]
    z_refs, y_refs = tiles[: len(tiles) // 2], tiles[len(tiles) // 2 :]
    out_refs = (mine_ref, theirs_ref)
    count, rows, lanes = mine_ref.shape
    freqs = 2 * count
    half = rows // 2
    components = spec_ref.shape[0]
    size, width, depth = piece_refs[0].shape
    chips = count // size * z_count
    step = depth // len(z_refs)
    lane = lax.broadcasted_iota(jnp.int32, (half, lanes), 1)
    is_real = (lane // own) % 2 == 0
    sign = jnp.where(is_real, -1.0, 1.0).astype(F32)

    copies = []
    for index, (core, offset) in enumerate(offsets):
        at = lax.rem(place_ref[0] + (offset % chips), chips)
        x_at = at // z_count
        z_at = jnp.where(x_at == 0, at, chips - 1 - at)
        target = beam_ref.at[
            pl.ds(core * count + x_at * size, size), pl.ds(pl.multiple_of(z_at * width, width), width)
        ]
        copies.append(pltpu.make_async_copy(piece_refs[index], target, sems.at[index]))
    for copy in copies:
        copy.start()

    def gather(side, place, carry):
        vec = vec_refs[side][0][place]
        for other in vec_refs[side][1:]:
            vec = vec + other[place]
        vec_ref[side * count + place] = vec.astype(BF16)
        return carry

    for side in range(2):
        lax.fori_loop(0, count, functools.partial(gather, side), 0, unroll=8)
    for copy in copies:
        copy.wait()

    def project(freq, carry):
        z = jnp.dot(vec_ref[freq], beam_ref[freq], preferred_element_type=F32)
        for tile, z_ref in enumerate(z_refs):
            z_ref[pl.ds(freq, rows, stride=freqs), :] = z[:, tile * step : (tile + 1) * step]
        return carry

    lax.fori_loop(0, freqs, project, 0, unroll=32)

    def mix(row, carry):
        start = pl.multiple_of(row * freqs, freqs)
        z = jnp.concatenate([z_ref[pl.ds(start, freqs), :] for z_ref in z_refs], axis=1)
        scaled = [(z * spec_ref[k][None, :]).astype(BF16) for k in range(components)]
        y = jnp.dot(cov_ref[...], jnp.concatenate(scaled, axis=0), preferred_element_type=F32)
        for tile, y_ref in enumerate(y_refs):
            y_ref[pl.ds(start, freqs), :] = y[:, tile * step : (tile + 1) * step]
        return carry

    lax.fori_loop(0, rows, mix, 0, unroll=8)

    def expand(side, place, carry):
        freq = side * count + place
        y = [y_ref[pl.ds(freq, rows, stride=freqs), :].astype(BF16) for y_ref in y_refs]
        product = lax.dot_general(
            jnp.concatenate(y, axis=1),
            beam_ref[freq],
            (((1,), (1,)), ((), ())),
            preferred_element_type=F32,
        )
        swapped = jnp.where(
            jnp.concatenate([is_real, is_real], axis=0),
            rolled(product, -own),
            rolled(product, own),
        )
        top = product[:half] + sign * swapped[half:]
        bottom = product[half:] - sign * swapped[:half]
        out_refs[side][place] = jnp.concatenate([top, bottom], axis=0)
        return carry

    for side in range(2):
        lax.fori_loop(0, count, functools.partial(expand, side), 0, unroll=32)


def apply_covariance(place, vecs, beams, cov, spec, own, z_count):
    count, rows, lanes = vecs[0][0].shape
    freqs = 2 * count
    depth = spec.shape[1]
    step = min(depth, 128)
    flops = 2 * freqs * rows * (2 * lanes * depth + 2 * freqs * depth)
    vmem = pl.BlockSpec(memory_space=pltpu.VMEM)
    n_vec = len(vecs[0])
    offsets = tuple((core, offset) for _, core, offset in beams)
    tile = pltpu.VMEM((rows * freqs, step), F32)
    return pl.pallas_call(
        functools.partial(apply_kernel, n_vec, z_count, own, offsets),
        out_shape=[jax.ShapeDtypeStruct((count, rows, lanes), F32)] * 2,
        in_specs=[pl.BlockSpec(memory_space=pltpu.SMEM)]
        + [vmem] * (2 * n_vec)
        + [pl.BlockSpec(memory_space=pl.ANY)] * len(beams)
        + [vmem] * 2,
        out_specs=[vmem] * 2,
        scratch_shapes=[
            pltpu.VMEM((freqs, lanes, depth), BF16),
            pltpu.VMEM((freqs, rows, lanes), BF16),
            *[tile] * (2 * depth // step),
            pltpu.SemaphoreType.DMA((len(beams),)),
        ],
        compiler_params=pltpu.CompilerParams(vmem_limit_bytes=VMEM_BYTES),
        cost_estimate=pl.CostEstimate(
            flops=flops, bytes_accessed=freqs * lanes * depth * 2, transcendentals=0
        ),
    )(place, *vecs[0], *vecs[1], *[piece for piece, _, _ in beams], cov, spec)


def pack_kernel(own, first_ref, second_ref, out_ref):
    x_count, z_count, groups = out_ref.shape[:3]
    freqs, rows, lanes = first_ref.shape
    per_group = lanes // own
    lane = lax.broadcasted_iota(jnp.int32, (rows, lanes), 1) // own

    def group(index, carry):
        x_index, group_index = index // groups, index % groups
        totals = [jnp.zeros((rows, lanes), F32)] * z_count
        for place in range(per_group):
            freq = index * per_group + place
            image = first_ref[freq] + second_ref[freq]
            for z_index in range(z_count):
                moved = rolled(image, (place - 2 * z_index) * own)
                totals[z_index] = jnp.where(lane == place, moved, totals[z_index])
        for z_index in range(z_count):
            out_ref[x_index, z_index, group_index] = totals[z_index].astype(BF16)
        return carry

    lax.fori_loop(0, x_count * groups, group, 0, unroll=2)


def pack(first, second, x_count, z_count, own):
    freqs, rows, lanes = first.shape
    groups = freqs * own // (x_count * lanes)
    return pl.pallas_call(
        functools.partial(pack_kernel, own),
        out_shape=jax.ShapeDtypeStruct((x_count, z_count, groups, rows, lanes), BF16),
        in_specs=[pl.BlockSpec(memory_space=pltpu.VMEM)] * 2,
        out_specs=pl.BlockSpec(memory_space=pltpu.VMEM),
        compiler_params=pltpu.CompilerParams(vmem_limit_bytes=VMEM_BYTES),
    )(first, second)


def gram_kernel(core_ref, rows_ref, start_ref, keep_ref, send_ref):
    senders, groups, parts, vectors, lanes = rows_ref.shape
    total = senders * vectors
    own = start_ref.shape[2]
    per_group = lanes // own
    first = jnp.zeros((total, total), F32)
    second = jnp.zeros((total, total), F32)
    for group in range(groups):
        for part in range(parts):
            flat = rows_ref[:, group, part].reshape(total, lanes)
            start = start_ref[part, group * per_group : (group + 1) * per_group].reshape(lanes, total)
            first += jnp.dot(flat, start.astype(BF16), preferred_element_type=F32)
            second += lax.dot_general(
                flat, flat, (((1,), (1,)), ((), ())), preferred_element_type=F32
            )
    is_first = core_ref[0] == 0
    keep_ref[...] = jnp.where(is_first, first, second)
    send_ref[...] = jnp.where(is_first, second, first)


def grams(core, rows, start):
    total = rows.shape[0] * rows.shape[3]
    return pl.pallas_call(
        gram_kernel,
        out_shape=[jax.ShapeDtypeStruct((total, total), F32)] * 2,
        in_specs=[pl.BlockSpec(memory_space=pltpu.SMEM)] + [pl.BlockSpec(memory_space=pltpu.VMEM)] * 2,
        out_specs=[pl.BlockSpec(memory_space=pltpu.VMEM)] * 2,
        compiler_params=pltpu.CompilerParams(vmem_limit_bytes=VMEM_BYTES),
    )(core, rows, start)


def triple(value):
    high = value.astype(BF16)
    rest = value - high.astype(F32)
    middle = rest.astype(BF16)
    return high, middle, (rest - middle.astype(F32)).astype(BF16)


def inverse_factor(work_ref, matrix):
    order = matrix.shape[0]
    step = 16
    row = lax.broadcasted_iota(jnp.int32, (step, order), 0)
    lane = lax.broadcasted_iota(jnp.int32, (step, order), 1)
    at = lax.broadcasted_iota(jnp.int32, (order, order), 0)
    work_ref[:, :order] = matrix
    work_ref[:, order:] = jnp.where(at == lax.broadcasted_iota(jnp.int32, (order, order), 1), 1.0, 0.0)
    for begin in range(0, order, step):
        block = slice(begin, begin + step)
        left, right = work_ref[block, :order], work_ref[block, order:]
        columns = [
            jnp.broadcast_to(left[:, begin + k : begin + k + 1], (step, order)) for k in range(step)
        ]
        for k in range(step):
            root = lax.rsqrt(columns[k][k : k + 1])
            factor = columns[k] * root

            def eliminate(value):
                pivot = value[k : k + 1] * root
                return jnp.where(row == k, pivot, jnp.where(row > k, value - factor * pivot, value))

            left, right = eliminate(left), eliminate(right)
            columns = columns[: k + 1] + [eliminate(c) for c in columns[k + 1 :]]
        work_ref[block, order:] = right
        end = begin + step
        if end < order:
            kept = jnp.where(lane >= end, left, 0.0)
            high, middle, low = triple(kept)
            first = jnp.concatenate([high, high, middle, high, low, middle], axis=0).astype(F32).T
            high, middle, low = triple(jnp.concatenate([kept, right], axis=1))
            second = jnp.concatenate([high, middle, high, low, high, middle], axis=0)
            change = jnp.dot(first[end:].astype(BF16), second, preferred_element_type=F32)
            work_ref[end:, :] = work_ref[end:, :] - change
    return work_ref[:, order:]


def finish_kernel(scale, core_ref, rows_ref, kept_ref, given_ref, out_ref, work_ref):
    senders, groups, parts, vectors, lanes = rows_ref.shape
    total = senders * vectors
    exact = functools.partial(lax.dot_general, precision=HIGH, preferred_element_type=F32)
    across = (((1,), (1,)), ((), ()))
    plain = (((1,), (0,)), ((), ()))
    is_first = core_ref[0] == 0
    gram_first = jnp.where(is_first, kept_ref[...], given_ref[...])
    first = inverse_factor(work_ref, 0.5 * (gram_first + gram_first.T))
    gram_second = jnp.where(is_first, given_ref[...], kept_ref[...])
    gram_second = exact(exact(first, gram_second, plain), first, across)
    second = inverse_factor(work_ref, gram_second)
    mixing = exact(second, first, plain) * scale
    high, middle, low = triple(mixing)
    for group in range(groups):
        for part in range(parts):
            flat = rows_ref[:, group, part].reshape(total, lanes)
            turned = flat.astype(F32).T.astype(BF16)
            dot = functools.partial(
                lax.dot_general, turned, dimension_numbers=across, preferred_element_type=F32
            )
            out_ref[part, group] = (dot(low) + dot(middle)) + dot(high)


def finish(core, rows, kept, given, scale):
    senders, groups, parts, vectors, lanes = rows.shape
    total = senders * vectors
    return pl.pallas_call(
        functools.partial(finish_kernel, scale),
        out_shape=jax.ShapeDtypeStruct((parts, groups, lanes, total), F32),
        in_specs=[pl.BlockSpec(memory_space=pltpu.SMEM)] + [pl.BlockSpec(memory_space=pltpu.VMEM)] * 3,
        out_specs=pl.BlockSpec(memory_space=pltpu.VMEM),
        scratch_shapes=[pltpu.VMEM((total, 2 * total), F32)],
        compiler_params=pltpu.CompilerParams(vmem_limit_bytes=VMEM_BYTES),
    )(core, rows, kept, given)


def whiten_kernel(core_ref, beam_ref, noise_ref, keep_ref, send_ref):
    parts, freqs, own, multipoles = beam_ref.shape
    half = multipoles // 2
    level = lax.rsqrt(noise_ref[...])
    is_first = core_ref[0] == 0
    for freq in range(freqs):
        column = jnp.broadcast_to(level[:, freq : freq + 1], (own, half))
        for part in range(parts):
            low = (beam_ref[part, freq, :, :half].astype(F32) * column).astype(BF16)
            high = (beam_ref[part, freq, :, half:].astype(F32) * column).astype(BF16)
            rows = slice(part * own, (part + 1) * own)
            keep_ref[freq, rows] = jnp.where(is_first, low, high)
            send_ref[freq, rows] = jnp.where(is_first, high, low)


def whiten(core, beam, noise):
    parts, freqs, own, multipoles = beam.shape
    return pl.pallas_call(
        whiten_kernel,
        out_shape=[jax.ShapeDtypeStruct((freqs, parts * own, multipoles // 2), BF16)] * 2,
        in_specs=[pl.BlockSpec(memory_space=pltpu.SMEM)] + [pl.BlockSpec(memory_space=pltpu.VMEM)] * 2,
        out_specs=[pl.BlockSpec(memory_space=pltpu.VMEM)] * 2,
        compiler_params=pltpu.CompilerParams(vmem_limit_bytes=VMEM_BYTES),
    )(core, beam, noise.T)


def turn_kernel(start_ref, out_ref):
    parts, freqs, own, vectors = start_ref.shape
    receivers, groups, mine, lanes = out_ref.shape
    per_group = lanes // (parts * own)

    def group(index, carry):
        tiles = [
            start_ref[part, index * per_group + place]
            for place in range(per_group)
            for part in range(parts)
        ]
        turned = jnp.concatenate(tiles, axis=0).T
        out_ref[:, index] = turned.reshape(receivers, mine, lanes).astype(BF16)
        return carry

    lax.fori_loop(0, groups, group, 0)


def turn(start, receivers, lanes):
    parts, freqs, own, vectors = start.shape
    groups = parts * freqs * own // lanes
    return pl.pallas_call(
        turn_kernel,
        out_shape=jax.ShapeDtypeStruct((receivers, groups, vectors // receivers, lanes), BF16),
        in_specs=[pl.BlockSpec(memory_space=pltpu.VMEM)],
        out_specs=pl.BlockSpec(memory_space=pltpu.VMEM),
        compiler_params=pltpu.CompilerParams(vmem_limit_bytes=VMEM_BYTES),
    )(start)


def operand_kernel(own, *refs):
    x_count, z_count, groups, mine, lanes = refs[0].shape
    parts = lanes // (z_count * own)
    width = parts * own
    lane = lax.broadcasted_iota(jnp.int32, (mine, lanes), 1)
    is_real = (lane // own) % 2 == 0

    def group(side, index, carry):
        x_index, at = index // groups, index % groups
        tiles = [refs[side][x_index, z, at].astype(F32) for z in range(z_count)]
        for place in range(z_count):
            top = tiles[0]
            for z in range(z_count):
                top = jnp.where(lane // width == z, rolled(tiles[z], (z - place) * width), top)
            bottom = jnp.where(is_real, rolled(top, -own), -rolled(top, own))
            image = jnp.concatenate([top, bottom], axis=0).astype(BF16)
            refs[2 + side][index * z_count + place] = image
        return carry

    for side in range(2):
        lax.fori_loop(0, x_count * groups, functools.partial(group, side), 0, unroll=2)


def start_operand(sides, own):
    x_count, z_count, groups, mine, lanes = sides[0].shape
    freqs = x_count * groups * z_count
    return pl.pallas_call(
        functools.partial(operand_kernel, own),
        out_shape=[jax.ShapeDtypeStruct((freqs, 2 * mine, lanes), BF16)] * 2,
        in_specs=[pl.BlockSpec(memory_space=pltpu.VMEM)] * 2,
        out_specs=[pl.BlockSpec(memory_space=pltpu.VMEM)] * 2,
        compiler_params=pltpu.CompilerParams(vmem_limit_bytes=VMEM_BYTES),
    )(*sides)


def swap_cores(value):
    return lax.ppermute(value, "core", [(0, 1), (1, 0)])


def after(value, event):
    return lax.optimization_barrier((value, event))


def gather_ring(blocks, late, x_count, z_count):
    count = x_count * z_count
    ring = [k if k < z_count else z_count + count - 1 - k for k in range(count)]
    pairs = {
        1: [(ring[k], ring[(k + 1) % count]) for k in range(count)],
        -1: [(ring[(k + 1) % count], ring[k]) for k in range(count)],
    }
    x_place, z_place = lax.axis_index("x"), lax.axis_index("fc")
    place = jnp.where(x_place == 0, z_place, count - 1 - z_place).astype(jnp.int32).reshape(1)
    moving = {(core, way): block for core, block in enumerate(blocks) for way in (1, -1)}
    found = [(block, core, 0) for core, block in enumerate(blocks)]
    for hop in range(1, count // 2 + 1):
        for core, way in moving:
            if 2 * hop == count and (way == 1) != (core == 0):
                continue
            moving[core, way] = lax.ppermute(moving[core, way], ("x", "fc"), pairs[way])
            if hop == 1 and core == 0 and way == 1:
                late, moving[core, way] = after(late, moving[core, way])
            found.append((moving[core, way], core, -way * hop))
    return place, found, late


def sum_devices(keep, send, z_count):
    value = keep + swap_cores(send)
    value = value + lax.ppermute(value, "x", [(0, 1), (1, 0)])
    if z_count & (z_count - 1):
        value = lax.psum(value, "fc")
    else:
        terms = [value] + [
            lax.ppermute(value, "fc", [(j, j ^ s) for j in range(z_count)]) for s in range(1, z_count)
        ]
        while len(terms) > 1:
            terms = [terms[i] + terms[i + 1] for i in range(0, len(terms), 2)]
        value = terms[0]
    return value, swap_cores(value)


def body_split(x_count, z_count, beam_transfer, noise_var, spectra, freq_covariance, start_vectors):
    parts, freqs, own, multipoles = beam_transfer.shape
    vectors = start_vectors.shape[3]
    cores = 2
    core = lax.axis_index("core")
    all_freqs = x_count * cores * freqs
    mine_vectors = vectors // (x_count * z_count)
    depth = multipoles // cores

    core_index = core.astype(jnp.int32).reshape(1)
    kept, given = whiten(core_index, beam_transfer, noise_var)
    given = swap_cores(given)
    start = turn(start_vectors, x_count * z_count, z_count * parts * own)
    place, beams, start = gather_ring([kept, given], start, x_count, z_count)

    spec = spectra.reshape(-1, cores, depth)
    spec = lax.dynamic_index_in_dim(spec, core, 1, False)
    cov = freq_covariance.reshape(-1, x_count, cores, freqs, x_count, cores, freqs).astype(BF16)
    cov = jnp.where(core == 0, cov, jnp.flip(cov, (2, 5)))
    cov = cov.transpose(2, 1, 3, 0, 5, 4, 6).reshape(all_freqs, -1)

    start = lax.all_to_all(start, ("x", "fc"), 0, 0, tiled=True)
    start = start.reshape(x_count, z_count, *start.shape[1:])
    operand = start_operand([start, swap_cores(start)], own)

    mine, theirs = apply_covariance(
        place, [[operand[0]], [operand[1]]], beams, cov, spec, own, z_count
    )
    got_mine, got_theirs = swap_cores(theirs), swap_cores(mine)
    second_mine, second_theirs = apply_covariance(
        place, [[mine, got_mine], [theirs, got_theirs]], beams, cov, spec, own, z_count
    )
    packed = pack(second_mine, swap_cores(second_theirs), x_count, z_count, own)
    packed = packed.reshape(x_count * z_count, *packed.shape[2:])
    received = lax.all_to_all(packed, ("x", "fc"), 0, 0, tiled=True)
    groups, lanes = received.shape[1], received.shape[3]
    received = received.reshape(-1, groups, parts, mine_vectors, lanes)

    kept_gram, given_gram = sum_devices(*grams(core_index, received, start_vectors), z_count)
    scale = math.sqrt(2.0 * all_freqs * z_count * own)
    basis = finish(core_index, received, kept_gram, given_gram, scale)
    return basis.reshape(parts, freqs, own, vectors)


def row_operands(row_part, spectra):
    scaled = (row_part.astype(F32)[None] * spectra[:, None, None, :]).astype(BF16)
    real_rows = jnp.concatenate([scaled[:, 0], scaled[:, 1]], axis=-1)
    imag_rows = jnp.concatenate([scaled[:, 1], -scaled[:, 0]], axis=-1)
    return jnp.stack([real_rows, imag_rows], axis=1)


def apply_tile(pair_tile, vec_bf):
    row_count = pair_tile.shape[1]
    stacked = pair_tile.reshape(2 * row_count, pair_tile.shape[2])
    with_real = jnp.dot(stacked, vec_bf[0], preferred_element_type=F32)
    with_imag = jnp.dot(stacked, vec_bf[1], preferred_element_type=F32)
    real_part = with_real[:row_count] - with_imag[row_count:]
    imag_part = with_real[row_count:] + with_imag[:row_count]
    return jnp.stack([real_part, imag_part], axis=0)


def partial_gram(image):
    flat = image.reshape(-1, image.shape[-1])
    return jnp.dot(flat.T, flat, precision=HIGH, preferred_element_type=F32)


def orthonormalize(image, gram_matrix):
    lower = jnp.linalg.cholesky(gram_matrix)
    flat = image.reshape(-1, image.shape[-1])
    solved = lax.linalg.triangular_solve(lower, flat, left_side=False, lower=True, transpose_a=True)
    return solved.reshape(image.shape)


def body_general(beam_transfer, noise_var, spectra, freq_covariance, start_vectors):
    row_axes = ("x", "core")
    whitened = (beam_transfer.astype(F32) * lax.rsqrt(noise_var)[None, :, :, None]).astype(BF16)
    row_beams = lax.all_gather(whitened, "fc", axis=2, tiled=True)
    _, freq_rows, mode_count, multipoles = row_beams.shape
    row_total = freq_rows * mode_count
    components = spectra.shape[0]
    vectors_count = start_vectors.shape[3]
    row_operand = row_operands(row_beams.reshape(2, row_total, multipoles), spectra)
    row_start = lax.axis_index(row_axes) * freq_rows
    row_cov = lax.dynamic_slice_in_dim(freq_covariance, row_start, freq_rows, 1)
    piece = lax.all_gather(whitened, row_axes, axis=1, tiled=True)
    _, piece_freqs, piece_modes, _ = piece.shape
    columns = piece.reshape(2, piece_freqs * piece_modes, multipoles)
    col_operand = jnp.concatenate([columns[0], columns[1]], axis=-1)
    products = lax.dot_general(
        row_operand, col_operand, (((3,), (1,)), ((), ())), preferred_element_type=F32
    )
    weight = jnp.broadcast_to(
        row_cov[:, :, None, :, None], (components, freq_rows, mode_count, piece_freqs, piece_modes)
    )
    weight = weight.reshape(components, row_total, piece_freqs * piece_modes)
    pair_tile = jnp.einsum("kxy,kcxy->cxy", weight, products).astype(BF16)
    vectors = start_vectors
    own_modes = start_vectors.shape[2]
    for _ in range(ITERS):
        gathered = lax.all_gather(vectors.astype(BF16), row_axes, axis=1, tiled=True)
        vec_bf = gathered.reshape(2, -1, vectors_count)
        partial_value = apply_tile(pair_tile, vec_bf).reshape(2, freq_rows, mode_count, vectors_count)
        summed = lax.psum(partial_value, "fc")
        gram_matrix = lax.psum(partial_gram(summed), row_axes)
        own_rows = lax.dynamic_slice_in_dim(summed, lax.axis_index("fc") * own_modes, own_modes, 2)
        vectors = orthonormalize(own_rows, gram_matrix)
    return vectors * math.sqrt(2.0 * piece_freqs * mode_count)


def body(x_count, z_count, *args):
    beam_transfer, start_vectors = args[0], args[4]
    parts, freqs, own, multipoles = beam_transfer.shape
    vectors = start_vectors.shape[3]
    lanes = parts * own * z_count
    fits = (
        x_count == 2
        and vectors % (16 * x_count * z_count) == 0
        and lanes == 128
        and own % 16 == 0
        and multipoles % 256 == 0
        and (freqs * own) % lanes == 0
    )
    if fits:
        return body_split(x_count, z_count, *args)
    return body_general(*args)


def solution(mesh):
    sizes = dict(mesh.shape)
    x_count = sizes["fr"] // 2
    shape = (sizes["ma"], x_count, 2, sizes["fc"])
    devices = mesh.devices.reshape(shape)
    split = Mesh(devices, ("ma", "x", "core", "fc"))
    rows = ("ma", "x", "core")
    in_specs = (
        P(None, rows, "fc", None),
        P(rows, "fc"),
        P(),
        P(),
        P(None, rows, "fc", None),
    )
    return jax.shard_map(
        functools.partial(body, x_count, sizes["fc"]),
        mesh=split,
        in_specs=in_specs,
        out_specs=P(None, rows, "fc", None),
        check_vma=False,
    )
```

```python
import functools
import math

import jax
import jax.numpy as jnp
from jax import lax
from jax.experimental import pallas as pl
from jax.experimental.pallas import tpu as pltpu
from jax.sharding import Mesh
from jax.sharding import PartitionSpec as P

ITERS = 2
BF16 = jnp.bfloat16
F32 = jnp.float32
MIB = 1024 * 1024
APPLY_BYTES = 30 * MIB
SMALL_BYTES = 8 * MIB
HIGH = lax.Precision.HIGHEST


def rolled(value, shift):
    return pltpu.roll(value, shift % value.shape[-1], 1)


def apply_kernel(n_vec, z_count, own, offsets, keep, send, *refs):
    place_ref, *refs = refs
    vec_refs = (refs[:n_vec], refs[n_vec : 2 * n_vec])
    piece_refs = refs[2 * n_vec : 2 * n_vec + len(offsets)]
    cov_ref, spec_ref, *refs = refs[2 * n_vec + len(offsets) :]
    *refs, beam_ref, vec_ref, z_ref, y_ref, sems = refs
    n_out = len(keep) + len(send)
    added, out_refs = refs[: len(refs) - n_out], refs[len(refs) - n_out :]
    count, rows, lanes = out_refs[0].shape
    freqs = 2 * count
    half = rows // 2
    components = spec_ref.shape[0]
    size, width, part_depth = piece_refs[0].shape
    chips = count // size * z_count
    tiles, _, step = z_ref.shape
    lane = lax.broadcasted_iota(jnp.int32, (half, lanes), 1)
    is_real = (lane // own) % 2 == 0
    sign = jnp.where(is_real, -1.0, 1.0).astype(F32)

    copies = []
    for index, (core, offset, part) in enumerate(offsets):
        at = lax.rem(place_ref[0] + (offset % chips), chips)
        x_at = at // z_count
        z_at = jnp.where(x_at == 0, at, chips - 1 - at)
        target = beam_ref.at[
            pl.ds(core * count + x_at * size, size),
            pl.ds(pl.multiple_of(z_at * width, width), width),
            pl.ds(part * part_depth, part_depth),
        ]
        copies.append(pltpu.make_async_copy(piece_refs[index], target, sems.at[index]))
    for copy in copies:
        copy.start()

    def gather(side, place, carry):
        vec = vec_refs[side][0][place]
        for other in vec_refs[side][1:]:
            vec = vec + other[place]
        vec_ref[side * count + place] = vec.astype(BF16)
        return carry

    for side in range(2):
        lax.fori_loop(0, count, functools.partial(gather, side), 0, unroll=8)
    for copy in copies:
        copy.wait()

    def project(freq, carry):
        z = jnp.dot(vec_ref[freq], beam_ref[freq], preferred_element_type=F32)
        for tile in range(tiles):
            z_ref[tile, pl.ds(freq, rows, stride=freqs), :] = z[:, tile * step : (tile + 1) * step]
        return carry

    lax.fori_loop(0, freqs, project, 0, unroll=64)

    def mix(row, carry):
        start = pl.multiple_of(row * freqs, freqs)
        z = jnp.concatenate([z_ref[tile, pl.ds(start, freqs), :] for tile in range(tiles)], axis=1)
        scaled = [(z * spec_ref[k][None, :]).astype(BF16) for k in range(components)]
        y = jnp.dot(cov_ref[...], jnp.concatenate(scaled, axis=0), preferred_element_type=F32)
        for tile in range(tiles):
            y_ref[tile, pl.ds(start, freqs), :] = y[:, tile * step : (tile + 1) * step]
        return carry

    lax.fori_loop(0, rows, mix, 0, unroll=32)

    def expand(side, place, carry):
        freq = side * count + place
        y = [
            y_ref[tile, pl.ds(freq, rows, stride=freqs), :].astype(BF16) for tile in range(tiles)
        ]
        product = lax.dot_general(
            jnp.concatenate(y, axis=1),
            beam_ref[freq],
            (((1,), (1,)), ((), ())),
            preferred_element_type=F32,
        )
        swapped = jnp.where(
            jnp.concatenate([is_real, is_real], axis=0),
            rolled(product, -own),
            rolled(product, own),
        )
        top = product[:half] + sign * swapped[half:]
        bottom = product[half:] - sign * swapped[:half]
        image = jnp.concatenate([top, bottom], axis=0)
        if added:
            image = image + added[side][place]
        if side in keep:
            out_refs[keep.index(side)][place] = image
        if side in send:
            out_refs[len(keep) + send.index(side)][place] = image.astype(BF16)
        return carry

    for side in range(2):
        lax.fori_loop(0, count, functools.partial(expand, side), 0, unroll=64)


def apply_covariance(place, vecs, beams, cov, spec, own, z_count, keep, send, added=()):
    count, rows, lanes = vecs[0][0].shape
    freqs = 2 * count
    depth = spec.shape[1]
    step = min(depth, 128)
    flops = 2 * freqs * rows * (2 * lanes * depth + 2 * freqs * depth)
    vmem = pl.BlockSpec(memory_space=pltpu.VMEM)
    n_vec = len(vecs[0])
    offsets = tuple(beam[1:] for beam in beams)
    tiles = pltpu.VMEM((depth // step, rows * freqs, step), F32)
    return pl.pallas_call(
        functools.partial(apply_kernel, n_vec, z_count, own, offsets, keep, send),
        out_shape=[jax.ShapeDtypeStruct((count, rows, lanes), F32)] * len(keep)
        + [jax.ShapeDtypeStruct((count, rows, lanes), BF16)] * len(send),
        in_specs=[pl.BlockSpec(memory_space=pltpu.SMEM)]
        + [vmem] * (2 * n_vec)
        + [pl.BlockSpec(memory_space=pl.ANY)] * len(beams)
        + [vmem] * (2 + len(added)),
        out_specs=[vmem] * (len(keep) + len(send)),
        scratch_shapes=[
            pltpu.VMEM((freqs, lanes, depth), BF16),
            pltpu.VMEM((freqs, rows, lanes), BF16),
            tiles,
            tiles,
            pltpu.SemaphoreType.DMA((len(beams),)),
        ],
        compiler_params=pltpu.CompilerParams(vmem_limit_bytes=APPLY_BYTES),
        cost_estimate=pl.CostEstimate(
            flops=flops, bytes_accessed=freqs * lanes * depth * 2, transcendentals=0
        ),
    )(place, *vecs[0], *vecs[1], *[beam[0] for beam in beams], cov, spec, *added)


def pack_kernel(own, first_ref, second_ref, out_ref):
    x_count, z_count, groups = out_ref.shape[:3]
    freqs, rows, lanes = first_ref.shape
    per_group = lanes // own
    lane = lax.broadcasted_iota(jnp.int32, (rows, lanes), 1) // own

    def group(index, carry):
        x_index, group_index = index // groups, index % groups
        totals = [jnp.zeros((rows, lanes), F32)] * z_count
        for place in range(per_group):
            freq = index * per_group + place
            image = first_ref[freq] + second_ref[freq]
            for z_index in range(z_count):
                moved = rolled(image, (place - 2 * z_index) * own)
                totals[z_index] = jnp.where(lane == place, moved, totals[z_index])
        for z_index in range(z_count):
            out_ref[x_index, z_index, group_index] = totals[z_index].astype(BF16)
        return carry

    lax.fori_loop(0, x_count * groups, group, 0, unroll=2)


def pack(first, second, x_count, z_count, own):
    freqs, rows, lanes = first.shape
    groups = freqs * own // (x_count * lanes)
    return pl.pallas_call(
        functools.partial(pack_kernel, own),
        out_shape=jax.ShapeDtypeStruct((x_count, z_count, groups, rows, lanes), BF16),
        in_specs=[pl.BlockSpec(memory_space=pltpu.VMEM)] * 2,
        out_specs=pl.BlockSpec(memory_space=pltpu.VMEM),
        compiler_params=pltpu.CompilerParams(vmem_limit_bytes=SMALL_BYTES),
    )(first, second)


def gram_kernel(core_ref, rows_ref, start_ref, keep_ref, send_ref):
    senders, groups, parts, vectors, lanes = rows_ref.shape
    total = senders * vectors
    own = start_ref.shape[2]
    per_group = lanes // own
    first = jnp.zeros((total, total), F32)
    second = jnp.zeros((total, total), F32)
    for group in range(groups):
        for part in range(parts):
            flat = rows_ref[:, group, part].reshape(total, lanes)
            start = start_ref[part, group * per_group : (group + 1) * per_group].reshape(lanes, total)
            first += jnp.dot(flat, start.astype(BF16), preferred_element_type=F32)
            second += lax.dot_general(
                flat, flat, (((1,), (1,)), ((), ())), preferred_element_type=F32
            )
    is_first = core_ref[0] == 0
    keep_ref[...] = jnp.where(is_first, first, second)
    send_ref[...] = jnp.where(is_first, second, first)


def grams(core, rows, start):
    total = rows.shape[0] * rows.shape[3]
    return pl.pallas_call(
        gram_kernel,
        out_shape=[jax.ShapeDtypeStruct((total, total), F32)] * 2,
        in_specs=[pl.BlockSpec(memory_space=pltpu.SMEM)] + [pl.BlockSpec(memory_space=pltpu.VMEM)] * 2,
        out_specs=[pl.BlockSpec(memory_space=pltpu.VMEM)] * 2,
        compiler_params=pltpu.CompilerParams(vmem_limit_bytes=SMALL_BYTES),
    )(core, rows, start)


def triple(value):
    high = value.astype(BF16)
    rest = value - high.astype(F32)
    middle = rest.astype(BF16)
    return high, middle, (rest - middle.astype(F32)).astype(BF16)


def inverse_factor(work_ref, matrix):
    order = matrix.shape[0]
    step = 16
    row = lax.broadcasted_iota(jnp.int32, (step, order), 0)
    lane = lax.broadcasted_iota(jnp.int32, (step, order), 1)
    at = lax.broadcasted_iota(jnp.int32, (order, order), 0)
    work_ref[:, :order] = matrix
    work_ref[:, order:] = jnp.where(at == lax.broadcasted_iota(jnp.int32, (order, order), 1), 1.0, 0.0)
    for begin in range(0, order, step):
        block = slice(begin, begin + step)
        left, right = work_ref[block, :order], work_ref[block, order:]
        columns = [
            jnp.broadcast_to(left[:, begin + k : begin + k + 1], (step, order)) for k in range(step)
        ]
        for k in range(step):
            root = lax.rsqrt(columns[k][k : k + 1])
            factor = columns[k] * root

            def eliminate(value):
                pivot = value[k : k + 1] * root
                return jnp.where(row == k, pivot, jnp.where(row > k, value - factor * pivot, value))

            left, right = eliminate(left), eliminate(right)
            columns = columns[: k + 1] + [eliminate(c) for c in columns[k + 1 :]]
        work_ref[block, order:] = right
        end = begin + step
        if end < order:
            kept = jnp.where(lane >= end, left, 0.0)
            high, middle, low = triple(kept)
            first = jnp.concatenate([high, high, middle, high, low, middle], axis=0).astype(F32).T
            high, middle, low = triple(jnp.concatenate([kept, right], axis=1))
            second = jnp.concatenate([high, middle, high, low, high, middle], axis=0)
            change = jnp.dot(first[end:].astype(BF16), second, preferred_element_type=F32)
            work_ref[end:, :] = work_ref[end:, :] - change
    return work_ref[:, order:]


def finish_kernel(scale, core_ref, rows_ref, kept_ref, given_ref, out_ref, work_ref):
    senders, groups, parts, vectors, lanes = rows_ref.shape
    total = senders * vectors
    exact = functools.partial(lax.dot_general, precision=HIGH, preferred_element_type=F32)
    across = (((1,), (1,)), ((), ()))
    plain = (((1,), (0,)), ((), ()))
    is_first = core_ref[0] == 0
    gram_first = jnp.where(is_first, kept_ref[...], given_ref[...])
    first = inverse_factor(work_ref, 0.5 * (gram_first + gram_first.T))
    gram_second = jnp.where(is_first, given_ref[...], kept_ref[...])
    gram_second = exact(exact(first, gram_second, plain), first, across)
    second = inverse_factor(work_ref, gram_second)
    mixing = exact(second, first, plain) * scale
    high, middle, low = triple(mixing)
    for group in range(groups):
        for part in range(parts):
            flat = rows_ref[:, group, part].reshape(total, lanes)
            turned = flat.astype(F32).T.astype(BF16)
            dot = functools.partial(
                lax.dot_general, turned, dimension_numbers=across, preferred_element_type=F32
            )
            out_ref[part, group] = (dot(low) + dot(middle)) + dot(high)


def finish(core, rows, kept, given, scale):
    senders, groups, parts, vectors, lanes = rows.shape
    total = senders * vectors
    return pl.pallas_call(
        functools.partial(finish_kernel, scale),
        out_shape=jax.ShapeDtypeStruct((parts, groups, lanes, total), F32),
        in_specs=[pl.BlockSpec(memory_space=pltpu.SMEM)] + [pl.BlockSpec(memory_space=pltpu.VMEM)] * 3,
        out_specs=pl.BlockSpec(memory_space=pltpu.VMEM),
        scratch_shapes=[pltpu.VMEM((total, 2 * total), F32)],
        compiler_params=pltpu.CompilerParams(vmem_limit_bytes=SMALL_BYTES),
    )(core, rows, kept, given)


def whiten_kernel(core_ref, beam_ref, noise_ref, keep_ref, send_ref):
    parts, freqs, own, multipoles = beam_ref.shape
    half = multipoles // 2
    level = lax.rsqrt(noise_ref[...])
    is_first = core_ref[0] == 0
    for freq in range(freqs):
        column = jnp.broadcast_to(level[:, freq : freq + 1], (own, half))
        for part in range(parts):
            low = (beam_ref[part, freq, :, :half].astype(F32) * column).astype(BF16)
            high = (beam_ref[part, freq, :, half:].astype(F32) * column).astype(BF16)
            rows = slice(part * own, (part + 1) * own)
            keep_ref[freq, rows] = jnp.where(is_first, low, high)
            send_ref[freq, rows] = jnp.where(is_first, high, low)


def whiten(core, beam, noise):
    parts, freqs, own, multipoles = beam.shape
    return pl.pallas_call(
        whiten_kernel,
        out_shape=[jax.ShapeDtypeStruct((freqs, parts * own, multipoles // 2), BF16)] * 2,
        in_specs=[pl.BlockSpec(memory_space=pltpu.SMEM)] + [pl.BlockSpec(memory_space=pltpu.VMEM)] * 2,
        out_specs=[pl.BlockSpec(memory_space=pltpu.VMEM)] * 2,
        compiler_params=pltpu.CompilerParams(vmem_limit_bytes=SMALL_BYTES),
    )(core, beam, noise.T)


def turn_kernel(start_ref, out_ref):
    parts, freqs, own, vectors = start_ref.shape
    receivers, groups, mine, lanes = out_ref.shape
    per_group = lanes // (parts * own)

    def group(index, carry):
        tiles = [
            start_ref[part, index * per_group + place]
            for place in range(per_group)
            for part in range(parts)
        ]
        turned = jnp.concatenate(tiles, axis=0).T
        out_ref[:, index] = turned.reshape(receivers, mine, lanes).astype(BF16)
        return carry

    lax.fori_loop(0, groups, group, 0)


def turn(start, receivers, lanes):
    parts, freqs, own, vectors = start.shape
    groups = parts * freqs * own // lanes
    return pl.pallas_call(
        turn_kernel,
        out_shape=jax.ShapeDtypeStruct((receivers, groups, vectors // receivers, lanes), BF16),
        in_specs=[pl.BlockSpec(memory_space=pltpu.VMEM)],
        out_specs=pl.BlockSpec(memory_space=pltpu.VMEM),
        compiler_params=pltpu.CompilerParams(vmem_limit_bytes=SMALL_BYTES),
    )(start)


def operand_kernel(own, *refs):
    x_count, z_count, groups, mine, lanes = refs[0].shape
    parts = lanes // (z_count * own)
    width = parts * own
    lane = lax.broadcasted_iota(jnp.int32, (mine, lanes), 1)
    is_real = (lane // own) % 2 == 0

    def group(side, index, carry):
        x_index, at = index // groups, index % groups
        tiles = [refs[side][x_index, z, at].astype(F32) for z in range(z_count)]
        for place in range(z_count):
            top = tiles[0]
            for z in range(z_count):
                top = jnp.where(lane // width == z, rolled(tiles[z], (z - place) * width), top)
            bottom = jnp.where(is_real, rolled(top, -own), -rolled(top, own))
            image = jnp.concatenate([top, bottom], axis=0).astype(BF16)
            refs[2 + side][index * z_count + place] = image
        return carry

    for side in range(2):
        lax.fori_loop(0, x_count * groups, functools.partial(group, side), 0, unroll=2)


def start_operand(sides, own):
    x_count, z_count, groups, mine, lanes = sides[0].shape
    freqs = x_count * groups * z_count
    return pl.pallas_call(
        functools.partial(operand_kernel, own),
        out_shape=[jax.ShapeDtypeStruct((freqs, 2 * mine, lanes), BF16)] * 2,
        in_specs=[pl.BlockSpec(memory_space=pltpu.VMEM)] * 2,
        out_specs=[pl.BlockSpec(memory_space=pltpu.VMEM)] * 2,
        compiler_params=pltpu.CompilerParams(vmem_limit_bytes=SMALL_BYTES),
    )(*sides)


def swap_cores(value):
    return lax.ppermute(value, "core", [(0, 1), (1, 0)])


def after(value, event):
    return lax.optimization_barrier((value, event))


def gather_ring(blocks, late, x_count, z_count):
    count = x_count * z_count
    ring = [k if k < z_count else z_count + count - 1 - k for k in range(count)]
    pairs = {
        1: [(ring[k], ring[(k + 1) % count]) for k in range(count)],
        -1: [(ring[(k + 1) % count], ring[k]) for k in range(count)],
    }
    x_place, z_place = lax.axis_index("x"), lax.axis_index("fc")
    place = jnp.where(x_place == 0, z_place, count - 1 - z_place).astype(jnp.int32).reshape(1)
    moving = {(core, way): block for core, block in enumerate(blocks) for way in (1, -1)}
    found = [(block, core, 0, 0) for core, block in enumerate(blocks)]
    for hop in range(1, count // 2 + 1):
        for core, way in moving:
            if 2 * hop == count and (way == 1) != (core == 0):
                continue
            moving[core, way] = lax.ppermute(moving[core, way], ("x", "fc"), pairs[way])
            if hop == 1 and core == 0 and way == 1:
                late, moving[core, way] = after(late, moving[core, way])
            found.append((moving[core, way], core, -way * hop, 0))
    return place, found, late


def sum_devices(keep, send, z_count):
    value = keep + swap_cores(send)
    value = value + lax.ppermute(value, "x", [(0, 1), (1, 0)])
    if z_count & (z_count - 1):
        value = lax.psum(value, "fc")
    else:
        terms = [value] + [
            lax.ppermute(value, "fc", [(j, j ^ s) for j in range(z_count)]) for s in range(1, z_count)
        ]
        while len(terms) > 1:
            terms = [terms[i] + terms[i + 1] for i in range(0, len(terms), 2)]
        value = terms[0]
    return value, swap_cores(value)


def body_split(x_count, z_count, beam_transfer, noise_var, spectra, freq_covariance, start_vectors):
    parts, freqs, own, multipoles = beam_transfer.shape
    vectors = start_vectors.shape[3]
    cores = 2
    core = lax.axis_index("core")
    all_freqs = x_count * cores * freqs
    mine_vectors = vectors // (x_count * z_count)
    depth = multipoles // cores

    core_index = core.astype(jnp.int32).reshape(1)
    kept, given = whiten(core_index, beam_transfer, noise_var)
    given = swap_cores(given)
    start = turn(start_vectors, x_count * z_count, z_count * parts * own)
    place, beams, start = gather_ring([kept, given], start, x_count, z_count)

    spec = spectra.reshape(-1, cores, depth)
    spec = lax.dynamic_index_in_dim(spec, core, 1, False)
    cov = freq_covariance.reshape(-1, x_count, cores, freqs, x_count, cores, freqs).astype(BF16)
    cov = jnp.where(core == 0, cov, jnp.flip(cov, (2, 5)))
    cov = cov.transpose(2, 1, 3, 0, 5, 4, 6).reshape(all_freqs, -1)

    start = lax.all_to_all(start, ("x", "fc"), 0, 0, tiled=True)
    start = start.reshape(x_count, z_count, *start.shape[1:])
    operand = start_operand([start, swap_cores(start)], own)

    apply = functools.partial(apply_covariance, place)
    mine, theirs, mine_sent, theirs_sent = apply(
        [[operand[0]], [operand[1]]], beams, cov, spec, own, z_count, (0, 1), (0, 1)
    )
    got_mine, got_theirs = swap_cores(theirs_sent), swap_cores(mine_sent)
    second_mine, second_sent = apply(
        [[mine, got_mine], [theirs, got_theirs]], beams, cov, spec, own, z_count, (0,), (1,)
    )
    packed = pack(second_mine, swap_cores(second_sent), x_count, z_count, own)
    packed = packed.reshape(x_count * z_count, *packed.shape[2:])
    received = lax.all_to_all(packed, ("x", "fc"), 0, 0, tiled=True)
    groups, lanes = received.shape[1], received.shape[3]
    received = received.reshape(-1, groups, parts, mine_vectors, lanes)

    kept_gram, given_gram = sum_devices(*grams(core_index, received, start_vectors), z_count)
    scale = math.sqrt(2.0 * all_freqs * z_count * own)
    basis = finish(core_index, received, kept_gram, given_gram, scale)
    return basis.reshape(parts, freqs, own, vectors)


def row_operands(row_part, spectra):
    scaled = (row_part.astype(F32)[None] * spectra[:, None, None, :]).astype(BF16)
    real_rows = jnp.concatenate([scaled[:, 0], scaled[:, 1]], axis=-1)
    imag_rows = jnp.concatenate([scaled[:, 1], -scaled[:, 0]], axis=-1)
    return jnp.stack([real_rows, imag_rows], axis=1)


def apply_tile(pair_tile, vec_bf):
    row_count = pair_tile.shape[1]
    stacked = pair_tile.reshape(2 * row_count, pair_tile.shape[2])
    with_real = jnp.dot(stacked, vec_bf[0], preferred_element_type=F32)
    with_imag = jnp.dot(stacked, vec_bf[1], preferred_element_type=F32)
    real_part = with_real[:row_count] - with_imag[row_count:]
    imag_part = with_real[row_count:] + with_imag[:row_count]
    return jnp.stack([real_part, imag_part], axis=0)


def partial_gram(image):
    flat = image.reshape(-1, image.shape[-1])
    return jnp.dot(flat.T, flat, precision=HIGH, preferred_element_type=F32)


def orthonormalize(image, gram_matrix):
    lower = jnp.linalg.cholesky(gram_matrix)
    flat = image.reshape(-1, image.shape[-1])
    solved = lax.linalg.triangular_solve(lower, flat, left_side=False, lower=True, transpose_a=True)
    return solved.reshape(image.shape)


def body_general(beam_transfer, noise_var, spectra, freq_covariance, start_vectors):
    row_axes = ("x", "core")
    whitened = (beam_transfer.astype(F32) * lax.rsqrt(noise_var)[None, :, :, None]).astype(BF16)
    row_beams = lax.all_gather(whitened, "fc", axis=2, tiled=True)
    _, freq_rows, mode_count, multipoles = row_beams.shape
    row_total = freq_rows * mode_count
    components = spectra.shape[0]
    vectors_count = start_vectors.shape[3]
    row_operand = row_operands(row_beams.reshape(2, row_total, multipoles), spectra)
    row_start = lax.axis_index(row_axes) * freq_rows
    row_cov = lax.dynamic_slice_in_dim(freq_covariance, row_start, freq_rows, 1)
    piece = lax.all_gather(whitened, row_axes, axis=1, tiled=True)
    _, piece_freqs, piece_modes, _ = piece.shape
    columns = piece.reshape(2, piece_freqs * piece_modes, multipoles)
    col_operand = jnp.concatenate([columns[0], columns[1]], axis=-1)
    products = lax.dot_general(
        row_operand, col_operand, (((3,), (1,)), ((), ())), preferred_element_type=F32
    )
    weight = jnp.broadcast_to(
        row_cov[:, :, None, :, None], (components, freq_rows, mode_count, piece_freqs, piece_modes)
    )
    weight = weight.reshape(components, row_total, piece_freqs * piece_modes)
    pair_tile = jnp.einsum("kxy,kcxy->cxy", weight, products).astype(BF16)
    vectors = start_vectors
    own_modes = start_vectors.shape[2]
    for _ in range(ITERS):
        gathered = lax.all_gather(vectors.astype(BF16), row_axes, axis=1, tiled=True)
        vec_bf = gathered.reshape(2, -1, vectors_count)
        partial_value = apply_tile(pair_tile, vec_bf).reshape(2, freq_rows, mode_count, vectors_count)
        summed = lax.psum(partial_value, "fc")
        gram_matrix = lax.psum(partial_gram(summed), row_axes)
        own_rows = lax.dynamic_slice_in_dim(summed, lax.axis_index("fc") * own_modes, own_modes, 2)
        vectors = orthonormalize(own_rows, gram_matrix)
    return vectors * math.sqrt(2.0 * piece_freqs * mode_count)


def body(x_count, z_count, *args):
    beam_transfer, start_vectors = args[0], args[4]
    parts, freqs, own, multipoles = beam_transfer.shape
    vectors = start_vectors.shape[3]
    lanes = parts * own * z_count
    fits = (
        x_count == 2
        and vectors % (16 * x_count * z_count) == 0
        and lanes == 128
        and own % 16 == 0
        and multipoles % 256 == 0
        and (freqs * own) % lanes == 0
    )
    if fits:
        return body_split(x_count, z_count, *args)
    return body_general(*args)


def solution(mesh):
    sizes = dict(mesh.shape)
    x_count = sizes["fr"] // 2
    shape = (sizes["ma"], x_count, 2, sizes["fc"])
    devices = mesh.devices.reshape(shape)
    split = Mesh(devices, ("ma", "x", "core", "fc"))
    rows = ("ma", "x", "core")
    in_specs = (
        P(None, rows, "fc", None),
        P(rows, "fc"),
        P(),
        P(),
        P(None, rows, "fc", None),
    )
    return jax.shard_map(
        functools.partial(body, x_count, sizes["fc"]),
        mesh=split,
        in_specs=in_specs,
        out_specs=P(None, rows, "fc", None),
        check_vma=False,
    )
```

```python
import functools
import math

import jax
import jax.numpy as jnp
from jax import lax
from jax.experimental import pallas as pl
from jax.experimental.pallas import tpu as pltpu
from jax.sharding import Mesh
from jax.sharding import PartitionSpec as P

ITERS = 2
BF16 = jnp.bfloat16
F32 = jnp.float32
MIB = 1024 * 1024
APPLY_BYTES = 30 * MIB
SMALL_BYTES = 8 * MIB
HIGH = lax.Precision.HIGHEST


def rolled(value, shift):
    return pltpu.roll(value, shift % value.shape[-1], 1)


def apply_kernel(n_vec, z_count, own, offsets, keep, send, *refs):
    place_ref, *refs = refs
    vec_refs = (refs[:n_vec], refs[n_vec : 2 * n_vec])
    piece_refs = refs[2 * n_vec : 2 * n_vec + len(offsets)]
    cov_ref, spec_ref, *refs = refs[2 * n_vec + len(offsets) :]
    *refs, beam_ref, vec_ref, z_ref, y_ref, sems = refs
    n_out = len(keep) + len(send)
    added, out_refs = refs[: len(refs) - n_out], refs[len(refs) - n_out :]
    count, rows, lanes = out_refs[0].shape
    freqs = 2 * count
    half = rows // 2
    components = spec_ref.shape[0]
    size, width, part_depth = piece_refs[0].shape
    chips = count // size * z_count
    tiles, _, step = z_ref.shape
    lane = lax.broadcasted_iota(jnp.int32, (half, lanes), 1)
    is_real = (lane // own) % 2 == 0
    sign = jnp.where(is_real, -1.0, 1.0).astype(F32)

    copies = []
    for index, (core, offset, part) in enumerate(offsets):
        at = lax.rem(place_ref[0] + (offset % chips), chips)
        x_at = at // z_count
        z_at = jnp.where(x_at == 0, at, chips - 1 - at)
        target = beam_ref.at[
            pl.ds(core * count + x_at * size, size),
            pl.ds(pl.multiple_of(z_at * width, width), width),
            pl.ds(part * part_depth, part_depth),
        ]
        copies.append(pltpu.make_async_copy(piece_refs[index], target, sems.at[index]))
    for copy in copies:
        copy.start()

    def gather(side, place, carry):
        vec = vec_refs[side][0][place]
        for other in vec_refs[side][1:]:
            vec = vec + other[place]
        vec_ref[side * count + place] = vec.astype(BF16)
        return carry

    for side in range(2):
        lax.fori_loop(0, count, functools.partial(gather, side), 0, unroll=8)
    for copy in copies:
        copy.wait()

    def project(freq, carry):
        z = jnp.dot(vec_ref[freq], beam_ref[freq], preferred_element_type=F32)
        for tile in range(tiles):
            z_ref[tile, pl.ds(freq, rows, stride=freqs), :] = z[:, tile * step : (tile + 1) * step]
        return carry

    lax.fori_loop(0, freqs, project, 0, unroll=64)

    def mix(row, carry):
        start = pl.multiple_of(row * freqs, freqs)
        z = jnp.concatenate([z_ref[tile, pl.ds(start, freqs), :] for tile in range(tiles)], axis=1)
        scaled = [(z * spec_ref[k][None, :]).astype(BF16) for k in range(components)]
        y = jnp.dot(cov_ref[...], jnp.concatenate(scaled, axis=0), preferred_element_type=F32)
        for tile in range(tiles):
            y_ref[tile, pl.ds(start, freqs), :] = y[:, tile * step : (tile + 1) * step]
        return carry

    lax.fori_loop(0, rows, mix, 0, unroll=32)

    def expand(side, place, carry):
        freq = side * count + place
        y = [
            y_ref[tile, pl.ds(freq, rows, stride=freqs), :].astype(BF16) for tile in range(tiles)
        ]
        product = lax.dot_general(
            jnp.concatenate(y, axis=1),
            beam_ref[freq],
            (((1,), (1,)), ((), ())),
            preferred_element_type=F32,
        )
        swapped = jnp.where(
            jnp.concatenate([is_real, is_real], axis=0),
            rolled(product, -own),
            rolled(product, own),
        )
        top = product[:half] + sign * swapped[half:]
        bottom = product[half:] - sign * swapped[:half]
        image = jnp.concatenate([top, bottom], axis=0)
        if added:
            image = image + added[side][place]
        if side in keep:
            out_refs[keep.index(side)][place] = image
        if side in send:
            out_refs[len(keep) + send.index(side)][place] = image.astype(BF16)
        return carry

    for side in range(2):
        lax.fori_loop(0, count, functools.partial(expand, side), 0, unroll=64)


def apply_covariance(place, vecs, beams, cov, spec, own, z_count, keep, send, added=()):
    count, rows, lanes = vecs[0][0].shape
    freqs = 2 * count
    depth = spec.shape[1]
    step = min(depth, 128)
    flops = 2 * freqs * rows * (2 * lanes * depth + 2 * freqs * depth)
    vmem = pl.BlockSpec(memory_space=pltpu.VMEM)
    n_vec = len(vecs[0])
    offsets = tuple(beam[1:] for beam in beams)
    tiles = pltpu.VMEM((depth // step, rows * freqs, step), F32)
    return pl.pallas_call(
        functools.partial(apply_kernel, n_vec, z_count, own, offsets, keep, send),
        out_shape=[jax.ShapeDtypeStruct((count, rows, lanes), F32)] * len(keep)
        + [jax.ShapeDtypeStruct((count, rows, lanes), BF16)] * len(send),
        in_specs=[pl.BlockSpec(memory_space=pltpu.SMEM)]
        + [vmem] * (2 * n_vec)
        + [pl.BlockSpec(memory_space=pl.ANY)] * len(beams)
        + [vmem] * (2 + len(added)),
        out_specs=[vmem] * (len(keep) + len(send)),
        scratch_shapes=[
            pltpu.VMEM((freqs, lanes, depth), BF16),
            pltpu.VMEM((freqs, rows, lanes), BF16),
            tiles,
            tiles,
            pltpu.SemaphoreType.DMA((len(beams),)),
        ],
        compiler_params=pltpu.CompilerParams(vmem_limit_bytes=APPLY_BYTES),
        cost_estimate=pl.CostEstimate(
            flops=flops, bytes_accessed=freqs * lanes * depth * 2, transcendentals=0
        ),
    )(place, *vecs[0], *vecs[1], *[beam[0] for beam in beams], cov, spec, *added)


def pack_kernel(own, first_ref, second_ref, out_ref):
    x_count, z_count, groups = out_ref.shape[:3]
    freqs, rows, lanes = first_ref.shape
    per_group = lanes // own
    lane = lax.broadcasted_iota(jnp.int32, (rows, lanes), 1) // own

    def group(index, carry):
        x_index, group_index = index // groups, index % groups
        totals = [jnp.zeros((rows, lanes), F32)] * z_count
        for place in range(per_group):
            freq = index * per_group + place
            image = first_ref[freq] + second_ref[freq]
            for z_index in range(z_count):
                moved = rolled(image, (place - 2 * z_index) * own)
                totals[z_index] = jnp.where(lane == place, moved, totals[z_index])
        for z_index in range(z_count):
            out_ref[x_index, z_index, group_index] = totals[z_index].astype(BF16)
        return carry

    lax.fori_loop(0, x_count * groups, group, 0, unroll=2)


def pack(first, second, x_count, z_count, own):
    freqs, rows, lanes = first.shape
    groups = freqs * own // (x_count * lanes)
    return pl.pallas_call(
        functools.partial(pack_kernel, own),
        out_shape=jax.ShapeDtypeStruct((x_count, z_count, groups, rows, lanes), BF16),
        in_specs=[pl.BlockSpec(memory_space=pltpu.VMEM)] * 2,
        out_specs=pl.BlockSpec(memory_space=pltpu.VMEM),
        compiler_params=pltpu.CompilerParams(vmem_limit_bytes=SMALL_BYTES),
    )(first, second)


def fold(matrix):
    half = matrix.shape[0] // 2
    row = lax.broadcasted_iota(jnp.int32, (half, 2 * half), 0)
    lane = lax.broadcasted_iota(jnp.int32, (half, 2 * half), 1)
    top, bottom = rolled(matrix[:half], half), matrix[half:]
    square = jnp.where((lane >= half) & (row >= lane - half), top, bottom)
    diagonal = jnp.sum(jnp.where(row == lane - half, bottom, 0.0), axis=0, keepdims=True)
    return jnp.concatenate([square, jnp.broadcast_to(diagonal, (8, 2 * half))], axis=0)


def unfold(folded):
    order = folded.shape[1]
    half = order // 2
    lane = lax.broadcasted_iota(jnp.int32, (half, order), 1)
    bottom = folded[:half]
    top = jnp.where(lane < half, rolled(bottom, half), bottom)
    whole = jnp.concatenate([top, bottom], axis=0)
    row = lax.broadcasted_iota(jnp.int32, (order, order), 0)
    lane = lax.broadcasted_iota(jnp.int32, (order, order), 1)
    own = ((row < half) & (row >= lane)) | ((row >= half) & ((lane < half) | (row < lane)))
    matrix = jnp.where(own, whole, whole.T)
    return jnp.where((row == lane) & (row >= half), folded[half : half + 1], matrix)


def gram_kernel(core_ref, rows_ref, start_ref, keep_ref, send_ref):
    senders, groups, parts, vectors, lanes = rows_ref.shape
    total = senders * vectors
    own = start_ref.shape[2]
    per_group = lanes // own
    first = jnp.zeros((total, total), F32)
    second = jnp.zeros((total, total), F32)
    for group in range(groups):
        for part in range(parts):
            flat = rows_ref[:, group, part].reshape(total, lanes)
            start = start_ref[part, group * per_group : (group + 1) * per_group].reshape(lanes, total)
            first += jnp.dot(flat, start.astype(BF16), preferred_element_type=F32)
            second += lax.dot_general(
                flat, flat, (((1,), (1,)), ((), ())), preferred_element_type=F32
            )
    first, second = fold(0.5 * (first + first.T)), fold(second)
    is_first = core_ref[0] == 0
    keep_ref[...] = jnp.where(is_first, first, second)
    send_ref[...] = jnp.where(is_first, second, first)


def grams(core, rows, start):
    total = rows.shape[0] * rows.shape[3]
    return pl.pallas_call(
        gram_kernel,
        out_shape=[jax.ShapeDtypeStruct((total // 2 + 8, total), F32)] * 2,
        in_specs=[pl.BlockSpec(memory_space=pltpu.SMEM)] + [pl.BlockSpec(memory_space=pltpu.VMEM)] * 2,
        out_specs=[pl.BlockSpec(memory_space=pltpu.VMEM)] * 2,
        compiler_params=pltpu.CompilerParams(vmem_limit_bytes=SMALL_BYTES),
    )(core, rows, start)


def triple(value):
    high = value.astype(BF16)
    rest = value - high.astype(F32)
    middle = rest.astype(BF16)
    return high, middle, (rest - middle.astype(F32)).astype(BF16)


def inverse_factor(work_ref, matrix):
    order = matrix.shape[0]
    step = 16
    row = lax.broadcasted_iota(jnp.int32, (step, order), 0)
    lane = lax.broadcasted_iota(jnp.int32, (step, order), 1)
    at = lax.broadcasted_iota(jnp.int32, (order, order), 0)
    work_ref[:, :order] = matrix
    work_ref[:, order:] = jnp.where(at == lax.broadcasted_iota(jnp.int32, (order, order), 1), 1.0, 0.0)
    for begin in range(0, order, step):
        block = slice(begin, begin + step)
        left, right = work_ref[block, :order], work_ref[block, order:]
        columns = [
            jnp.broadcast_to(left[:, begin + k : begin + k + 1], (step, order)) for k in range(step)
        ]
        for k in range(step):
            root = lax.rsqrt(columns[k][k : k + 1])
            factor = columns[k] * root

            def eliminate(value):
                pivot = value[k : k + 1] * root
                return jnp.where(row == k, pivot, jnp.where(row > k, value - factor * pivot, value))

            left, right = eliminate(left), eliminate(right)
            columns = columns[: k + 1] + [eliminate(c) for c in columns[k + 1 :]]
        work_ref[block, order:] = right
        end = begin + step
        if end < order:
            kept = jnp.where(lane >= end, left, 0.0)
            high, middle, low = triple(kept)
            first = jnp.concatenate([high, high, middle, high, low, middle], axis=0).astype(F32).T
            high, middle, low = triple(jnp.concatenate([kept, right], axis=1))
            second = jnp.concatenate([high, middle, high, low, high, middle], axis=0)
            change = jnp.dot(first[end:].astype(BF16), second, preferred_element_type=F32)
            work_ref[end:, :] = work_ref[end:, :] - change
    return work_ref[:, order:]


def finish_kernel(scale, core_ref, rows_ref, kept_ref, given_ref, out_ref, work_ref):
    senders, groups, parts, vectors, lanes = rows_ref.shape
    total = senders * vectors
    exact = functools.partial(lax.dot_general, precision=HIGH, preferred_element_type=F32)
    across = (((1,), (1,)), ((), ()))
    plain = (((1,), (0,)), ((), ()))
    is_first = core_ref[0] == 0
    first = inverse_factor(work_ref, unfold(jnp.where(is_first, kept_ref[...], given_ref[...])))
    gram_second = unfold(jnp.where(is_first, given_ref[...], kept_ref[...]))
    gram_second = exact(exact(first, gram_second, plain), first, across)
    second = inverse_factor(work_ref, gram_second)
    mixing = exact(second, first, plain) * scale
    high, middle, low = triple(mixing)
    for group in range(groups):
        for part in range(parts):
            flat = rows_ref[:, group, part].reshape(total, lanes)
            turned = flat.astype(F32).T.astype(BF16)
            dot = functools.partial(
                lax.dot_general, turned, dimension_numbers=across, preferred_element_type=F32
            )
            out_ref[part, group] = (dot(low) + dot(middle)) + dot(high)


def finish(core, rows, kept, given, scale):
    senders, groups, parts, vectors, lanes = rows.shape
    total = senders * vectors
    return pl.pallas_call(
        functools.partial(finish_kernel, scale),
        out_shape=jax.ShapeDtypeStruct((parts, groups, lanes, total), F32),
        in_specs=[pl.BlockSpec(memory_space=pltpu.SMEM)] + [pl.BlockSpec(memory_space=pltpu.VMEM)] * 3,
        out_specs=pl.BlockSpec(memory_space=pltpu.VMEM),
        scratch_shapes=[pltpu.VMEM((total, 2 * total), F32)],
        compiler_params=pltpu.CompilerParams(vmem_limit_bytes=SMALL_BYTES),
    )(core, rows, kept, given)


def whiten_kernel(core_ref, beam_ref, noise_ref, *out_refs):
    chunks = len(out_refs) // 2
    depth = out_refs[0].shape[2]
    parts, freqs, own, multipoles = beam_ref.shape
    half = multipoles // 2
    level = lax.rsqrt(noise_ref[...])
    is_first = core_ref[0] == 0
    for freq in range(freqs):
        column = jnp.broadcast_to(level[:, freq : freq + 1], (own, half))
        for part in range(parts):
            low = (beam_ref[part, freq, :, :half].astype(F32) * column).astype(BF16)
            high = (beam_ref[part, freq, :, half:].astype(F32) * column).astype(BF16)
            rows = slice(part * own, (part + 1) * own)
            keep = jnp.where(is_first, low, high)
            send = jnp.where(is_first, high, low)
            for chunk in range(chunks):
                cut = slice(chunk * depth, (chunk + 1) * depth)
                out_refs[chunk][freq, rows] = keep[:, cut]
                out_refs[chunks + chunk][freq, rows] = send[:, cut]


def whiten(core, beam, noise, chunks):
    parts, freqs, own, multipoles = beam.shape
    depth = multipoles // (2 * chunks)
    return pl.pallas_call(
        whiten_kernel,
        out_shape=[jax.ShapeDtypeStruct((freqs, parts * own, depth), BF16)] * (2 * chunks),
        in_specs=[pl.BlockSpec(memory_space=pltpu.SMEM)] + [pl.BlockSpec(memory_space=pltpu.VMEM)] * 2,
        out_specs=[pl.BlockSpec(memory_space=pltpu.VMEM)] * (2 * chunks),
        compiler_params=pltpu.CompilerParams(vmem_limit_bytes=SMALL_BYTES),
    )(core, beam, noise.T)


def turn_kernel(start_ref, out_ref):
    parts, freqs, own, vectors = start_ref.shape
    receivers, groups, mine, lanes = out_ref.shape
    per_group = lanes // (parts * own)

    def group(index, carry):
        tiles = [
            start_ref[part, index * per_group + place]
            for place in range(per_group)
            for part in range(parts)
        ]
        turned = jnp.concatenate(tiles, axis=0).T
        out_ref[:, index] = turned.reshape(receivers, mine, lanes).astype(BF16)
        return carry

    lax.fori_loop(0, groups, group, 0)


def turn(start, receivers, lanes):
    parts, freqs, own, vectors = start.shape
    groups = parts * freqs * own // lanes
    return pl.pallas_call(
        turn_kernel,
        out_shape=jax.ShapeDtypeStruct((receivers, groups, vectors // receivers, lanes), BF16),
        in_specs=[pl.BlockSpec(memory_space=pltpu.VMEM)],
        out_specs=pl.BlockSpec(memory_space=pltpu.VMEM),
        compiler_params=pltpu.CompilerParams(vmem_limit_bytes=SMALL_BYTES),
    )(start)


def operand_kernel(own, *refs):
    x_count, z_count, groups, mine, lanes = refs[0].shape
    parts = lanes // (z_count * own)
    width = parts * own
    lane = lax.broadcasted_iota(jnp.int32, (mine, lanes), 1)
    is_real = (lane // own) % 2 == 0

    def group(side, index, carry):
        x_index, at = index // groups, index % groups
        tiles = [refs[side][x_index, z, at].astype(F32) for z in range(z_count)]
        for place in range(z_count):
            top = tiles[0]
            for z in range(z_count):
                top = jnp.where(lane // width == z, rolled(tiles[z], (z - place) * width), top)
            bottom = jnp.where(is_real, rolled(top, -own), -rolled(top, own))
            image = jnp.concatenate([top, bottom], axis=0).astype(BF16)
            refs[2 + side][index * z_count + place] = image
        return carry

    for side in range(2):
        lax.fori_loop(0, x_count * groups, functools.partial(group, side), 0, unroll=4)


def start_operand(sides, own):
    x_count, z_count, groups, mine, lanes = sides[0].shape
    freqs = x_count * groups * z_count
    return pl.pallas_call(
        functools.partial(operand_kernel, own),
        out_shape=[jax.ShapeDtypeStruct((freqs, 2 * mine, lanes), BF16)] * 2,
        in_specs=[pl.BlockSpec(memory_space=pltpu.VMEM)] * 2,
        out_specs=[pl.BlockSpec(memory_space=pltpu.VMEM)] * 2,
        compiler_params=pltpu.CompilerParams(vmem_limit_bytes=SMALL_BYTES),
    )(*sides)


def swap_cores(value):
    return lax.ppermute(value, "core", [(0, 1), (1, 0)])


def after(value, event):
    return lax.optimization_barrier((value, event))


def gather_ring(sets, late, x_count, z_count):
    count = x_count * z_count
    ring = [k if k < z_count else z_count + count - 1 - k for k in range(count)]
    pairs = {
        1: [(ring[k], ring[(k + 1) % count]) for k in range(count)],
        -1: [(ring[(k + 1) % count], ring[k]) for k in range(count)],
    }
    x_place, z_place = lax.axis_index("x"), lax.axis_index("fc")
    place = jnp.where(x_place == 0, z_place, count - 1 - z_place).astype(jnp.int32).reshape(1)
    moving, found = {}, []
    for chunk, blocks in enumerate(sets):
        for core, block in enumerate(blocks):
            found.append((block, core, 0, chunk))
            moving[chunk, core, 1] = moving[chunk, core, -1] = block
    for hop in range(1, count // 2 + 1):
        for key in moving:
            chunk, core, way = key
            if 2 * hop == count and (way == 1) != (core == 0):
                continue
            moving[key] = lax.ppermute(moving[key], ("x", "fc"), pairs[way])
            if hop == 1 and key == (0, 0, 1):
                late, moving[key] = after(late, moving[key])
            found.append((moving[key], core, -way * hop, chunk))
    return place, found, late


def sum_devices(keep, send, z_count):
    value = keep + swap_cores(send)
    value = value + lax.ppermute(value, "x", [(0, 1), (1, 0)])
    if z_count & (z_count - 1):
        value = lax.psum(value, "fc")
    else:
        terms = [value] + [
            lax.ppermute(value, "fc", [(j, j ^ s) for j in range(z_count)]) for s in range(1, z_count)
        ]
        while len(terms) > 1:
            terms = [terms[i] + terms[i + 1] for i in range(0, len(terms), 2)]
        value = terms[0]
    return value, swap_cores(value)


def body_split(x_count, z_count, beam_transfer, noise_var, spectra, freq_covariance, start_vectors):
    parts, freqs, own, multipoles = beam_transfer.shape
    vectors = start_vectors.shape[3]
    cores = 2
    core = lax.axis_index("core")
    all_freqs = x_count * cores * freqs
    mine_vectors = vectors // (x_count * z_count)
    depth = multipoles // cores

    core_index = core.astype(jnp.int32).reshape(1)
    chunks = 2 if depth % 256 == 0 else 1
    cut = whiten(core_index, beam_transfer, noise_var, chunks)
    sets = [[cut[chunk], swap_cores(cut[chunks + chunk])] for chunk in range(chunks)]
    start = turn(start_vectors, x_count * z_count, z_count * parts * own)
    place, beams, start = gather_ring(sets, start, x_count, z_count)

    spec = spectra.reshape(-1, cores, depth)
    spec = lax.dynamic_index_in_dim(spec, core, 1, False)
    cov = freq_covariance.reshape(-1, x_count, cores, freqs, x_count, cores, freqs).astype(BF16)
    cov = jnp.where(core == 0, cov, jnp.flip(cov, (2, 5)))
    cov = cov.transpose(2, 1, 3, 0, 5, 4, 6).reshape(all_freqs, -1)

    start = lax.all_to_all(start, ("x", "fc"), 0, 0, tiled=True)
    start = start.reshape(x_count, z_count, *start.shape[1:])
    operand = start_operand([start, swap_cores(start)], own)

    apply = functools.partial(apply_covariance, place)
    added, width = (), depth // chunks
    for chunk in range(chunks):
        part = [(piece, at, offset, 0) for piece, at, offset, which in beams if which == chunk]
        part_spec = spec[:, chunk * width : (chunk + 1) * width]
        send = (0, 1) if chunk == chunks - 1 else ()
        added = apply(
            [[operand[0]], [operand[1]]], part, cov, part_spec, own, z_count, (0, 1), send, added
        )
    mine, theirs, mine_sent, theirs_sent = added
    got_mine, got_theirs = swap_cores(theirs_sent), swap_cores(mine_sent)
    second_mine, second_sent = apply(
        [[mine, got_mine], [theirs, got_theirs]], beams, cov, spec, own, z_count, (0,), (1,)
    )
    packed = pack(second_mine, swap_cores(second_sent), x_count, z_count, own)
    packed = packed.reshape(x_count * z_count, *packed.shape[2:])
    received = lax.all_to_all(packed, ("x", "fc"), 0, 0, tiled=True)
    groups, lanes = received.shape[1], received.shape[3]
    received = received.reshape(-1, groups, parts, mine_vectors, lanes)

    kept_gram, given_gram = sum_devices(*grams(core_index, received, start_vectors), z_count)
    scale = math.sqrt(2.0 * all_freqs * z_count * own)
    basis = finish(core_index, received, kept_gram, given_gram, scale)
    return basis.reshape(parts, freqs, own, vectors)


def row_operands(row_part, spectra):
    scaled = (row_part.astype(F32)[None] * spectra[:, None, None, :]).astype(BF16)
    real_rows = jnp.concatenate([scaled[:, 0], scaled[:, 1]], axis=-1)
    imag_rows = jnp.concatenate([scaled[:, 1], -scaled[:, 0]], axis=-1)
    return jnp.stack([real_rows, imag_rows], axis=1)


def apply_tile(pair_tile, vec_bf):
    row_count = pair_tile.shape[1]
    stacked = pair_tile.reshape(2 * row_count, pair_tile.shape[2])
    with_real = jnp.dot(stacked, vec_bf[0], preferred_element_type=F32)
    with_imag = jnp.dot(stacked, vec_bf[1], preferred_element_type=F32)
    real_part = with_real[:row_count] - with_imag[row_count:]
    imag_part = with_real[row_count:] + with_imag[:row_count]
    return jnp.stack([real_part, imag_part], axis=0)


def partial_gram(image):
    flat = image.reshape(-1, image.shape[-1])
    return jnp.dot(flat.T, flat, precision=HIGH, preferred_element_type=F32)


def orthonormalize(image, gram_matrix):
    lower = jnp.linalg.cholesky(gram_matrix)
    flat = image.reshape(-1, image.shape[-1])
    solved = lax.linalg.triangular_solve(lower, flat, left_side=False, lower=True, transpose_a=True)
    return solved.reshape(image.shape)


def body_general(beam_transfer, noise_var, spectra, freq_covariance, start_vectors):
    row_axes = ("x", "core")
    whitened = (beam_transfer.astype(F32) * lax.rsqrt(noise_var)[None, :, :, None]).astype(BF16)
    row_beams = lax.all_gather(whitened, "fc", axis=2, tiled=True)
    _, freq_rows, mode_count, multipoles = row_beams.shape
    row_total = freq_rows * mode_count
    components = spectra.shape[0]
    vectors_count = start_vectors.shape[3]
    row_operand = row_operands(row_beams.reshape(2, row_total, multipoles), spectra)
    row_start = lax.axis_index(row_axes) * freq_rows
    row_cov = lax.dynamic_slice_in_dim(freq_covariance, row_start, freq_rows, 1)
    piece = lax.all_gather(whitened, row_axes, axis=1, tiled=True)
    _, piece_freqs, piece_modes, _ = piece.shape
    columns = piece.reshape(2, piece_freqs * piece_modes, multipoles)
    col_operand = jnp.concatenate([columns[0], columns[1]], axis=-1)
    products = lax.dot_general(
        row_operand, col_operand, (((3,), (1,)), ((), ())), preferred_element_type=F32
    )
    weight = jnp.broadcast_to(
        row_cov[:, :, None, :, None], (components, freq_rows, mode_count, piece_freqs, piece_modes)
    )
    weight = weight.reshape(components, row_total, piece_freqs * piece_modes)
    pair_tile = jnp.einsum("kxy,kcxy->cxy", weight, products).astype(BF16)
    vectors = start_vectors
    own_modes = start_vectors.shape[2]
    for _ in range(ITERS):
        gathered = lax.all_gather(vectors.astype(BF16), row_axes, axis=1, tiled=True)
        vec_bf = gathered.reshape(2, -1, vectors_count)
        partial_value = apply_tile(pair_tile, vec_bf).reshape(2, freq_rows, mode_count, vectors_count)
        summed = lax.psum(partial_value, "fc")
        gram_matrix = lax.psum(partial_gram(summed), row_axes)
        own_rows = lax.dynamic_slice_in_dim(summed, lax.axis_index("fc") * own_modes, own_modes, 2)
        vectors = orthonormalize(own_rows, gram_matrix)
    return vectors * math.sqrt(2.0 * piece_freqs * mode_count)


def body(x_count, z_count, *args):
    beam_transfer, start_vectors = args[0], args[4]
    parts, freqs, own, multipoles = beam_transfer.shape
    vectors = start_vectors.shape[3]
    lanes = parts * own * z_count
    fits = (
        x_count == 2
        and vectors % (16 * x_count * z_count) == 0
        and lanes == 128
        and own % 16 == 0
        and multipoles % 256 == 0
        and (freqs * own) % lanes == 0
    )
    if fits:
        return body_split(x_count, z_count, *args)
    return body_general(*args)


def solution(mesh):
    sizes = dict(mesh.shape)
    x_count = sizes["fr"] // 2
    shape = (sizes["ma"], x_count, 2, sizes["fc"])
    devices = mesh.devices.reshape(shape)
    split = Mesh(devices, ("ma", "x", "core", "fc"))
    rows = ("ma", "x", "core")
    in_specs = (
        P(None, rows, "fc", None),
        P(rows, "fc"),
        P(),
        P(),
        P(None, rows, "fc", None),
    )
    return jax.shard_map(
        functools.partial(body, x_count, sizes["fc"]),
        mesh=split,
        in_specs=in_specs,
        out_specs=P(None, rows, "fc", None),
        check_vma=False,
    )
```

```python
import functools
import math

import jax
import jax.numpy as jnp
from jax import lax
from jax.experimental import pallas as pl
from jax.experimental.pallas import tpu as pltpu
from jax.sharding import Mesh
from jax.sharding import PartitionSpec as P

ITERS = 2
BF16 = jnp.bfloat16
F32 = jnp.float32
MIB = 1024 * 1024
APPLY_BYTES = 30 * MIB
SMALL_BYTES = 8 * MIB
HIGH = lax.Precision.HIGHEST


def rolled(value, shift):
    return pltpu.roll(value, shift % value.shape[-1], 1)


def apply_kernel(n_vec, n_whole, z_count, own, offsets, keep, send, *refs):
    place_ref, *refs = refs
    vec_refs = (refs[:n_vec], refs[n_vec : 2 * n_vec])
    n_beam = len(offsets) + n_whole
    beam_refs = refs[2 * n_vec : 2 * n_vec + n_beam]
    cov_ref, spec_ref, *refs = refs[2 * n_vec + n_beam :]
    *refs, beam_ref, vec_ref, z_ref, y_ref, sems = refs
    n_out = len(keep) + len(send)
    added, out_refs = refs[: len(refs) - n_out], refs[len(refs) - n_out :]
    count, rows, lanes = out_refs[0].shape
    freqs = 2 * count
    half = rows // 2
    components = spec_ref.shape[0]
    tiles, _, step = z_ref.shape
    lane = lax.broadcasted_iota(jnp.int32, (half, lanes), 1)
    is_real = (lane // own) % 2 == 0
    sign = jnp.where(is_real, -1.0, 1.0).astype(F32)

    copies = []
    for index, (core, offset) in enumerate(offsets):
        size, width, _ = beam_refs[index].shape
        chips = count // size * z_count
        at = lax.rem(place_ref[0] + (offset % chips), chips)
        x_at = at // z_count
        z_at = jnp.where(x_at == 0, at, chips - 1 - at)
        target = beam_ref.at[
            pl.ds(core * count + x_at * size, size), pl.ds(pl.multiple_of(z_at * width, width), width)
        ]
        copies.append(pltpu.make_async_copy(beam_refs[index], target, sems.at[index]))
    for copy in copies:
        copy.start()

    def beam_of(freq):
        side_by_side = [beam_ref, *beam_refs[len(offsets) :]]
        return jnp.concatenate([beam[freq] for beam in side_by_side], axis=1)

    def gather(side, place, carry):
        vec = vec_refs[side][0][place]
        for other in vec_refs[side][1:]:
            vec = vec + other[place]
        vec_ref[side * count + place] = vec.astype(BF16)
        return carry

    for side in range(2):
        lax.fori_loop(0, count, functools.partial(gather, side), 0, unroll=8)
    for copy in copies:
        copy.wait()

    def project(freq, carry):
        z = jnp.dot(vec_ref[freq], beam_of(freq), preferred_element_type=F32)
        for tile in range(tiles):
            z_ref[tile, pl.ds(freq, rows, stride=freqs), :] = z[:, tile * step : (tile + 1) * step]
        return carry

    lax.fori_loop(0, freqs, project, 0, unroll=64)

    def mix(row, carry):
        start = pl.multiple_of(row * freqs, freqs)
        z = jnp.concatenate([z_ref[tile, pl.ds(start, freqs), :] for tile in range(tiles)], axis=1)
        scaled = [(z * spec_ref[k][None, :]).astype(BF16) for k in range(components)]
        y = jnp.dot(cov_ref[...], jnp.concatenate(scaled, axis=0), preferred_element_type=F32)
        for tile in range(tiles):
            y_ref[tile, pl.ds(start, freqs), :] = y[:, tile * step : (tile + 1) * step]
        return carry

    lax.fori_loop(0, rows, mix, 0, unroll=32)

    def expand(side, place, carry):
        freq = side * count + place
        y = [
            y_ref[tile, pl.ds(freq, rows, stride=freqs), :].astype(BF16) for tile in range(tiles)
        ]
        product = lax.dot_general(
            jnp.concatenate(y, axis=1),
            beam_of(freq),
            (((1,), (1,)), ((), ())),
            preferred_element_type=F32,
        )
        swapped = jnp.where(
            jnp.concatenate([is_real, is_real], axis=0),
            rolled(product, -own),
            rolled(product, own),
        )
        top = product[:half] + sign * swapped[half:]
        bottom = product[half:] - sign * swapped[:half]
        image = jnp.concatenate([top, bottom], axis=0)
        if added:
            image = image + added[side][place]
        if side in keep:
            out_refs[keep.index(side)][place] = image
        if side in send:
            out_refs[len(keep) + send.index(side)][place] = image.astype(BF16)
        return carry

    for side in range(2):
        lax.fori_loop(0, count, functools.partial(expand, side), 0, unroll=64)


def apply_covariance(place, vecs, beams, wholes, cov, spec, own, z_count, keep, send, give, added=()):
    count, rows, lanes = vecs[0][0].shape
    freqs = 2 * count
    depth = spec.shape[1]
    step = min(depth, 128)
    flops = 2 * freqs * rows * (2 * lanes * depth + 2 * freqs * depth)
    vmem = pl.BlockSpec(memory_space=pltpu.VMEM)
    n_vec = len(vecs[0])
    offsets = tuple(beam[1:] for beam in beams)
    arrays = [beam[0] for beam in beams] + wholes
    whole = (freqs, lanes, beams[0][0].shape[2])
    out_shape = [jax.ShapeDtypeStruct((count, rows, lanes), F32)] * len(keep)
    out_shape += [jax.ShapeDtypeStruct((count, rows, lanes), BF16)] * len(send)
    out_shape += [jax.ShapeDtypeStruct(whole, BF16)] * give
    tiles = pltpu.VMEM((depth // step, rows * freqs, step), F32)
    kernel = functools.partial(
        apply_kernel, n_vec, len(wholes), z_count, own, offsets, keep, send
    )
    return pl.pallas_call(
        kernel,
        out_shape=out_shape,
        in_specs=[pl.BlockSpec(memory_space=pltpu.SMEM)]
        + [vmem] * (2 * n_vec)
        + [pl.BlockSpec(memory_space=pl.ANY)] * len(beams)
        + [vmem] * (len(wholes) + 2 + len(added)),
        out_specs=[vmem] * len(out_shape),
        scratch_shapes=[pltpu.VMEM(whole, BF16)] * (not give)
        + [pltpu.VMEM((freqs, rows, lanes), BF16), tiles, tiles, pltpu.SemaphoreType.DMA((len(beams),))],
        compiler_params=pltpu.CompilerParams(vmem_limit_bytes=APPLY_BYTES),
        cost_estimate=pl.CostEstimate(
            flops=flops, bytes_accessed=freqs * lanes * depth * 2, transcendentals=0
        ),
    )(place, *vecs[0], *vecs[1], *arrays, cov, spec, *added)


def pack_kernel(own, first_ref, second_ref, out_ref):
    x_count, z_count, groups = out_ref.shape[:3]
    freqs, rows, lanes = first_ref.shape
    per_group = lanes // own
    lane = lax.broadcasted_iota(jnp.int32, (rows, lanes), 1) // own

    def group(index, carry):
        x_index, group_index = index // groups, index % groups
        totals = [jnp.zeros((rows, lanes), F32)] * z_count
        for place in range(per_group):
            freq = index * per_group + place
            image = first_ref[freq] + second_ref[freq]
            for z_index in range(z_count):
                moved = rolled(image, (place - 2 * z_index) * own)
                totals[z_index] = jnp.where(lane == place, moved, totals[z_index])
        for z_index in range(z_count):
            out_ref[x_index, z_index, group_index] = totals[z_index].astype(BF16)
        return carry

    lax.fori_loop(0, x_count * groups, group, 0, unroll=2)


def pack(first, second, x_count, z_count, own):
    freqs, rows, lanes = first.shape
    groups = freqs * own // (x_count * lanes)
    return pl.pallas_call(
        functools.partial(pack_kernel, own),
        out_shape=jax.ShapeDtypeStruct((x_count, z_count, groups, rows, lanes), BF16),
        in_specs=[pl.BlockSpec(memory_space=pltpu.VMEM)] * 2,
        out_specs=pl.BlockSpec(memory_space=pltpu.VMEM),
        compiler_params=pltpu.CompilerParams(vmem_limit_bytes=SMALL_BYTES),
    )(first, second)


def fold(matrix):
    half = matrix.shape[0] // 2
    row = lax.broadcasted_iota(jnp.int32, (half, 2 * half), 0)
    lane = lax.broadcasted_iota(jnp.int32, (half, 2 * half), 1)
    top, bottom = rolled(matrix[:half], half), matrix[half:]
    square = jnp.where((lane >= half) & (row >= lane - half), top, bottom)
    diagonal = jnp.sum(jnp.where(row == lane - half, bottom, 0.0), axis=0, keepdims=True)
    return jnp.concatenate([square, jnp.broadcast_to(diagonal, (8, 2 * half))], axis=0)


def unfold(folded):
    order = folded.shape[1]
    half = order // 2
    lane = lax.broadcasted_iota(jnp.int32, (half, order), 1)
    bottom = folded[:half]
    top = jnp.where(lane < half, rolled(bottom, half), bottom)
    whole = jnp.concatenate([top, bottom], axis=0)
    row = lax.broadcasted_iota(jnp.int32, (order, order), 0)
    lane = lax.broadcasted_iota(jnp.int32, (order, order), 1)
    own = ((row < half) & (row >= lane)) | ((row >= half) & ((lane < half) | (row < lane)))
    matrix = jnp.where(own, whole, whole.T)
    return jnp.where((row == lane) & (row >= half), folded[half : half + 1], matrix)


def gram_kernel(core_ref, rows_ref, start_ref, keep_ref, send_ref):
    senders, groups, parts, vectors, lanes = rows_ref.shape
    total = senders * vectors
    own = start_ref.shape[2]
    per_group = lanes // own
    first = jnp.zeros((total, total), F32)
    second = jnp.zeros((total, total), F32)
    for group in range(groups):
        for part in range(parts):
            flat = rows_ref[:, group, part].reshape(total, lanes)
            start = start_ref[part, group * per_group : (group + 1) * per_group].reshape(lanes, total)
            first += jnp.dot(flat, start.astype(BF16), preferred_element_type=F32)
            second += lax.dot_general(
                flat, flat, (((1,), (1,)), ((), ())), preferred_element_type=F32
            )
    first, second = fold(0.5 * (first + first.T)), fold(second)
    is_first = core_ref[0] == 0
    keep_ref[...] = jnp.where(is_first, first, second)
    send_ref[...] = jnp.where(is_first, second, first)


def grams(core, rows, start):
    total = rows.shape[0] * rows.shape[3]
    return pl.pallas_call(
        gram_kernel,
        out_shape=[jax.ShapeDtypeStruct((total // 2 + 8, total), F32)] * 2,
        in_specs=[pl.BlockSpec(memory_space=pltpu.SMEM)] + [pl.BlockSpec(memory_space=pltpu.VMEM)] * 2,
        out_specs=[pl.BlockSpec(memory_space=pltpu.VMEM)] * 2,
        compiler_params=pltpu.CompilerParams(vmem_limit_bytes=SMALL_BYTES),
    )(core, rows, start)


def triple(value):
    high = value.astype(BF16)
    rest = value - high.astype(F32)
    middle = rest.astype(BF16)
    return high, middle, (rest - middle.astype(F32)).astype(BF16)


def inverse_factor(work_ref, matrix):
    order = matrix.shape[0]
    step = 16
    row = lax.broadcasted_iota(jnp.int32, (step, order), 0)
    lane = lax.broadcasted_iota(jnp.int32, (step, order), 1)
    at = lax.broadcasted_iota(jnp.int32, (order, order), 0)
    work_ref[:, :order] = matrix
    work_ref[:, order:] = jnp.where(at == lax.broadcasted_iota(jnp.int32, (order, order), 1), 1.0, 0.0)
    for begin in range(0, order, step):
        block = slice(begin, begin + step)
        left, right = work_ref[block, :order], work_ref[block, order:]
        columns = [
            jnp.broadcast_to(left[:, begin + k : begin + k + 1], (step, order)) for k in range(step)
        ]
        for k in range(step):
            root = lax.rsqrt(columns[k][k : k + 1])
            factor = columns[k] * root

            def eliminate(value):
                pivot = value[k : k + 1] * root
                return jnp.where(row == k, pivot, jnp.where(row > k, value - factor * pivot, value))

            left, right = eliminate(left), eliminate(right)
            columns = columns[: k + 1] + [eliminate(c) for c in columns[k + 1 :]]
        work_ref[block, order:] = right
        end = begin + step
        if end < order:
            kept = jnp.where(lane >= end, left, 0.0)
            high, middle, low = triple(kept)
            first = jnp.concatenate([high, high, middle, high, low, middle], axis=0).astype(F32).T
            high, middle, low = triple(jnp.concatenate([kept, right], axis=1))
            second = jnp.concatenate([high, middle, high, low, high, middle], axis=0)
            change = jnp.dot(first[end:].astype(BF16), second, preferred_element_type=F32)
            work_ref[end:, :] = work_ref[end:, :] - change
    return work_ref[:, order:]


def finish_kernel(scale, core_ref, rows_ref, kept_ref, given_ref, out_ref, work_ref):
    senders, groups, parts, vectors, lanes = rows_ref.shape
    total = senders * vectors
    exact = functools.partial(lax.dot_general, precision=HIGH, preferred_element_type=F32)
    across = (((1,), (1,)), ((), ()))
    plain = (((1,), (0,)), ((), ()))
    is_first = core_ref[0] == 0
    first = inverse_factor(work_ref, unfold(jnp.where(is_first, kept_ref[...], given_ref[...])))
    gram_second = unfold(jnp.where(is_first, given_ref[...], kept_ref[...]))
    gram_second = exact(exact(first, gram_second, plain), first, across)
    second = inverse_factor(work_ref, gram_second)
    mixing = exact(second, first, plain) * scale
    high, middle, low = triple(mixing)
    for group in range(groups):
        for part in range(parts):
            flat = rows_ref[:, group, part].reshape(total, lanes)
            turned = flat.astype(F32).T.astype(BF16)
            dot = functools.partial(
                lax.dot_general, turned, dimension_numbers=across, preferred_element_type=F32
            )
            out_ref[part, group] = (dot(low) + dot(middle)) + dot(high)


def finish(core, rows, kept, given, scale):
    senders, groups, parts, vectors, lanes = rows.shape
    total = senders * vectors
    return pl.pallas_call(
        functools.partial(finish_kernel, scale),
        out_shape=jax.ShapeDtypeStruct((parts, groups, lanes, total), F32),
        in_specs=[pl.BlockSpec(memory_space=pltpu.SMEM)] + [pl.BlockSpec(memory_space=pltpu.VMEM)] * 3,
        out_specs=pl.BlockSpec(memory_space=pltpu.VMEM),
        scratch_shapes=[pltpu.VMEM((total, 2 * total), F32)],
        compiler_params=pltpu.CompilerParams(vmem_limit_bytes=SMALL_BYTES),
    )(core, rows, kept, given)


def whiten_kernel(core_ref, beam_ref, noise_ref, *out_refs):
    chunks = len(out_refs) // 2
    depth = out_refs[0].shape[2]
    parts, freqs, own, multipoles = beam_ref.shape
    half = multipoles // 2
    level = lax.rsqrt(noise_ref[...])
    is_first = core_ref[0] == 0
    for freq in range(freqs):
        column = jnp.broadcast_to(level[:, freq : freq + 1], (own, half))
        for part in range(parts):
            low = (beam_ref[part, freq, :, :half].astype(F32) * column).astype(BF16)
            high = (beam_ref[part, freq, :, half:].astype(F32) * column).astype(BF16)
            rows = slice(part * own, (part + 1) * own)
            keep = jnp.where(is_first, low, high)
            send = jnp.where(is_first, high, low)
            for chunk in range(chunks):
                cut = slice(chunk * depth, (chunk + 1) * depth)
                out_refs[chunk][freq, rows] = keep[:, cut]
                out_refs[chunks + chunk][freq, rows] = send[:, cut]


def whiten(core, beam, noise, chunks):
    parts, freqs, own, multipoles = beam.shape
    depth = multipoles // (2 * chunks)
    return pl.pallas_call(
        whiten_kernel,
        out_shape=[jax.ShapeDtypeStruct((freqs, parts * own, depth), BF16)] * (2 * chunks),
        in_specs=[pl.BlockSpec(memory_space=pltpu.SMEM)] + [pl.BlockSpec(memory_space=pltpu.VMEM)] * 2,
        out_specs=[pl.BlockSpec(memory_space=pltpu.VMEM)] * (2 * chunks),
        compiler_params=pltpu.CompilerParams(vmem_limit_bytes=SMALL_BYTES),
    )(core, beam, noise.T)


def order_kernel(size, core_ref, cov_ref, out_ref):
    components, order, _ = cov_ref.shape
    places = range(order // (2 * size))
    is_first = core_ref[0] == 0

    def ordered(value):
        found = []
        for core in range(2):
            starts = [(2 * x + (side ^ core)) * size for side in range(2) for x in places]
            found.append(jnp.concatenate([value[start : start + size] for start in starts], axis=0))
        return jnp.where(is_first, found[0], found[1])

    for k in range(components):
        out_ref[:, k * order : (k + 1) * order] = ordered(ordered(cov_ref[k]).T).T.astype(BF16)


def order_covariance(core, cov, size):
    components, order, _ = cov.shape
    return pl.pallas_call(
        functools.partial(order_kernel, size),
        out_shape=jax.ShapeDtypeStruct((order, components * order), BF16),
        in_specs=[pl.BlockSpec(memory_space=pltpu.SMEM), pl.BlockSpec(memory_space=pltpu.VMEM)],
        out_specs=pl.BlockSpec(memory_space=pltpu.VMEM),
        compiler_params=pltpu.CompilerParams(vmem_limit_bytes=SMALL_BYTES),
    )(core, cov)


def turn_kernel(start_ref, out_ref):
    parts, freqs, own, vectors = start_ref.shape
    receivers, groups, mine, lanes = out_ref.shape
    per_group = lanes // (parts * own)

    def group(index, carry):
        tiles = [
            start_ref[part, index * per_group + place]
            for place in range(per_group)
            for part in range(parts)
        ]
        turned = jnp.concatenate(tiles, axis=0).T
        out_ref[:, index] = turned.reshape(receivers, mine, lanes).astype(BF16)
        return carry

    lax.fori_loop(0, groups, group, 0)


def turn(start, receivers, lanes):
    parts, freqs, own, vectors = start.shape
    groups = parts * freqs * own // lanes
    return pl.pallas_call(
        turn_kernel,
        out_shape=jax.ShapeDtypeStruct((receivers, groups, vectors // receivers, lanes), BF16),
        in_specs=[pl.BlockSpec(memory_space=pltpu.VMEM)],
        out_specs=pl.BlockSpec(memory_space=pltpu.VMEM),
        compiler_params=pltpu.CompilerParams(vmem_limit_bytes=SMALL_BYTES),
    )(start)


def operand_kernel(own, *refs):
    x_count, z_count, groups, mine, lanes = refs[0].shape
    parts = lanes // (z_count * own)
    width = parts * own
    lane = lax.broadcasted_iota(jnp.int32, (mine, lanes), 1)
    is_real = (lane // own) % 2 == 0

    def group(side, index, carry):
        x_index, at = index // groups, index % groups
        tiles = [refs[side][x_index, z, at].astype(F32) for z in range(z_count)]
        for place in range(z_count):
            top = tiles[0]
            for z in range(z_count):
                top = jnp.where(lane // width == z, rolled(tiles[z], (z - place) * width), top)
            bottom = jnp.where(is_real, rolled(top, -own), -rolled(top, own))
            image = jnp.concatenate([top, bottom], axis=0).astype(BF16)
            refs[2 + side][index * z_count + place] = image
        return carry

    for side in range(2):
        lax.fori_loop(0, x_count * groups, functools.partial(group, side), 0, unroll=4)


def start_operand(sides, own):
    x_count, z_count, groups, mine, lanes = sides[0].shape
    freqs = x_count * groups * z_count
    return pl.pallas_call(
        functools.partial(operand_kernel, own),
        out_shape=[jax.ShapeDtypeStruct((freqs, 2 * mine, lanes), BF16)] * 2,
        in_specs=[pl.BlockSpec(memory_space=pltpu.VMEM)] * 2,
        out_specs=[pl.BlockSpec(memory_space=pltpu.VMEM)] * 2,
        compiler_params=pltpu.CompilerParams(vmem_limit_bytes=SMALL_BYTES),
    )(*sides)


def swap_cores(value):
    return lax.ppermute(value, "core", [(0, 1), (1, 0)])


def after(value, event):
    return lax.optimization_barrier((value, event))


def gather_ring(sets, late, x_count, z_count):
    count = x_count * z_count
    ring = [k if k < z_count else z_count + count - 1 - k for k in range(count)]
    pairs = {
        1: [(ring[k], ring[(k + 1) % count]) for k in range(count)],
        -1: [(ring[(k + 1) % count], ring[k]) for k in range(count)],
    }
    x_place, z_place = lax.axis_index("x"), lax.axis_index("fc")
    place = jnp.where(x_place == 0, z_place, count - 1 - z_place).astype(jnp.int32).reshape(1)
    moving, found = {}, []
    for chunk, blocks in enumerate(sets):
        for core, block in enumerate(blocks):
            found.append((block, core, 0, chunk))
            moving[chunk, core, 1] = moving[chunk, core, -1] = block
    for hop in range(1, count // 2 + 1):
        for key in moving:
            chunk, core, way = key
            if 2 * hop == count and (way == 1) != (core == 0):
                continue
            moving[key] = lax.ppermute(moving[key], ("x", "fc"), pairs[way])
            if hop == 1 and key == (0, 0, 1):
                late, moving[key] = after(late, moving[key])
            found.append((moving[key], core, -way * hop, chunk))
    return place, found, late


def sum_devices(keep, send, z_count):
    value = keep + swap_cores(send)
    value = value + lax.ppermute(value, "x", [(0, 1), (1, 0)])
    if z_count & (z_count - 1):
        value = lax.psum(value, "fc")
    else:
        terms = [value] + [
            lax.ppermute(value, "fc", [(j, j ^ s) for j in range(z_count)]) for s in range(1, z_count)
        ]
        while len(terms) > 1:
            terms = [terms[i] + terms[i + 1] for i in range(0, len(terms), 2)]
        value = terms[0]
    return value, swap_cores(value)


def body_split(x_count, z_count, beam_transfer, noise_var, spectra, freq_covariance, start_vectors):
    parts, freqs, own, multipoles = beam_transfer.shape
    vectors = start_vectors.shape[3]
    cores = 2
    core = lax.axis_index("core")
    all_freqs = x_count * cores * freqs
    mine_vectors = vectors // (x_count * z_count)
    depth = multipoles // cores

    core_index = core.astype(jnp.int32).reshape(1)
    chunks = 2 if depth % 256 == 0 else 1
    cut = whiten(core_index, beam_transfer, noise_var, chunks)
    sets = [[cut[chunk], swap_cores(cut[chunks + chunk])] for chunk in range(chunks)]
    start = turn(start_vectors, x_count * z_count, z_count * parts * own)
    place, beams, start = gather_ring(sets, start, x_count, z_count)

    spec = spectra.reshape(-1, cores, depth)
    spec = lax.dynamic_index_in_dim(spec, core, 1, False)
    cov = order_covariance(core_index, freq_covariance, freqs)

    start = lax.all_to_all(start, ("x", "fc"), 0, 0, tiled=True)
    start = start.reshape(x_count, z_count, *start.shape[1:])
    operand = start_operand([start, swap_cores(start)], own)

    apply = functools.partial(apply_covariance, place)
    added, wholes, width = [], [], depth // chunks
    cut_beams = [
        [(piece, at, offset) for piece, at, offset, which in beams if which == chunk]
        for chunk in range(chunks)
    ]
    for chunk in range(chunks):
        part_spec = spec[:, chunk * width : (chunk + 1) * width]
        send = (0, 1) if chunk == chunks - 1 else ()
        found = apply(
            [[operand[0]], [operand[1]]],
            cut_beams[chunk],
            [],
            cov,
            part_spec,
            own,
            z_count,
            (0, 1),
            send,
            chunk > 0,
            added,
        )
        added, whole = found[: 2 + len(send)], found[2 + len(send) :]
        wholes += whole
    mine, theirs, mine_sent, theirs_sent = added
    got_mine, got_theirs = swap_cores(theirs_sent), swap_cores(mine_sent)
    second_mine, second_sent = apply(
        [[mine, got_mine], [theirs, got_theirs]], cut_beams[0], wholes, cov, spec, own, z_count, (0,), (1,), False
    )
    packed = pack(second_mine, swap_cores(second_sent), x_count, z_count, own)
    packed = packed.reshape(x_count * z_count, *packed.shape[2:])
    received = lax.all_to_all(packed, ("x", "fc"), 0, 0, tiled=True)
    groups, lanes = received.shape[1], received.shape[3]
    received = received.reshape(-1, groups, parts, mine_vectors, lanes)

    kept_gram, given_gram = sum_devices(*grams(core_index, received, start_vectors), z_count)
    scale = math.sqrt(2.0 * all_freqs * z_count * own)
    basis = finish(core_index, received, kept_gram, given_gram, scale)
    return basis.reshape(parts, freqs, own, vectors)


def row_operands(row_part, spectra):
    scaled = (row_part.astype(F32)[None] * spectra[:, None, None, :]).astype(BF16)
    real_rows = jnp.concatenate([scaled[:, 0], scaled[:, 1]], axis=-1)
    imag_rows = jnp.concatenate([scaled[:, 1], -scaled[:, 0]], axis=-1)
    return jnp.stack([real_rows, imag_rows], axis=1)


def apply_tile(pair_tile, vec_bf):
    row_count = pair_tile.shape[1]
    stacked = pair_tile.reshape(2 * row_count, pair_tile.shape[2])
    with_real = jnp.dot(stacked, vec_bf[0], preferred_element_type=F32)
    with_imag = jnp.dot(stacked, vec_bf[1], preferred_element_type=F32)
    real_part = with_real[:row_count] - with_imag[row_count:]
    imag_part = with_real[row_count:] + with_imag[:row_count]
    return jnp.stack([real_part, imag_part], axis=0)


def partial_gram(image):
    flat = image.reshape(-1, image.shape[-1])
    return jnp.dot(flat.T, flat, precision=HIGH, preferred_element_type=F32)


def orthonormalize(image, gram_matrix):
    lower = jnp.linalg.cholesky(gram_matrix)
    flat = image.reshape(-1, image.shape[-1])
    solved = lax.linalg.triangular_solve(lower, flat, left_side=False, lower=True, transpose_a=True)
    return solved.reshape(image.shape)


def body_general(beam_transfer, noise_var, spectra, freq_covariance, start_vectors):
    row_axes = ("x", "core")
    whitened = (beam_transfer.astype(F32) * lax.rsqrt(noise_var)[None, :, :, None]).astype(BF16)
    row_beams = lax.all_gather(whitened, "fc", axis=2, tiled=True)
    _, freq_rows, mode_count, multipoles = row_beams.shape
    row_total = freq_rows * mode_count
    components = spectra.shape[0]
    vectors_count = start_vectors.shape[3]
    row_operand = row_operands(row_beams.reshape(2, row_total, multipoles), spectra)
    row_start = lax.axis_index(row_axes) * freq_rows
    row_cov = lax.dynamic_slice_in_dim(freq_covariance, row_start, freq_rows, 1)
    piece = lax.all_gather(whitened, row_axes, axis=1, tiled=True)
    _, piece_freqs, piece_modes, _ = piece.shape
    columns = piece.reshape(2, piece_freqs * piece_modes, multipoles)
    col_operand = jnp.concatenate([columns[0], columns[1]], axis=-1)
    products = lax.dot_general(
        row_operand, col_operand, (((3,), (1,)), ((), ())), preferred_element_type=F32
    )
    weight = jnp.broadcast_to(
        row_cov[:, :, None, :, None], (components, freq_rows, mode_count, piece_freqs, piece_modes)
    )
    weight = weight.reshape(components, row_total, piece_freqs * piece_modes)
    pair_tile = jnp.einsum("kxy,kcxy->cxy", weight, products).astype(BF16)
    vectors = start_vectors
    own_modes = start_vectors.shape[2]
    for _ in range(ITERS):
        gathered = lax.all_gather(vectors.astype(BF16), row_axes, axis=1, tiled=True)
        vec_bf = gathered.reshape(2, -1, vectors_count)
        partial_value = apply_tile(pair_tile, vec_bf).reshape(2, freq_rows, mode_count, vectors_count)
        summed = lax.psum(partial_value, "fc")
        gram_matrix = lax.psum(partial_gram(summed), row_axes)
        own_rows = lax.dynamic_slice_in_dim(summed, lax.axis_index("fc") * own_modes, own_modes, 2)
        vectors = orthonormalize(own_rows, gram_matrix)
    return vectors * math.sqrt(2.0 * piece_freqs * mode_count)


def body(x_count, z_count, *args):
    beam_transfer, start_vectors = args[0], args[4]
    parts, freqs, own, multipoles = beam_transfer.shape
    vectors = start_vectors.shape[3]
    lanes = parts * own * z_count
    fits = (
        x_count == 2
        and vectors % (16 * x_count * z_count) == 0
        and lanes == 128
        and own % 16 == 0
        and multipoles % 256 == 0
        and (freqs * own) % lanes == 0
    )
    if fits:
        return body_split(x_count, z_count, *args)
    return body_general(*args)


def solution(mesh):
    sizes = dict(mesh.shape)
    x_count = sizes["fr"] // 2
    shape = (sizes["ma"], x_count, 2, sizes["fc"])
    devices = mesh.devices.reshape(shape)
    split = Mesh(devices, ("ma", "x", "core", "fc"))
    rows = ("ma", "x", "core")
    in_specs = (
        P(None, rows, "fc", None),
        P(rows, "fc"),
        P(),
        P(),
        P(None, rows, "fc", None),
    )
    return jax.shard_map(
        functools.partial(body, x_count, sizes["fc"]),
        mesh=split,
        in_specs=in_specs,
        out_specs=P(None, rows, "fc", None),
        check_vma=False,
    )
```

```python
import functools
import math

import jax
import jax.numpy as jnp
from jax import lax
from jax.experimental import pallas as pl
from jax.experimental.pallas import tpu as pltpu
from jax.sharding import Mesh
from jax.sharding import PartitionSpec as P

ITERS = 2
BF16 = jnp.bfloat16
F32 = jnp.float32
MIB = 1024 * 1024
APPLY_BYTES = 30 * MIB
SMALL_BYTES = 8 * MIB
HIGH = lax.Precision.HIGHEST


def rolled(value, shift):
    return pltpu.roll(value, shift % value.shape[-1], 1)


def apply_kernel(n_vec, n_whole, z_count, own, offsets, keep, send, *refs):
    place_ref, *refs = refs
    vec_refs = (refs[:n_vec], refs[n_vec : 2 * n_vec])
    n_beam = len(offsets) + n_whole
    beam_refs = refs[2 * n_vec : 2 * n_vec + n_beam]
    cov_ref, spec_ref, *refs = refs[2 * n_vec + n_beam :]
    *refs, beam_ref, vec_ref, z_ref, y_ref, sems = refs
    n_out = len(keep) + len(send)
    added, out_refs = refs[: len(refs) - n_out], refs[len(refs) - n_out :]
    count, rows, lanes = out_refs[0].shape
    freqs = 2 * count
    half = rows // 2
    components = spec_ref.shape[0]
    tiles, _, step = z_ref.shape
    lane = lax.broadcasted_iota(jnp.int32, (half, lanes), 1)
    is_real = (lane // own) % 2 == 0
    sign = jnp.where(is_real, -1.0, 1.0).astype(F32)

    copies = []
    for index, (core, offset) in enumerate(offsets):
        size, width, _ = beam_refs[index].shape
        chips = count // size * z_count
        at = lax.rem(place_ref[0] + (offset % chips), chips)
        x_at = at // z_count
        z_at = jnp.where(x_at == 0, at, chips - 1 - at)
        target = beam_ref.at[
            pl.ds(core * count + x_at * size, size), pl.ds(pl.multiple_of(z_at * width, width), width)
        ]
        copies.append(pltpu.make_async_copy(beam_refs[index], target, sems.at[index]))
    for copy in copies:
        copy.start()

    def beam_of(freq):
        side_by_side = [beam_ref, *beam_refs[len(offsets) :]]
        return jnp.concatenate([beam[freq] for beam in side_by_side], axis=1)

    def gather(side, place, carry):
        vec = vec_refs[side][0][place]
        for other in vec_refs[side][1:]:
            vec = vec + other[place]
        vec_ref[side * count + place] = vec.astype(BF16)
        return carry

    for side in range(2):
        lax.fori_loop(0, count, functools.partial(gather, side), 0, unroll=8)
    for copy in copies:
        copy.wait()

    def project(freq, carry):
        z = jnp.dot(vec_ref[freq], beam_of(freq), preferred_element_type=F32)
        for tile in range(tiles):
            z_ref[tile, pl.ds(freq, rows, stride=freqs), :] = z[:, tile * step : (tile + 1) * step]
        return carry

    lax.fori_loop(0, freqs, project, 0, unroll=64)

    def mix(row, carry):
        start = pl.multiple_of(row * freqs, freqs)
        z = jnp.concatenate([z_ref[tile, pl.ds(start, freqs), :] for tile in range(tiles)], axis=1)
        scaled = [(z * spec_ref[k][None, :]).astype(BF16) for k in range(components)]
        y = jnp.dot(cov_ref[...], jnp.concatenate(scaled, axis=0), preferred_element_type=F32)
        for tile in range(tiles):
            y_ref[tile, pl.ds(start, freqs), :] = y[:, tile * step : (tile + 1) * step]
        return carry

    lax.fori_loop(0, rows, mix, 0, unroll=32)

    def expand(side, place, carry):
        freq = side * count + place
        y = [
            y_ref[tile, pl.ds(freq, rows, stride=freqs), :].astype(BF16) for tile in range(tiles)
        ]
        product = lax.dot_general(
            jnp.concatenate(y, axis=1),
            beam_of(freq),
            (((1,), (1,)), ((), ())),
            preferred_element_type=F32,
        )
        swapped = jnp.where(
            jnp.concatenate([is_real, is_real], axis=0),
            rolled(product, -own),
            rolled(product, own),
        )
        top = product[:half] + sign * swapped[half:]
        bottom = product[half:] - sign * swapped[:half]
        image = jnp.concatenate([top, bottom], axis=0)
        if added:
            image = image + added[side][place]
        if side in keep:
            out_refs[keep.index(side)][place] = image
        if side in send:
            out_refs[len(keep) + send.index(side)][place] = image.astype(BF16)
        return carry

    for side in range(2):
        lax.fori_loop(0, count, functools.partial(expand, side), 0, unroll=64)


def apply_covariance(place, vecs, beams, wholes, cov, spec, own, z_count, keep, send, give, added=()):
    count, rows, lanes = vecs[0][0].shape
    freqs = 2 * count
    depth = spec.shape[1]
    step = min(depth, 128)
    flops = 2 * freqs * rows * (2 * lanes * depth + 2 * freqs * depth)
    vmem = pl.BlockSpec(memory_space=pltpu.VMEM)
    n_vec = len(vecs[0])
    offsets = tuple(beam[1:] for beam in beams)
    arrays = [beam[0] for beam in beams] + wholes
    whole = (freqs, lanes, beams[0][0].shape[2])
    out_shape = [jax.ShapeDtypeStruct((count, rows, lanes), F32)] * len(keep)
    out_shape += [jax.ShapeDtypeStruct((count, rows, lanes), BF16)] * len(send)
    out_shape += [jax.ShapeDtypeStruct(whole, BF16)] * give
    tiles = pltpu.VMEM((depth // step, rows * freqs, step), F32)
    kernel = functools.partial(
        apply_kernel, n_vec, len(wholes), z_count, own, offsets, keep, send
    )
    return pl.pallas_call(
        kernel,
        out_shape=out_shape,
        in_specs=[pl.BlockSpec(memory_space=pltpu.SMEM)]
        + [vmem] * (2 * n_vec)
        + [pl.BlockSpec(memory_space=pl.ANY)] * len(beams)
        + [vmem] * (len(wholes) + 2 + len(added)),
        out_specs=[vmem] * len(out_shape),
        scratch_shapes=[pltpu.VMEM(whole, BF16)] * (not give)
        + [pltpu.VMEM((freqs, rows, lanes), BF16), tiles, tiles, pltpu.SemaphoreType.DMA((len(beams),))],
        compiler_params=pltpu.CompilerParams(vmem_limit_bytes=APPLY_BYTES),
        cost_estimate=pl.CostEstimate(
            flops=flops, bytes_accessed=freqs * lanes * depth * 2, transcendentals=0
        ),
    )(place, *vecs[0], *vecs[1], *arrays, cov, spec, *added)


def pack_kernel(own, first_ref, second_ref, out_ref):
    x_count, z_count, groups = out_ref.shape[:3]
    freqs, rows, lanes = first_ref.shape
    per_group = lanes // own
    lane = lax.broadcasted_iota(jnp.int32, (rows, lanes), 1) // own

    def group(index, carry):
        x_index, group_index = index // groups, index % groups
        totals = [jnp.zeros((rows, lanes), F32)] * z_count
        for place in range(per_group):
            freq = index * per_group + place
            image = first_ref[freq] + second_ref[freq]
            for z_index in range(z_count):
                moved = rolled(image, (place - 2 * z_index) * own)
                totals[z_index] = jnp.where(lane == place, moved, totals[z_index])
        for z_index in range(z_count):
            out_ref[x_index, z_index, group_index] = totals[z_index].astype(BF16)
        return carry

    lax.fori_loop(0, x_count * groups, group, 0, unroll=2)


def pack(first, second, x_count, z_count, own):
    freqs, rows, lanes = first.shape
    groups = freqs * own // (x_count * lanes)
    return pl.pallas_call(
        functools.partial(pack_kernel, own),
        out_shape=jax.ShapeDtypeStruct((x_count, z_count, groups, rows, lanes), BF16),
        in_specs=[pl.BlockSpec(memory_space=pltpu.VMEM)] * 2,
        out_specs=pl.BlockSpec(memory_space=pltpu.VMEM),
        compiler_params=pltpu.CompilerParams(vmem_limit_bytes=SMALL_BYTES),
    )(first, second)


def fold(matrix):
    half = matrix.shape[0] // 2
    row = lax.broadcasted_iota(jnp.int32, (half, 2 * half), 0)
    lane = lax.broadcasted_iota(jnp.int32, (half, 2 * half), 1)
    top, bottom = rolled(matrix[:half], half), matrix[half:]
    square = jnp.where((lane >= half) & (row >= lane - half), top, bottom)
    diagonal = jnp.sum(jnp.where(row == lane - half, bottom, 0.0), axis=0, keepdims=True)
    return jnp.concatenate([square, jnp.broadcast_to(diagonal, (8, 2 * half))], axis=0)


def unfold(folded):
    order = folded.shape[1]
    half = order // 2
    lane = lax.broadcasted_iota(jnp.int32, (half, order), 1)
    bottom = folded[:half]
    top = jnp.where(lane < half, rolled(bottom, half), bottom)
    whole = jnp.concatenate([top, bottom], axis=0)
    row = lax.broadcasted_iota(jnp.int32, (order, order), 0)
    lane = lax.broadcasted_iota(jnp.int32, (order, order), 1)
    own = ((row < half) & (row >= lane)) | ((row >= half) & ((lane < half) | (row < lane)))
    matrix = jnp.where(own, whole, whole.T)
    return jnp.where((row == lane) & (row >= half), folded[half : half + 1], matrix)


def gram_kernel(core_ref, rows_ref, start_ref, keep_ref, send_ref):
    senders, groups, parts, vectors, lanes = rows_ref.shape
    total = senders * vectors
    own = start_ref.shape[2]
    per_group = lanes // own
    first = jnp.zeros((total, total), F32)
    second = jnp.zeros((total, total), F32)
    for group in range(groups):
        for part in range(parts):
            flat = rows_ref[:, group, part].reshape(total, lanes)
            start = start_ref[part, group * per_group : (group + 1) * per_group].reshape(lanes, total)
            first += jnp.dot(flat, start.astype(BF16), preferred_element_type=F32)
            second += lax.dot_general(
                flat, flat, (((1,), (1,)), ((), ())), preferred_element_type=F32
            )
    first, second = fold(0.5 * (first + first.T)), fold(second)
    is_first = core_ref[0] == 0
    keep_ref[...] = jnp.where(is_first, first, second)
    send_ref[...] = jnp.where(is_first, second, first)


def grams(core, rows, start):
    total = rows.shape[0] * rows.shape[3]
    return pl.pallas_call(
        gram_kernel,
        out_shape=[jax.ShapeDtypeStruct((total // 2 + 8, total), F32)] * 2,
        in_specs=[pl.BlockSpec(memory_space=pltpu.SMEM)] + [pl.BlockSpec(memory_space=pltpu.VMEM)] * 2,
        out_specs=[pl.BlockSpec(memory_space=pltpu.VMEM)] * 2,
        compiler_params=pltpu.CompilerParams(vmem_limit_bytes=SMALL_BYTES),
    )(core, rows, start)


def triple(value):
    high = value.astype(BF16)
    rest = value - high.astype(F32)
    middle = rest.astype(BF16)
    return high, middle, (rest - middle.astype(F32)).astype(BF16)


def inverse_factor(work_ref, matrix):
    order = matrix.shape[0]
    step = 16
    row = lax.broadcasted_iota(jnp.int32, (step, order), 0)
    lane = lax.broadcasted_iota(jnp.int32, (step, order), 1)
    at = lax.broadcasted_iota(jnp.int32, (order, order), 0)
    work_ref[:, :order] = matrix
    work_ref[:, order:] = jnp.where(at == lax.broadcasted_iota(jnp.int32, (order, order), 1), 1.0, 0.0)
    for begin in range(0, order, step):
        block = slice(begin, begin + step)
        left, right = work_ref[block, :order], work_ref[block, order:]
        columns = [
            jnp.broadcast_to(left[:, begin + k : begin + k + 1], (step, order)) for k in range(step)
        ]
        for k in range(step):
            root = lax.rsqrt(columns[k][k : k + 1])
            factor = columns[k] * root

            def eliminate(value):
                pivot = value[k : k + 1] * root
                return jnp.where(row == k, pivot, jnp.where(row > k, value - factor * pivot, value))

            left, right = eliminate(left), eliminate(right)
            columns = columns[: k + 1] + [eliminate(c) for c in columns[k + 1 :]]
        work_ref[block, order:] = right
        end = begin + step
        if end < order:
            kept = jnp.where(lane >= end, left, 0.0)
            high, middle, low = triple(kept)
            first = jnp.concatenate([high, high, middle, high, low, middle], axis=0).astype(F32).T
            high, middle, low = triple(jnp.concatenate([kept, right], axis=1))
            second = jnp.concatenate([high, middle, high, low, high, middle], axis=0)
            change = jnp.dot(first[end:].astype(BF16), second, preferred_element_type=F32)
            work_ref[end:, :] = work_ref[end:, :] - change
    return work_ref[:, order:]


def finish_kernel(scale, core_ref, rows_ref, kept_ref, given_ref, out_ref, work_ref):
    senders, groups, parts, vectors, lanes = rows_ref.shape
    total = senders * vectors
    exact = functools.partial(lax.dot_general, precision=HIGH, preferred_element_type=F32)
    across = (((1,), (1,)), ((), ()))
    plain = (((1,), (0,)), ((), ()))
    is_first = core_ref[0] == 0
    first = inverse_factor(work_ref, unfold(jnp.where(is_first, kept_ref[...], given_ref[...])))
    gram_second = unfold(jnp.where(is_first, given_ref[...], kept_ref[...]))
    gram_second = exact(exact(first, gram_second, plain), first, across)
    second = inverse_factor(work_ref, gram_second)
    mixing = exact(second, first, plain) * scale
    high, middle, low = triple(mixing)
    for group in range(groups):
        for part in range(parts):
            flat = rows_ref[:, group, part].reshape(total, lanes)
            turned = flat.astype(F32).T.astype(BF16)
            dot = functools.partial(
                lax.dot_general, turned, dimension_numbers=across, preferred_element_type=F32
            )
            out_ref[part, group] = (dot(low) + dot(middle)) + dot(high)


def finish(core, rows, kept, given, scale):
    senders, groups, parts, vectors, lanes = rows.shape
    total = senders * vectors
    return pl.pallas_call(
        functools.partial(finish_kernel, scale),
        out_shape=jax.ShapeDtypeStruct((parts, groups, lanes, total), F32),
        in_specs=[pl.BlockSpec(memory_space=pltpu.SMEM)] + [pl.BlockSpec(memory_space=pltpu.VMEM)] * 3,
        out_specs=pl.BlockSpec(memory_space=pltpu.VMEM),
        scratch_shapes=[pltpu.VMEM((total, 2 * total), F32)],
        compiler_params=pltpu.CompilerParams(vmem_limit_bytes=SMALL_BYTES),
    )(core, rows, kept, given)


def whiten_kernel(core_ref, beam_ref, noise_ref, *out_refs):
    chunks = len(out_refs) // 2
    depth = out_refs[0].shape[2]
    parts, freqs, own, multipoles = beam_ref.shape
    half = multipoles // 2
    level = lax.rsqrt(noise_ref[...])
    is_first = core_ref[0] == 0
    for freq in range(freqs):
        column = jnp.broadcast_to(level[:, freq : freq + 1], (own, half))
        for part in range(parts):
            low = (beam_ref[part, freq, :, :half].astype(F32) * column).astype(BF16)
            high = (beam_ref[part, freq, :, half:].astype(F32) * column).astype(BF16)
            rows = slice(part * own, (part + 1) * own)
            keep = jnp.where(is_first, low, high)
            send = jnp.where(is_first, high, low)
            for chunk in range(chunks):
                cut = slice(chunk * depth, (chunk + 1) * depth)
                out_refs[chunk][freq, rows] = keep[:, cut]
                out_refs[chunks + chunk][freq, rows] = send[:, cut]


def whiten(core, beam, noise, chunks):
    parts, freqs, own, multipoles = beam.shape
    depth = multipoles // (2 * chunks)
    return pl.pallas_call(
        whiten_kernel,
        out_shape=[jax.ShapeDtypeStruct((freqs, parts * own, depth), BF16)] * (2 * chunks),
        in_specs=[pl.BlockSpec(memory_space=pltpu.SMEM)] + [pl.BlockSpec(memory_space=pltpu.VMEM)] * 2,
        out_specs=[pl.BlockSpec(memory_space=pltpu.VMEM)] * (2 * chunks),
        compiler_params=pltpu.CompilerParams(vmem_limit_bytes=SMALL_BYTES),
    )(core, beam, noise.T)


def order_kernel(size, core_ref, cov_ref, out_ref):
    components, order, _ = cov_ref.shape
    places = range(order // (2 * size))
    is_first = core_ref[0] == 0

    def ordered(value):
        found = []
        for core in range(2):
            starts = [(2 * x + (side ^ core)) * size for side in range(2) for x in places]
            found.append(jnp.concatenate([value[start : start + size] for start in starts], axis=0))
        return jnp.where(is_first, found[0], found[1])

    for k in range(components):
        out_ref[:, k * order : (k + 1) * order] = ordered(ordered(cov_ref[k]).T).T.astype(BF16)


def order_covariance(core, cov, size):
    components, order, _ = cov.shape
    return pl.pallas_call(
        functools.partial(order_kernel, size),
        out_shape=jax.ShapeDtypeStruct((order, components * order), BF16),
        in_specs=[pl.BlockSpec(memory_space=pltpu.SMEM), pl.BlockSpec(memory_space=pltpu.VMEM)],
        out_specs=pl.BlockSpec(memory_space=pltpu.VMEM),
        compiler_params=pltpu.CompilerParams(vmem_limit_bytes=SMALL_BYTES),
    )(core, cov)


def turn_kernel(start_ref, out_ref):
    parts, freqs, own, vectors = start_ref.shape
    receivers, groups, mine, lanes = out_ref.shape
    per_group = lanes // (parts * own)

    def group(index, carry):
        tiles = [
            start_ref[part, index * per_group + place]
            for place in range(per_group)
            for part in range(parts)
        ]
        turned = jnp.concatenate(tiles, axis=0).T
        out_ref[:, index] = turned.reshape(receivers, mine, lanes).astype(BF16)
        return carry

    lax.fori_loop(0, groups, group, 0)


def turn(start, receivers, lanes):
    parts, freqs, own, vectors = start.shape
    groups = parts * freqs * own // lanes
    return pl.pallas_call(
        turn_kernel,
        out_shape=jax.ShapeDtypeStruct((receivers, groups, vectors // receivers, lanes), BF16),
        in_specs=[pl.BlockSpec(memory_space=pltpu.VMEM)],
        out_specs=pl.BlockSpec(memory_space=pltpu.VMEM),
        compiler_params=pltpu.CompilerParams(vmem_limit_bytes=SMALL_BYTES),
    )(start)


def operand_kernel(own, *refs):
    x_count, z_count, groups, mine, lanes = refs[0].shape
    parts = lanes // (z_count * own)
    width = parts * own
    lane = lax.broadcasted_iota(jnp.int32, (mine, lanes), 1)
    is_real = (lane // own) % 2 == 0

    def group(side, index, carry):
        x_index, at = index // groups, index % groups
        tiles = [refs[side][x_index, z, at].astype(F32) for z in range(z_count)]
        for place in range(z_count):
            top = tiles[0]
            for z in range(z_count):
                top = jnp.where(lane // width == z, rolled(tiles[z], (z - place) * width), top)
            bottom = jnp.where(is_real, rolled(top, -own), -rolled(top, own))
            image = jnp.concatenate([top, bottom], axis=0).astype(BF16)
            refs[2 + side][index * z_count + place] = image
        return carry

    for side in range(2):
        lax.fori_loop(0, x_count * groups, functools.partial(group, side), 0, unroll=4)


def start_operand(sides, own):
    x_count, z_count, groups, mine, lanes = sides[0].shape
    freqs = x_count * groups * z_count
    return pl.pallas_call(
        functools.partial(operand_kernel, own),
        out_shape=[jax.ShapeDtypeStruct((freqs, 2 * mine, lanes), BF16)] * 2,
        in_specs=[pl.BlockSpec(memory_space=pltpu.VMEM)] * 2,
        out_specs=[pl.BlockSpec(memory_space=pltpu.VMEM)] * 2,
        compiler_params=pltpu.CompilerParams(vmem_limit_bytes=SMALL_BYTES),
    )(*sides)


def swap_cores(value):
    return lax.ppermute(value, "core", [(0, 1), (1, 0)])


def after(value, event):
    return lax.optimization_barrier((value, event))


def gather_ring(sets, late, x_count, z_count):
    count = x_count * z_count
    ring = [k if k < z_count else z_count + count - 1 - k for k in range(count)]
    pairs = {
        1: [(ring[k], ring[(k + 1) % count]) for k in range(count)],
        -1: [(ring[(k + 1) % count], ring[k]) for k in range(count)],
    }
    x_place, z_place = lax.axis_index("x"), lax.axis_index("fc")
    place = jnp.where(x_place == 0, z_place, count - 1 - z_place).astype(jnp.int32).reshape(1)
    moving, found = {}, []
    for chunk, blocks in enumerate(sets):
        for core, block in enumerate(blocks):
            found.append((block, core, 0, chunk))
            moving[chunk, core, 1] = moving[chunk, core, -1] = block
    for hop in range(1, count // 2 + 1):
        for key in moving:
            chunk, core, way = key
            if 2 * hop == count and (way == 1) != (core == 0):
                continue
            moving[key] = lax.ppermute(moving[key], ("x", "fc"), pairs[way])
            if hop == 1 and key == (0, 0, 1):
                late, moving[key] = after(late, moving[key])
            found.append((moving[key], core, -way * hop, chunk))
    return place, found, late


def sum_devices(keep, send, z_count):
    far = lax.ppermute(send, ("x", "core"), [(0, 3), (1, 2), (2, 1), (3, 0)])
    across = lax.ppermute(keep, "x", [(0, 1), (1, 0)])
    value = (keep + swap_cores(send)) + (across + far)
    if z_count & (z_count - 1):
        value = lax.psum(value, "fc")
    else:
        terms = [value] + [
            lax.ppermute(value, "fc", [(j, j ^ s) for j in range(z_count)]) for s in range(1, z_count)
        ]
        while len(terms) > 1:
            terms = [terms[i] + terms[i + 1] for i in range(0, len(terms), 2)]
        value = terms[0]
    return value, swap_cores(value)


def body_split(x_count, z_count, beam_transfer, noise_var, spectra, freq_covariance, start_vectors):
    parts, freqs, own, multipoles = beam_transfer.shape
    vectors = start_vectors.shape[3]
    cores = 2
    core = lax.axis_index("core")
    all_freqs = x_count * cores * freqs
    mine_vectors = vectors // (x_count * z_count)
    depth = multipoles // cores

    core_index = core.astype(jnp.int32).reshape(1)
    chunks = 2 if depth % 256 == 0 else 1
    cut = whiten(core_index, beam_transfer, noise_var, chunks)
    sets = [[cut[chunk], swap_cores(cut[chunks + chunk])] for chunk in range(chunks)]
    start = turn(start_vectors, x_count * z_count, z_count * parts * own)
    place, beams, start = gather_ring(sets, start, x_count, z_count)

    spec = spectra.reshape(-1, cores, depth)
    spec = lax.dynamic_index_in_dim(spec, core, 1, False)
    cov = order_covariance(core_index, freq_covariance, freqs)

    start = lax.all_to_all(start, ("x", "fc"), 0, 0, tiled=True)
    start = start.reshape(x_count, z_count, *start.shape[1:])
    operand = start_operand([start, swap_cores(start)], own)

    apply = functools.partial(apply_covariance, place)
    added, wholes, width = [], [], depth // chunks
    cut_beams = [
        [(piece, at, offset) for piece, at, offset, which in beams if which == chunk]
        for chunk in range(chunks)
    ]
    for chunk in range(chunks):
        part_spec = spec[:, chunk * width : (chunk + 1) * width]
        send = (0, 1) if chunk == chunks - 1 else ()
        found = apply(
            [[operand[0]], [operand[1]]],
            cut_beams[chunk],
            [],
            cov,
            part_spec,
            own,
            z_count,
            (0, 1),
            send,
            chunk > 0,
            added,
        )
        added, whole = found[: 2 + len(send)], found[2 + len(send) :]
        wholes += whole
    mine, theirs, mine_sent, theirs_sent = added
    got_mine, got_theirs = swap_cores(theirs_sent), swap_cores(mine_sent)
    second_mine, second_sent = apply(
        [[mine, got_mine], [theirs, got_theirs]], cut_beams[0], wholes, cov, spec, own, z_count, (0,), (1,), False
    )
    packed = pack(second_mine, swap_cores(second_sent), x_count, z_count, own)
    packed = packed.reshape(x_count * z_count, *packed.shape[2:])
    received = lax.all_to_all(packed, ("x", "fc"), 0, 0, tiled=True)
    groups, lanes = received.shape[1], received.shape[3]
    received = received.reshape(-1, groups, parts, mine_vectors, lanes)

    kept_gram, given_gram = sum_devices(*grams(core_index, received, start_vectors), z_count)
    scale = math.sqrt(2.0 * all_freqs * z_count * own)
    basis = finish(core_index, received, kept_gram, given_gram, scale)
    return basis.reshape(parts, freqs, own, vectors)


def row_operands(row_part, spectra):
    scaled = (row_part.astype(F32)[None] * spectra[:, None, None, :]).astype(BF16)
    real_rows = jnp.concatenate([scaled[:, 0], scaled[:, 1]], axis=-1)
    imag_rows = jnp.concatenate([scaled[:, 1], -scaled[:, 0]], axis=-1)
    return jnp.stack([real_rows, imag_rows], axis=1)


def apply_tile(pair_tile, vec_bf):
    row_count = pair_tile.shape[1]
    stacked = pair_tile.reshape(2 * row_count, pair_tile.shape[2])
    with_real = jnp.dot(stacked, vec_bf[0], preferred_element_type=F32)
    with_imag = jnp.dot(stacked, vec_bf[1], preferred_element_type=F32)
    real_part = with_real[:row_count] - with_imag[row_count:]
    imag_part = with_real[row_count:] + with_imag[:row_count]
    return jnp.stack([real_part, imag_part], axis=0)


def partial_gram(image):
    flat = image.reshape(-1, image.shape[-1])
    return jnp.dot(flat.T, flat, precision=HIGH, preferred_element_type=F32)


def orthonormalize(image, gram_matrix):
    lower = jnp.linalg.cholesky(gram_matrix)
    flat = image.reshape(-1, image.shape[-1])
    solved = lax.linalg.triangular_solve(lower, flat, left_side=False, lower=True, transpose_a=True)
    return solved.reshape(image.shape)


def body_general(beam_transfer, noise_var, spectra, freq_covariance, start_vectors):
    row_axes = ("x", "core")
    whitened = (beam_transfer.astype(F32) * lax.rsqrt(noise_var)[None, :, :, None]).astype(BF16)
    row_beams = lax.all_gather(whitened, "fc", axis=2, tiled=True)
    _, freq_rows, mode_count, multipoles = row_beams.shape
    row_total = freq_rows * mode_count
    components = spectra.shape[0]
    vectors_count = start_vectors.shape[3]
    row_operand = row_operands(row_beams.reshape(2, row_total, multipoles), spectra)
    row_start = lax.axis_index(row_axes) * freq_rows
    row_cov = lax.dynamic_slice_in_dim(freq_covariance, row_start, freq_rows, 1)
    piece = lax.all_gather(whitened, row_axes, axis=1, tiled=True)
    _, piece_freqs, piece_modes, _ = piece.shape
    columns = piece.reshape(2, piece_freqs * piece_modes, multipoles)
    col_operand = jnp.concatenate([columns[0], columns[1]], axis=-1)
    products = lax.dot_general(
        row_operand, col_operand, (((3,), (1,)), ((), ())), preferred_element_type=F32
    )
    weight = jnp.broadcast_to(
        row_cov[:, :, None, :, None], (components, freq_rows, mode_count, piece_freqs, piece_modes)
    )
    weight = weight.reshape(components, row_total, piece_freqs * piece_modes)
    pair_tile = jnp.einsum("kxy,kcxy->cxy", weight, products).astype(BF16)
    vectors = start_vectors
    own_modes = start_vectors.shape[2]
    for _ in range(ITERS):
        gathered = lax.all_gather(vectors.astype(BF16), row_axes, axis=1, tiled=True)
        vec_bf = gathered.reshape(2, -1, vectors_count)
        partial_value = apply_tile(pair_tile, vec_bf).reshape(2, freq_rows, mode_count, vectors_count)
        summed = lax.psum(partial_value, "fc")
        gram_matrix = lax.psum(partial_gram(summed), row_axes)
        own_rows = lax.dynamic_slice_in_dim(summed, lax.axis_index("fc") * own_modes, own_modes, 2)
        vectors = orthonormalize(own_rows, gram_matrix)
    return vectors * math.sqrt(2.0 * piece_freqs * mode_count)


def body(x_count, z_count, *args):
    beam_transfer, start_vectors = args[0], args[4]
    parts, freqs, own, multipoles = beam_transfer.shape
    vectors = start_vectors.shape[3]
    lanes = parts * own * z_count
    fits = (
        x_count == 2
        and vectors % (16 * x_count * z_count) == 0
        and lanes == 128
        and own % 16 == 0
        and multipoles % 256 == 0
        and (freqs * own) % lanes == 0
    )
    if fits:
        return body_split(x_count, z_count, *args)
    return body_general(*args)


def solution(mesh):
    sizes = dict(mesh.shape)
    x_count = sizes["fr"] // 2
    shape = (sizes["ma"], x_count, 2, sizes["fc"])
    devices = mesh.devices.reshape(shape)
    split = Mesh(devices, ("ma", "x", "core", "fc"))
    rows = ("ma", "x", "core")
    in_specs = (
        P(None, rows, "fc", None),
        P(rows, "fc"),
        P(),
        P(),
        P(None, rows, "fc", None),
    )
    return jax.shard_map(
        functools.partial(body, x_count, sizes["fc"]),
        mesh=split,
        in_specs=in_specs,
        out_specs=P(None, rows, "fc", None),
        check_vma=False,
    )
```
